32 devices in a mesh: dp: 8 (over y, x, core), mp: 4 (over z).
Axes of the slice: x: 2, y: 2, z: 4, core: 2. Of those that a mesh axis runs over, the one named last changes fastest.
Arguments:
- layer_input: bfloat16 [16384, 2048], P(('dp', 'mp')), may hold values from -6 to 6
- out_grad: bfloat16 [16384, 2048], P(('dp', 'mp')), may hold values from -6 to 6
- norm_attn: float32 [2048], replicated, may hold values from 0.5 to 1.5
- query_norm: float32 [128], replicated, may hold values from 0.5 to 1.5
- key_norm: float32 [128], replicated, may hold values from 0.5 to 1.5
- w_query: bfloat16 [2048, 2048], P('dp', 'mp'), may hold values from -0.125 to 0.125
- key_matrix: bfloat16 [2048, 1024], P('dp', 'mp'), may hold values from -0.125 to 0.125
- value_matrix: bfloat16 [2048, 1024], P('dp', 'mp'), may hold values from -0.125 to 0.125
- w_output: bfloat16 [2048, 2048], P('mp', 'dp'), may hold values from -1 to 1
- norm_mlp: float32 [2048], replicated, may hold values from 0.5 to 1.5
- w_gate: bfloat16 [2048, 6144], P('dp', 'mp'), may hold values from -0.125 to 0.125
- w_up: bfloat16 [2048, 6144], P('dp', 'mp'), may hold values from -0.125 to 0.125
- w_down: bfloat16 [6144, 2048], P('mp', 'dp'), may hold values from -0.078125 to 0.078125
Outputs:
- layer_output: bfloat16 [16384, 2048], P(('dp', 'mp'))
- input_grad: float32 [16384, 2048], P(('dp', 'mp'))
- grad_norm_attn: float32 [2048], replicated
- grad_query_norm: float32 [128], replicated
- grad_key_norm: float32 [128], replicated
- grad_query: float32 [2048, 2048], P('dp', 'mp')
- grad_key: float32 [2048, 1024], P('dp', 'mp')
- grad_value: float32 [2048, 1024], P('dp', 'mp')
- grad_output: float32 [2048, 2048], P('mp', 'dp')
- grad_norm_mlp: float32 [2048], replicated
- grad_gate: float32 [2048, 6144], P('dp', 'mp')
- grad_up: float32 [2048, 6144], P('dp', 'mp')
- grad_down: float32 [6144, 2048], P('mp', 'dp')
The draws below stay inside these ranges and needn't reach their ends.
All inputs are finite; a program needn't handle non-finite values.
Results may differ from the reference program's by a relative error of at most 0.018.
Values may be sent and summed in bfloat16 or wider, within the bound.
A program may use at most 320 MiB of HBM per device.

```python
import jax
import jax.numpy as jnp
from jax import lax

MODEL_WIDTH = 2048
FF = 6144
QUERY_HEAD_COUNT = 16
KEY_VALUE_HEADS = 8
HEAD_SIZE = 128
SEQUENCE_LENGTH = 1024
SEQ_DP = 2
TOKENS = 16384
N_DP = 8


def shard_levels(rng, extent, cuts, least, high):
    loudness, own = 1.0, jax.random.fold_in(rng, 6)
    for dim, shards_of in cuts:
        steps = jnp.exp(jax.random.uniform(jax.random.fold_in(own, dim), (shards_of,), jnp.float32, least / len(cuts), high / len(cuts)))
        loudness = loudness * jnp.repeat(steps, extent[dim] // shards_of).reshape([-1 if axis == dim else 1 for axis in range(len(extent))])
    return loudness


def gaussian(rng, extent, scale, most, shards=(), held_as=jnp.bfloat16):
    factor_of = shard_levels(rng, extent, shards, -0.22, 0.18) if shards else 1.0
    array = jax.random.normal(rng, extent, jnp.float32) * scale * factor_of
    return jnp.minimum(jnp.maximum(array, -most), most).astype(held_as)


def setup_inputs(seed: int = 0) -> dict:
    arg_keys = jax.random.split(jax.random.key(seed), 14)
    return {
        "layer_input": gaussian(arg_keys[0], (TOKENS, MODEL_WIDTH), 1.0, 6.0, ((0, 32),)),
        "out_grad": gaussian(arg_keys[1], (TOKENS, MODEL_WIDTH), 1.0, 6.0, ((0, 32),)),
        "norm_attn": jnp.clip(1.0 + 0.1 * jax.random.normal(arg_keys[2], (MODEL_WIDTH,), jnp.float32), 0.5, 1.5),
        "query_norm": jnp.clip(1.0 + 0.1 * jax.random.normal(arg_keys[3], (HEAD_SIZE,), jnp.float32), 0.5, 1.5),
        "key_norm": jnp.clip(1.0 + 0.1 * jax.random.normal(arg_keys[4], (HEAD_SIZE,), jnp.float32), 0.5, 1.5),
        "w_query": gaussian(arg_keys[5], (MODEL_WIDTH, QUERY_HEAD_COUNT * HEAD_SIZE), MODEL_WIDTH ** -0.5, 0.125, ((0, 8), (1, 4))),
        "key_matrix": gaussian(arg_keys[6], (MODEL_WIDTH, KEY_VALUE_HEADS * HEAD_SIZE), MODEL_WIDTH ** -0.5, 0.125, ((0, 8), (1, 4))),
        "value_matrix": gaussian(arg_keys[7], (MODEL_WIDTH, KEY_VALUE_HEADS * HEAD_SIZE), MODEL_WIDTH ** -0.5, 0.125, ((0, 8), (1, 4))),
        "w_output": gaussian(arg_keys[8], (QUERY_HEAD_COUNT * HEAD_SIZE, MODEL_WIDTH), (QUERY_HEAD_COUNT * HEAD_SIZE // 64) ** -0.5, 1.0, ((0, 4), (1, 8))),
        "norm_mlp": jnp.clip(1.0 + 0.1 * jax.random.normal(arg_keys[9], (MODEL_WIDTH,), jnp.float32), 0.5, 1.5),
        "w_gate": gaussian(arg_keys[10], (MODEL_WIDTH, FF), MODEL_WIDTH ** -0.5, 0.125, ((0, 8), (1, 4))),
        "w_up": gaussian(arg_keys[11], (MODEL_WIDTH, FF), MODEL_WIDTH ** -0.5, 0.125, ((0, 8), (1, 4))),
        "w_down": gaussian(arg_keys[12], (FF, MODEL_WIDTH), FF ** -0.5, 0.078125, ((0, 4), (1, 8))),
    }


EPSILON = 1e-06
THETA = 1000000.0

@jax.custom_vjp
def reduced_copy(v):
    return lax.optimization_barrier(v.astype(jnp.bfloat16)).astype(jnp.float32)

@jax.custom_vjp
def reduced_backward(v):
    return v

def low_keep(v):
    return (reduced_copy(v), None)

def low_pass(kept, grad):
    return (grad,)

def back_keep(v):
    return (v, None)

def back_low(kept, grad):
    return (reduced_copy(grad),)
reduced_copy.defvjp(low_keep, low_pass)
reduced_backward.defvjp(back_keep, back_low)

def norm_rows(values, gain):
    factor = lax.rsqrt(lax.optimization_barrier(jnp.mean(values * values, -1, keepdims=True)) + EPSILON)
    return values * factor * gain

def tables(length, width):
    half_width = width // 2
    frequencies = THETA ** (-(jnp.arange(half_width, dtype=jnp.float32) * 2.0 / width))
    angles = jnp.arange(length, dtype=jnp.float32)[:, None] * frequencies[None, :]
    return (jnp.cos(angles), jnp.sin(angles))

def rotate(values, cosine_table, sine_table):
    half_width = values.shape[-1] // 2
    first_half = values[..., :half_width]
    second_half = values[..., half_width:]
    cosine_part = cosine_table[:, None, :]
    sine_part = sine_table[:, None, :]
    return jnp.concatenate([first_half * cosine_part - second_half * sine_part, second_half * cosine_part + first_half * sine_part], -1)

def matrix_product(left, right):
    return jnp.dot(left, right, precision=lax.Precision.HIGHEST)

def forward(inputs, norm_attn, query_norm, key_norm, w_query, key_matrix, value_matrix, w_output, norm_mlp, w_gate, w_up, w_down):
    total_rows = inputs.shape[0]
    sequence_batch = total_rows // SEQUENCE_LENGTH
    heads_per_group = QUERY_HEAD_COUNT // KEY_VALUE_HEADS
    first_normed = reduced_copy(norm_rows(inputs, norm_attn))
    query_proj = reduced_backward(matrix_product(first_normed, w_query)).reshape(sequence_batch, SEQUENCE_LENGTH, QUERY_HEAD_COUNT, HEAD_SIZE)
    key_projected = reduced_backward(matrix_product(first_normed, key_matrix)).reshape(sequence_batch, SEQUENCE_LENGTH, KEY_VALUE_HEADS, HEAD_SIZE)
    value_projected = reduced_copy(reduced_backward(matrix_product(first_normed, value_matrix))).reshape(sequence_batch, SEQUENCE_LENGTH, KEY_VALUE_HEADS, HEAD_SIZE)
    cosine_table, sine_table = tables(SEQUENCE_LENGTH, HEAD_SIZE)
    query_rotated = reduced_copy(rotate(norm_rows(query_proj, query_norm), cosine_table, sine_table))
    query_rotated = query_rotated.reshape(sequence_batch, SEQUENCE_LENGTH, KEY_VALUE_HEADS, heads_per_group, HEAD_SIZE)
    key_rot = reduced_copy(rotate(norm_rows(key_projected, key_norm), cosine_table, sine_table))
    scores = jnp.einsum('sqhgd,skhd->shgqk', query_rotated, key_rot, precision=lax.Precision.HIGHEST) * HEAD_SIZE ** (-0.5)
    scores = reduced_backward(scores)
    positions = jnp.arange(SEQUENCE_LENGTH)
    allowed = positions[None, :] <= positions[:, None]
    scores = jnp.where(allowed, scores, -jnp.inf)
    largest = lax.optimization_barrier(jnp.max(scores, -1, keepdims=True))
    expanded = jnp.exp(scores - largest)
    probs = reduced_copy(expanded / lax.optimization_barrier(jnp.sum(expanded, -1, keepdims=True)))
    attended = jnp.einsum('shgqk,skhd->sqhgd', probs, value_projected, precision=lax.Precision.HIGHEST).reshape(total_rows, QUERY_HEAD_COUNT * HEAD_SIZE)
    attended = reduced_copy(reduced_backward(attended))
    middle = inputs + reduced_backward(matrix_product(attended, w_output))
    normed_two = reduced_copy(norm_rows(middle, norm_mlp))
    gate_value = reduced_backward(matrix_product(normed_two, w_gate))
    up_value = reduced_backward(matrix_product(normed_two, w_up))
    hidden = reduced_copy(jax.nn.silu(gate_value) * up_value)
    return middle + reduced_backward(matrix_product(hidden, w_down))

def reference(layer_input, out_grad, norm_attn, query_norm, key_norm, w_query, key_matrix, value_matrix, w_output, norm_mlp, w_gate, w_up, w_down):
    params = tuple((weight.astype(jnp.float32) for weight in (norm_attn, query_norm, key_norm, w_query, key_matrix, value_matrix, w_output, norm_mlp, w_gate, w_up, w_down)))
    group_rows = SEQ_DP * SEQUENCE_LENGTH
    inputs = layer_input.astype(jnp.float32).reshape(N_DP, group_rows, MODEL_WIDTH)
    cotangents = out_grad.astype(jnp.float32).reshape(N_DP, group_rows, MODEL_WIDTH)

    def step(carry, pair):
        group_input, group_cotangent = pair
        output, pullback = jax.vjp(forward, group_input, *params)
        gradients = pullback(group_cotangent)
        carry = tuple((running + addition for running, addition in zip(carry, gradients[1:])))
        return (carry, (output, gradients[0]))
    start = tuple((jnp.zeros_like(weight) for weight in params))
    totals, (outputs, input_grads) = lax.scan(step, start, (inputs, cotangents))
    return (outputs.reshape(TOKENS, MODEL_WIDTH).astype(jnp.bfloat16), input_grads.reshape(TOKENS, MODEL_WIDTH), totals[0], totals[1], totals[2], totals[3], totals[4], totals[5], totals[6], totals[7], totals[8], totals[9], totals[10])
```

```python
import functools

import jax
import jax.numpy as jnp
from jax import lax
from jax.experimental import pallas as pl
from jax.experimental.pallas import tpu as pltpu
from jax.sharding import PartitionSpec as P

HEAD_SIZE = 128
SEQUENCE_LENGTH = 1024


EPSILON = 1e-06
THETA = 1000000.0


def norm_rows(values, gain):
    factor = lax.rsqrt(jnp.mean(values * values, -1, keepdims=True) + EPSILON)
    return (values * factor * gain, factor)


def norm_back(values, factor, gain, upstream):
    scaled = upstream * gain
    inner = jnp.mean(scaled * values, -1, keepdims=True)
    return factor * scaled - values * (factor * factor * factor) * inner


def tables(length, width):
    half_width = width // 2
    frequencies = THETA ** (-(jnp.arange(half_width, dtype=jnp.float32) * 2.0 / width))
    angles = jnp.arange(length, dtype=jnp.float32)[:, None] * frequencies[None, :]
    return (jnp.cos(angles), jnp.sin(angles))


def rotate(values, cosine_table, sine_table):
    half_width = values.shape[-1] // 2
    first_half = values[..., :half_width]
    second_half = values[..., half_width:]
    cosine_part = cosine_table[:, None, :]
    sine_part = sine_table[:, None, :]
    return jnp.concatenate(
        [
            first_half * cosine_part - second_half * sine_part,
            second_half * cosine_part + first_half * sine_part,
        ],
        -1,
    )


def rotate_back(grads, cosine_table, sine_table):
    half_width = grads.shape[-1] // 2
    first_half = grads[..., :half_width]
    second_half = grads[..., half_width:]
    cosine_part = cosine_table[:, None, :]
    sine_part = sine_table[:, None, :]
    return jnp.concatenate(
        [
            first_half * cosine_part + second_half * sine_part,
            second_half * cosine_part - first_half * sine_part,
        ],
        -1,
    )


def matmul(left, right):
    return jnp.dot(left, right, preferred_element_type=jnp.float32)


def dot_last(left, right):
    return lax.dot_general(
        left, right, (((1,), (1,)), ((), ())), preferred_element_type=jnp.float32
    )


def dot_first(left, right):
    return lax.dot_general(
        left, right, (((0,), (0,)), ((), ())), preferred_element_type=jnp.float32
    )


def masked_scores(query_block, keys, start, block_rows, scale):
    raw = (
        jnp.einsum("qhgd,khd->hgqk", query_block, keys, preferred_element_type=jnp.float32) * scale
    )
    query_places = start + jnp.arange(block_rows)[:, None]
    key_places = jnp.arange(keys.shape[0])[None, :]
    return jnp.where(key_places <= query_places, raw, -jnp.inf)


def generic(
    layer_input,
    out_grad,
    norm_attn,
    query_norm,
    key_norm,
    w_query,
    key_matrix,
    value_matrix,
    w_output,
    norm_mlp,
    w_gate,
    w_up,
    w_down,
):
    inputs = layer_input.astype(jnp.float32)
    query_full, key_full, value_full, output_full = (
        lax.all_gather(w_query, "dp", axis=0, tiled=True),
        lax.all_gather(key_matrix, "dp", axis=0, tiled=True),
        lax.all_gather(value_matrix, "dp", axis=0, tiled=True),
        lax.all_gather(w_output, "dp", axis=1, tiled=True),
    )
    first_normed, factor_one = norm_rows(inputs, norm_attn)
    normed_all = lax.all_gather(first_normed.astype(jnp.bfloat16), "mp", axis=0, tiled=True)
    total_rows = normed_all.shape[0]
    sequence_batch = total_rows // SEQUENCE_LENGTH
    query_heads = query_full.shape[1] // HEAD_SIZE
    shared_heads = key_full.shape[1] // HEAD_SIZE
    heads_per_group = query_heads // shared_heads
    query_proj = matmul(normed_all, query_full).reshape(
        sequence_batch, SEQUENCE_LENGTH, query_heads, HEAD_SIZE
    )
    key_projected = matmul(normed_all, key_full).reshape(
        sequence_batch, SEQUENCE_LENGTH, shared_heads, HEAD_SIZE
    )
    value_low = (
        matmul(normed_all, value_full)
        .astype(jnp.bfloat16)
        .reshape(sequence_batch, SEQUENCE_LENGTH, shared_heads, HEAD_SIZE)
    )
    cosine_table, sine_table = tables(SEQUENCE_LENGTH, HEAD_SIZE)
    query_normed, query_factor = norm_rows(query_proj, query_norm)
    query_rotated = rotate(query_normed, cosine_table, sine_table).astype(jnp.bfloat16)
    query_rotated = query_rotated.reshape(
        sequence_batch, SEQUENCE_LENGTH, shared_heads, heads_per_group, HEAD_SIZE
    )
    key_normed, key_factor = norm_rows(key_projected, key_norm)
    key_rot = rotate(key_normed, cosine_table, sine_table).astype(jnp.bfloat16)
    block_rows = min(512, SEQUENCE_LENGTH)
    block_count = SEQUENCE_LENGTH // block_rows
    scale = HEAD_SIZE ** (-0.5)
    attended_pieces = []
    log_totals = []
    for seq_index in range(sequence_batch):
        for block_index in range(block_count):
            start = block_index * block_rows
            query_block = query_rotated[seq_index, start : start + block_rows]
            scores = masked_scores(query_block, key_rot[seq_index], start, block_rows, scale)
            largest = jnp.max(scores, -1, keepdims=True)
            expanded = jnp.exp(scores - largest)
            summed = jnp.sum(expanded, -1, keepdims=True)
            probs_low = (expanded / summed).astype(jnp.bfloat16)
            block_out = jnp.einsum(
                "hgqk,khd->qhgd",
                probs_low,
                value_low[seq_index],
                preferred_element_type=jnp.float32,
            )
            attended_pieces.append(block_out.reshape(block_rows, query_heads * HEAD_SIZE))
            log_totals.append(largest + jnp.log(summed))
    attended = jnp.concatenate(attended_pieces, 0).astype(jnp.bfloat16)
    attn_sum = lax.psum_scatter(
        matmul(attended, output_full), "mp", scatter_dimension=0, tiled=True
    )
    middle = inputs + attn_sum
    gate_full, up_full, down_full = (
        lax.all_gather(w_gate, "dp", axis=0, tiled=True),
        lax.all_gather(w_up, "dp", axis=0, tiled=True),
        lax.all_gather(w_down, "dp", axis=1, tiled=True),
    )
    normed_two, factor_two = norm_rows(middle, norm_mlp)
    normed_two_all = lax.all_gather(normed_two.astype(jnp.bfloat16), "mp", axis=0, tiled=True)
    gate_value = matmul(normed_two_all, gate_full)
    up_value = matmul(normed_two_all, up_full)
    hidden_low = (jax.nn.silu(gate_value) * up_value).astype(jnp.bfloat16)
    mlp_sum = lax.psum_scatter(
        matmul(hidden_low, down_full).astype(jnp.bfloat16), "mp", scatter_dimension=0, tiled=True
    ).astype(jnp.float32)
    layer_output = (middle + mlp_sum).astype(jnp.bfloat16)
    grad_rows = lax.all_gather(out_grad, "mp", axis=0, tiled=True)
    gate_back, up_back, down_back = (
        lax.all_gather(w_gate, "dp", axis=0, tiled=True),
        lax.all_gather(w_up, "dp", axis=0, tiled=True),
        lax.all_gather(w_down, "dp", axis=1, tiled=True),
    )
    hidden_grad = dot_last(grad_rows, down_back)
    down_grad = dot_first(hidden_low, grad_rows)
    sigmoid_gate = jax.nn.sigmoid(gate_value)
    gate_grad = (
        hidden_grad * up_value * sigmoid_gate * (1.0 + gate_value * (1.0 - sigmoid_gate))
    ).astype(jnp.bfloat16)
    up_grad = (hidden_grad * gate_value * sigmoid_gate).astype(jnp.bfloat16)
    gate_weight_grad = dot_first(normed_two_all, gate_grad)
    up_weight_grad = dot_first(normed_two_all, up_grad)
    two_grad = lax.psum_scatter(
        dot_last(gate_grad, gate_back) + dot_last(up_grad, up_back),
        "mp",
        scatter_dimension=0,
        tiled=True,
    )
    gain_two_grad = jnp.sum(two_grad * middle * factor_two, 0)
    middle_grad = out_grad.astype(jnp.float32) + norm_back(middle, factor_two, norm_mlp, two_grad)
    mlp_grads = (
        lax.psum_scatter(
            gate_weight_grad.astype(jnp.bfloat16), "dp", scatter_dimension=0, tiled=True
        ).astype(jnp.float32),
        lax.psum_scatter(
            up_weight_grad.astype(jnp.bfloat16), "dp", scatter_dimension=0, tiled=True
        ).astype(jnp.float32),
        lax.psum_scatter(
            down_grad.astype(jnp.bfloat16), "dp", scatter_dimension=1, tiled=True
        ).astype(jnp.float32),
    )
    branch_all = lax.all_gather(middle_grad.astype(jnp.bfloat16), "mp", axis=0, tiled=True)
    output_weight_grad = dot_first(attended, branch_all)
    attended_grad = dot_last(branch_all, output_full).astype(jnp.bfloat16)
    attended_grad = attended_grad.reshape(
        sequence_batch, SEQUENCE_LENGTH, shared_heads, heads_per_group, HEAD_SIZE
    )
    query_grad_seqs = []
    key_grad_seqs = []
    value_grad_seqs = []
    for seq_index in range(sequence_batch):
        key_running = jnp.zeros((SEQUENCE_LENGTH, shared_heads, HEAD_SIZE), jnp.float32)
        value_running = jnp.zeros((SEQUENCE_LENGTH, shared_heads, HEAD_SIZE), jnp.float32)
        query_blocks = []
        for block_index in range(block_count):
            start = block_index * block_rows
            query_block = query_rotated[seq_index, start : start + block_rows]
            scores = masked_scores(query_block, key_rot[seq_index], start, block_rows, scale)
            probs_full = jnp.exp(scores - log_totals[seq_index * block_count + block_index])
            probs_low = probs_full.astype(jnp.bfloat16)
            grad_block = attended_grad[seq_index, start : start + block_rows]
            prob_grad = jnp.einsum(
                "qhgd,khd->hgqk",
                grad_block,
                value_low[seq_index],
                preferred_element_type=jnp.float32,
            )
            row_inner = jnp.sum(probs_full * prob_grad, -1, keepdims=True)
            score_grad = (probs_full * (prob_grad - row_inner)).astype(jnp.bfloat16)
            query_blocks.append(
                jnp.einsum(
                    "hgqk,khd->qhgd",
                    score_grad,
                    key_rot[seq_index],
                    preferred_element_type=jnp.float32,
                )
                * scale
            )
            key_running = (
                key_running
                + jnp.einsum(
                    "hgqk,qhgd->khd", score_grad, query_block, preferred_element_type=jnp.float32
                )
                * scale
            )
            value_running = value_running + jnp.einsum(
                "hgqk,qhgd->khd", probs_low, grad_block, preferred_element_type=jnp.float32
            )
        query_grad_seqs.append(jnp.concatenate(query_blocks, 0))
        key_grad_seqs.append(key_running)
        value_grad_seqs.append(value_running)
    rot_query_grad = jnp.stack(query_grad_seqs, 0).reshape(
        sequence_batch, SEQUENCE_LENGTH, query_heads, HEAD_SIZE
    )
    rot_key_grad = jnp.stack(key_grad_seqs, 0)
    value_grad = (
        jnp.stack(value_grad_seqs, 0)
        .reshape(total_rows, shared_heads * HEAD_SIZE)
        .astype(jnp.bfloat16)
    )
    query_normed_grad = rotate_back(rot_query_grad, cosine_table, sine_table)
    query_gain_grad = jnp.sum(query_normed_grad * query_proj * query_factor, (0, 1, 2))
    query_grad = norm_back(query_proj, query_factor, query_norm, query_normed_grad)
    query_grad = query_grad.reshape(total_rows, query_heads * HEAD_SIZE).astype(jnp.bfloat16)
    key_normed_grad = rotate_back(rot_key_grad, cosine_table, sine_table)
    key_gain_grad = jnp.sum(key_normed_grad * key_projected * key_factor, (0, 1, 2))
    key_grad = norm_back(key_projected, key_factor, key_norm, key_normed_grad)
    key_grad = key_grad.reshape(total_rows, shared_heads * HEAD_SIZE).astype(jnp.bfloat16)
    query_weight_grad = dot_first(normed_all, query_grad)
    key_weight_grad = dot_first(normed_all, key_grad)
    value_weight_grad = dot_first(normed_all, value_grad)
    one_partial = (
        dot_last(query_grad, query_full)
        + dot_last(key_grad, key_full)
        + dot_last(value_grad, value_full)
    )
    one_grad = lax.psum_scatter(
        one_partial.astype(jnp.bfloat16), "mp", scatter_dimension=0, tiled=True
    ).astype(jnp.float32)
    gain_one_grad = jnp.sum(one_grad * inputs * factor_one, 0)
    input_grad = middle_grad + norm_back(inputs, factor_one, norm_attn, one_grad)
    attn_grads = (
        lax.psum_scatter(
            query_weight_grad.astype(jnp.bfloat16), "dp", scatter_dimension=0, tiled=True
        ).astype(jnp.float32),
        lax.psum_scatter(
            key_weight_grad.astype(jnp.bfloat16), "dp", scatter_dimension=0, tiled=True
        ).astype(jnp.float32),
        lax.psum_scatter(
            value_weight_grad.astype(jnp.bfloat16), "dp", scatter_dimension=0, tiled=True
        ).astype(jnp.float32),
        lax.psum_scatter(
            output_weight_grad.astype(jnp.bfloat16), "dp", scatter_dimension=1, tiled=True
        ).astype(jnp.float32),
    )
    gain_sums = lax.psum(
        (gain_one_grad, query_gain_grad, key_gain_grad, gain_two_grad), ("dp", "mp")
    )
    return (
        layer_output,
        input_grad,
        gain_sums[0],
        gain_sums[1],
        gain_sums[2],
        attn_grads[0],
        attn_grads[1],
        attn_grads[2],
        attn_grads[3],
        gain_sums[3],
        mlp_grads[0],
        mlp_grads[1],
        mlp_grads[2],
    )


ROW_BLOCK = 256


def wide_tables(length):
    cosine_table, sine_table = tables(length, HEAD_SIZE)
    return (
        jnp.concatenate([cosine_table, cosine_table], 1),
        jnp.concatenate([-sine_table, sine_table], 1),
    )


def turn(values, cosines, sines):
    return values * cosines + pltpu.roll(values, HEAD_SIZE // 2, 1) * sines


def turn_back(values, cosines, sines):
    return values * cosines - pltpu.roll(values, HEAD_SIZE // 2, 1) * sines


def causal(rows):
    query_places = lax.broadcasted_iota(jnp.int32, (rows, rows), 0)
    key_places = lax.broadcasted_iota(jnp.int32, (rows, rows), 1)
    return key_places <= query_places


def attend_kernel(
    core, own, other, w0, w1, w2, w3_low, w3_high, cosines, sines, query_gain, key_gain,
    proj, query_rot, key_rot, value, attended, log_total,
):
    half = own.shape[0]
    length = 2 * half
    scale = HEAD_SIZE ** (-0.5)
    query_cols = query_rot.shape[1]
    heads = query_cols // HEAD_SIZE
    for h in range(2):
        here = core[0] == h
        rows = slice(h * half, (h + 1) * half)
        block = None
        start = 0
        for weight in (w0, w1, w2, w3_low, w3_high):
            cols = slice(start, start + weight.shape[0])
            start = cols.stop
            tokens = jnp.where(here, own[:, cols], other[:, cols])
            term = matmul(tokens, weight[...])
            block = term if block is None else block + term
        proj[rows, :] = block
        cos_rows, sin_rows = cosines[rows, :], sines[rows, :]
        for head in range(heads):
            cols = slice(head * HEAD_SIZE, (head + 1) * HEAD_SIZE)
            normed, _ = norm_rows(block[:, cols], query_gain[...])
            query_rot[rows, cols] = turn(normed, cos_rows, sin_rows).astype(jnp.bfloat16)
        cols = slice(query_cols, query_cols + HEAD_SIZE)
        normed, _ = norm_rows(block[:, cols], key_gain[...])
        key_rot[rows, :] = turn(normed, cos_rows, sin_rows).astype(jnp.bfloat16)
        value[rows, :] = block[:, query_cols + HEAD_SIZE :].astype(jnp.bfloat16)
    allowed = causal(ROW_BLOCK)

    def place(start):
        return pl.ds(pl.multiple_of((start + core[0] * half) % length, ROW_BLOCK), ROW_BLOCK)

    lane = lax.broadcasted_iota(jnp.int32, (ROW_BLOCK, HEAD_SIZE), 1)
    for start in range(0, length, ROW_BLOCK):
        rows = slice(start, start + ROW_BLOCK)
        logs = jnp.zeros((ROW_BLOCK, HEAD_SIZE), jnp.float32)
        for head in range(heads):
            cols = slice(head * HEAD_SIZE, (head + 1) * HEAD_SIZE)
            query = query_rot[rows, cols]
            scores = [jnp.where(allowed, dot_last(query, key_rot[rows, :]) * scale, -jnp.inf)]
            if start:
                scores.append(dot_last(query, key_rot[:start, :]) * scale)
            largest = functools.reduce(
                jnp.maximum, [jnp.max(s, -1, keepdims=True) for s in scores]
            )
            expanded = [jnp.exp(s - largest) for s in scores]
            summed = sum(jnp.sum(e, -1, keepdims=True) for e in expanded)
            out = matmul(expanded[0].astype(jnp.bfloat16), value[rows, :])
            if start:
                out = out + matmul(expanded[1].astype(jnp.bfloat16), value[:start, :])
            attended[place(start), cols] = (out / summed).astype(jnp.bfloat16)
            logs = jnp.where(lane == head, largest + jnp.log(summed), logs)
        log_total[rows, :] = logs


def attend(core, own, other, weights, cosines, sines, query_gain, key_gain, planes, query_cols):
    half, width = own.shape
    length = 2 * half
    cols = weights[0].shape[1]
    group = cols // planes
    whole = lambda shape: pl.BlockSpec(shape, lambda g, core: (0, 0))
    column = lambda rows, width: pl.BlockSpec((rows, width), lambda g, core: (0, g))
    shape = jax.ShapeDtypeStruct
    return pl.pallas_call(
        attend_kernel,
        grid_spec=pltpu.PrefetchScalarGridSpec(
            num_scalar_prefetch=1,
            grid=(planes,),
            in_specs=[whole((half, width))] * 2
            + [column(weight.shape[0], group) for weight in weights]
            + [whole((length, HEAD_SIZE))] * 2
            + [whole((1, HEAD_SIZE))] * 2,
            out_specs=[
                column(length, group),
                column(length, query_cols),
                column(length, HEAD_SIZE),
                column(length, HEAD_SIZE),
                column(length, query_cols),
                column(length, HEAD_SIZE),
            ],
        ),
        out_shape=[
            shape((length, cols), jnp.float32),
            shape((length, planes * query_cols), jnp.bfloat16),
            shape((length, planes * HEAD_SIZE), jnp.bfloat16),
            shape((length, planes * HEAD_SIZE), jnp.bfloat16),
            shape((length, planes * query_cols), jnp.bfloat16),
            shape((length, planes * HEAD_SIZE), jnp.float32),
        ],
        compiler_params=pltpu.CompilerParams(vmem_limit_bytes=56 * 2**20),
        cost_estimate=pl.CostEstimate(
            flops=2 * length * width * cols + 3 * planes * query_cols * length**2,
            bytes_accessed=30 * 2**20,
            transcendentals=planes * 2 * length**2,
        ),
    )(core, own, other, *weights, cosines, sines, query_gain, key_gain)


def attend_back_kernel(
    core, own, other, o0, o1, o2, o3_low, o3_high, cosines, sines, query_gain, key_gain,
    proj, query_rot, key_rot, value, log_total,
    proj_grad, gain_grads, grad, key_total, value_total,
):
    half = own.shape[0]
    length = 2 * half
    part = o0.shape[1]
    scale = HEAD_SIZE ** (-0.5)
    query_cols = query_rot.shape[1]
    heads = query_cols // HEAD_SIZE

    @pl.when(pl.program_id(0) == 0)
    def _():
        gain_grads[...] = jnp.zeros_like(gain_grads)

    low = pl.program_id(0) < pl.num_programs(0) // 2
    corner = jnp.where(low, o3_low[...], o3_high[...])
    for h in range(2):
        here = core[0] == h
        block = None
        for k, weight in enumerate((o0[...], o1[...], o2[...], corner)):
            cols = slice(k * part, (k + 1) * part)
            tokens = jnp.where(here, own[:, cols], other[:, cols])
            term = dot_last(tokens, weight)
            block = term if block is None else block + term
        grad[h * half : (h + 1) * half, :] = block.astype(jnp.bfloat16)
    key_total[...] = jnp.zeros_like(key_total)
    value_total[...] = jnp.zeros_like(value_total)
    allowed = causal(ROW_BLOCK)

    def fold(values):
        return jnp.sum(values.reshape(-1, 8, HEAD_SIZE), 0)

    def place(start):
        return pl.ds(pl.multiple_of((start + core[0] * half) % length, ROW_BLOCK), ROW_BLOCK)

    for start in range(0, length, ROW_BLOCK):
        rows = slice(start, start + ROW_BLOCK)
        for head in range(heads):
            cols = slice(head * HEAD_SIZE, (head + 1) * HEAD_SIZE)
            query = query_rot[rows, cols]
            upstream = grad[rows, cols]
            logs = log_total[rows, head : head + 1]
            spans = [rows] + ([slice(0, start)] if start else [])
            probs, prob_grads = [], []
            for n, span in enumerate(spans):
                raw = dot_last(query, key_rot[span, :]) * scale
                if n == 0:
                    raw = jnp.where(allowed, raw, -jnp.inf)
                probs.append(jnp.exp(raw - logs))
                prob_grads.append(dot_last(upstream, value[span, :]))
            inner = sum(jnp.sum(p * d, -1, keepdims=True) for p, d in zip(probs, prob_grads))
            query_back = None
            for span, p, d in zip(spans, probs, prob_grads):
                score_grad = (p * (d - inner)).astype(jnp.bfloat16)
                term = matmul(score_grad, key_rot[span, :])
                query_back = term if query_back is None else query_back + term
                key_total[span, :] += dot_first(score_grad, query)
                value_total[span, :] += dot_first(p.astype(jnp.bfloat16), upstream)
            normed_grad = turn_back(query_back * scale, cosines[rows, :], sines[rows, :])
            values = proj[rows, cols]
            _, factor = norm_rows(values, query_gain[...])
            gain_grads[:8, :] += fold(normed_grad * values * factor)
            back = norm_back(values, factor, query_gain[...], normed_grad)
            proj_grad[place(start), cols] = back.astype(jnp.bfloat16)
    for start in range(0, length, ROW_BLOCK):
        rows = slice(start, start + ROW_BLOCK)
        cols = slice(query_cols, query_cols + HEAD_SIZE)
        normed_grad = turn_back(key_total[rows, :] * scale, cosines[rows, :], sines[rows, :])
        values = proj[rows, cols]
        _, factor = norm_rows(values, key_gain[...])
        gain_grads[8:, :] += fold(normed_grad * values * factor)
        back = norm_back(values, factor, key_gain[...], normed_grad)
        proj_grad[place(start), cols] = back.astype(jnp.bfloat16)
        proj_grad[place(start), query_cols + HEAD_SIZE :] = value_total[rows, :].astype(
            jnp.bfloat16
        )


def attend_back(
    core, own, other, weights, cosines, sines, query_gain, key_gain, saved, planes, query_cols
):
    half, width = own.shape
    length = 2 * half
    part = weights[0].shape[1]
    proj, query_rot, key_rot, value, log_total = saved
    cols = proj.shape[1]
    group = cols // planes
    whole = lambda shape: pl.BlockSpec(shape, lambda g, core: (0, 0))
    column = lambda rows, width: pl.BlockSpec((rows, width), lambda g, core: (0, g))
    shape = jax.ShapeDtypeStruct
    return pl.pallas_call(
        attend_back_kernel,
        grid_spec=pltpu.PrefetchScalarGridSpec(
            num_scalar_prefetch=1,
            grid=(planes,),
            in_specs=[whole((half, width))] * 2
            + [pl.BlockSpec((query_cols, part), lambda g, core: (g, 0))] * 3
            + [
                pl.BlockSpec((query_cols, part), lambda g, core: (jnp.minimum(g, 1), 0)),
                pl.BlockSpec((query_cols, part), lambda g, core: (jnp.maximum(g - 2, 0), 0)),
            ]
            + [whole((length, HEAD_SIZE))] * 2
            + [whole((1, HEAD_SIZE))] * 2
            + [
                column(length, group),
                column(length, query_cols),
                column(length, HEAD_SIZE),
                column(length, HEAD_SIZE),
                column(length, HEAD_SIZE),
            ],
            out_specs=[column(length, group), whole((16, HEAD_SIZE))],
            scratch_shapes=[
                pltpu.VMEM((length, query_cols), jnp.bfloat16),
                pltpu.VMEM((length, HEAD_SIZE), jnp.float32),
                pltpu.VMEM((length, HEAD_SIZE), jnp.float32),
            ],
        ),
        out_shape=[
            shape((length, cols), jnp.bfloat16),
            shape((16, HEAD_SIZE), jnp.float32),
        ],
        compiler_params=pltpu.CompilerParams(vmem_limit_bytes=56 * 2**20),
        cost_estimate=pl.CostEstimate(
            flops=length * width * cols + 8 * planes * query_cols * length**2,
            bytes_accessed=30 * 2**20,
            transcendentals=planes * 2 * length**2,
        ),
    )(core, own, other, *weights, cosines, sines, query_gain, key_gain, *saved)


def feed_kernel(*refs):
    token_tiles, grad_tiles = refs[:4], refs[4:8]
    gate_up, down = refs[8:10]
    all_tokens, all_grads, all_hidden, all_gate, all_up = refs[-13:-8]
    out_tiles, two_tiles = refs[-8:-4], refs[-4:]
    step = pl.program_id(0)
    units = down.shape[1]
    width = down.shape[2]
    hidden_count = down.shape[0] * units
    gate_t = gate_up[:, :units, :].reshape(hidden_count, width)
    up_t = gate_up[:, units:, :].reshape(hidden_count, width)
    down_t = down[...].reshape(hidden_count, width)

    def select(tiles):
        low = jnp.where(step == 0, tiles[0][...], tiles[1][...])
        high = jnp.where(step == 2, tiles[2][...], tiles[3][...])
        return jnp.where(step < 2, low, high)

    all_tokens[...] = select(token_tiles)
    all_grads[...] = select(grad_tiles)
    tokens = all_tokens[...]
    grads = all_grads[...]
    for start in range(0, hidden_count, 256):
        cols = slice(start, start + 256)
        gate = dot_last(tokens, gate_t[cols])
        up = dot_last(tokens, up_t[cols])
        hidden_grad = dot_last(grads, down_t[cols])
        sigmoid_gate = 1.0 / (1.0 + jnp.exp(-gate))
        silu = gate * sigmoid_gate
        all_hidden[:, cols] = (silu * up).astype(jnp.bfloat16)
        all_gate[:, cols] = (
            hidden_grad * up * sigmoid_gate * (1.0 + gate * (1.0 - sigmoid_gate))
        ).astype(jnp.bfloat16)
        all_up[:, cols] = (hidden_grad * silu).astype(jnp.bfloat16)
    hidden, gate_grad, up_grad = all_hidden[...], all_gate[...], all_up[...]
    for start in range(0, width, 512):
        cols = slice(start, start + 512)
        out = matmul(hidden, down_t[:, cols]).astype(jnp.bfloat16)
        two = (matmul(gate_grad, gate_t[:, cols]) + matmul(up_grad, up_t[:, cols])).astype(
            jnp.bfloat16
        )
        for tile in range(4):

            @pl.when(step == tile)
            def _():
                out_tiles[tile][:, cols] = out
                two_tiles[tile][:, cols] = two


def feed(index, earlier, tokens, grads, gate_up, down):
    tile, width = 256, gate_up.shape[2]
    hidden_count = down.shape[0] * down.shape[1]
    count = 16 * tile
    placed = lambda t: (index * 4 + t, 0)
    spec = pl.BlockSpec
    shape = jax.ShapeDtypeStruct
    kept = [] if earlier is None else list(earlier)
    once = pl.Buffered(1)
    blocks = [
        spec((tile, width), lambda t, row=row: (row, 0), pipeline_mode=once)
        for _, row in tokens + grads
    ]
    return pl.pallas_call(
        feed_kernel,
        grid=(4,),
        in_specs=blocks
        + [
            spec(gate_up.shape, lambda t: (0, 0, 0), pipeline_mode=once),
            spec(down.shape, lambda t: (0, 0, 0), pipeline_mode=once),
        ]
        + [spec(memory_space=pl.ANY)] * len(kept),
        out_specs=[spec((tile, width), placed)] * 2
        + [spec((tile, hidden_count), placed)] * 3
        + [spec((tile, width), lambda t: (0, 0))] * 8,
        out_shape=[shape((count, width), jnp.bfloat16)] * 2
        + [shape((count, hidden_count), jnp.bfloat16)] * 3
        + [shape((tile, width), jnp.bfloat16)] * 8,
        input_output_aliases={10 + k: k for k in range(len(kept))},
        compiler_params=pltpu.CompilerParams(vmem_limit_bytes=60 * 2**20),
        cost_estimate=pl.CostEstimate(
            flops=48 * tile * width * hidden_count,
            bytes_accessed=40 * 2**20,
            transcendentals=4 * tile * hidden_count,
        ),
    )(*[array for array, _ in tokens + grads], gate_up, down, *kept)


def columns_kernel(transposed, place, left, w0, w1, w2, w3_low, w3_high, own, other):
    rows = own.shape[0]

    def write(lines, result):
        for ref, kind in ((own, jnp.float32), (other, jnp.bfloat16)):
            start = 0 if ref is own else rows
            ref[...] = result(lines[start : start + rows]).astype(kind)

    for k, weight in enumerate((w0, w1, w2)):

        @pl.when(pl.program_id(0) == k)
        def _():
            step = dot_last if transposed else matmul
            write(left, lambda lines: step(lines, weight[...]))

    @pl.when(pl.program_id(0) == 3)
    def _():
        if transposed:
            write(
                left,
                lambda lines: jnp.concatenate(
                    [dot_last(lines, w3_low[...]), dot_last(lines, w3_high[...])], 1
                ),
            )
        else:
            middle = w3_low.shape[0]
            write(
                left,
                lambda lines: matmul(lines[:, :middle], w3_low[...])
                + matmul(lines[:, middle:], w3_high[...]),
            )


def columns(place, left, weights, transposed):
    length, depth = left.shape
    rows = length // 2
    part = weights[0].shape[0 if transposed else 1]
    width = 4 * part
    whole = lambda array: pl.BlockSpec(array.shape, lambda k, place: (0, 0))
    block = pl.BlockSpec((rows, part), lambda k, place: (0, k ^ place[0]))
    shape = jax.ShapeDtypeStruct
    return pl.pallas_call(
        functools.partial(columns_kernel, transposed),
        grid_spec=pltpu.PrefetchScalarGridSpec(
            num_scalar_prefetch=1,
            grid=(4,),
            in_specs=[whole(array) for array in (left, *weights)],
            out_specs=[block, block],
        ),
        out_shape=[shape((rows, width), jnp.float32), shape((rows, width), jnp.bfloat16)],
        compiler_params=pltpu.CompilerParams(vmem_limit_bytes=56 * 2**20),
        cost_estimate=pl.CostEstimate(
            flops=2 * length * depth * width, bytes_accessed=20 * 2**20, transcendentals=0
        ),
    )(place, left, *weights)


def tile_call(kernel, place, ins, outs, kept):
    width = 2048
    tile = 256

    def spec(cut, columns):
        if cut == "rows":
            return pl.BlockSpec((tile, columns), lambda t, place: (t, 0))
        if cut == "low" or cut == "high":
            return pl.BlockSpec((tile, columns), lambda t, place: (0, 0))
        return pl.BlockSpec((cut, columns), lambda t, place: (0, 0))

    return pl.pallas_call(
        kernel,
        grid_spec=pltpu.PrefetchScalarGridSpec(
            num_scalar_prefetch=1,
            grid=(2,),
            in_specs=[spec(cut, array.shape[1]) for array, cut in ins],
            out_specs=[spec(cut, shape.shape[1]) for shape, cut in outs],
        ),
        out_shape=[shape for shape, _ in outs],
        compiler_params=pltpu.CompilerParams(vmem_limit_bytes=56 * 2**20),
        cost_estimate=pl.CostEstimate(
            flops=20 * 2**20, bytes_accessed=kept * 2**20, transcendentals=0
        ),
    )(place, *[array for array, _ in ins])


def put(low_ref, high_ref, values):
    first = pl.program_id(0) == 0

    @pl.when(first)
    def _():
        low_ref[...] = values

    @pl.when(jnp.logical_not(first))
    def _():
        high_ref[...] = values


def choose(low_ref, high_ref):
    return jnp.where(pl.program_id(0) == 0, low_ref[...], high_ref[...]).astype(jnp.float32)


def add_gain(gain_ref, values):
    @pl.when(pl.program_id(0) == 0)
    def _():
        gain_ref[...] = jnp.zeros_like(gain_ref)

    gain_ref[...] += jnp.sum(values.reshape(-1, 8, values.shape[1]), 0)


def relabelled(ref, values, place):
    width = values.shape[1] // 4
    for k in range(4):
        start = pl.multiple_of((place[0] ^ k) * width, width)
        ref[:, pl.ds(start, width)] = values[:, k * width : (k + 1) * width]


def first_norm_kernel(place, inputs, gain, normed):
    values, _ = norm_rows(inputs[...].astype(jnp.float32), gain[...])
    relabelled(normed, values.astype(jnp.bfloat16), place)


def middle_kernel(place, inputs, own, other, gain, middle, low, high):
    values = inputs[...].astype(jnp.float32) + own[...] + other[...].astype(jnp.float32)
    middle[...] = values
    put(low, high, norm_rows(values, gain[...])[0].astype(jnp.bfloat16))


def middle_back_kernel(
    place, middle, cotangent, own_low, own_high, x_low, x_high, y_low, y_high, gain,
    middle_grad, branch, gain_grad,
):
    two_grad = choose(own_low, own_high) + choose(x_low, x_high) + choose(y_low, y_high)
    values = middle[...]
    _, factor = norm_rows(values, gain[...])
    add_gain(gain_grad, two_grad * values * factor)
    grads = cotangent[...].astype(jnp.float32) + norm_back(values, factor, gain[...], two_grad)
    middle_grad[...] = grads
    relabelled(branch, grads.astype(jnp.bfloat16), place)


def input_back_kernel(
    place, inputs, middle_grad, own, other, gain, input_grad, rounded, gain_grad
):
    one_grad = own[...] + other[...].astype(jnp.float32)
    values = inputs[...].astype(jnp.float32)
    _, factor = norm_rows(values, gain[...])
    add_gain(gain_grad, one_grad * values * factor)
    grads = middle_grad[...] + norm_back(values, factor, gain[...], one_grad)
    input_grad[...] = grads
    rounded[...] = grads.astype(jnp.bfloat16)


def output_kernel(
    place, middle, own_low, own_high, x_low, x_high, y_low, y_high, output
):
    total_out = choose(own_low, own_high) + choose(x_low, x_high) + choose(y_low, y_high)
    output[...] = (middle[...] + total_out).astype(jnp.bfloat16)


def exchange(values, bit):
    return lax.ppermute(values, "dp", [(i, i ^ bit) for i in range(8)])


def swap_halves(values):
    pairs = []
    for i in range(8):
        for m in range(4):
            if (i & 1) != (m & 1):
                pairs.append((i * 4 + m, (i ^ 1) * 4 + (m ^ 1)))
    return lax.ppermute(values, ("dp", "mp"), pairs)


def after(values, earlier):
    return lax.optimization_barrier((values, earlier))[0]


def gather_weights(block):
    half = block.shape[0] // 2
    over_x = exchange(block, 2)
    over_y = exchange(block, 4)
    return [
        block,
        over_x,
        over_y,
        exchange(over_x[:half], 4),
        exchange(over_y[half:], 2),
    ]


def gather_near(low, high):
    return [exchange(low, 2), exchange(high, 2), exchange(low, 4), exchange(high, 4)]


def gather_far(near):
    return [exchange(near[0], 4), exchange(near[3], 2)]


def both_cores(halves):
    return list(halves) + [exchange(half, 1) for half in halves]


def add_low(left, right):
    return (left.astype(jnp.float32) + right.astype(jnp.float32)).astype(jnp.bfloat16)


def pick(values, index, width, axis):
    return lax.dynamic_slice_in_dim(values, index * width, width, axis)


def in_order(own, other, core, axis=0):
    return jnp.where(
        core == 0,
        jnp.concatenate([own, other], axis),
        jnp.concatenate([other, own], axis),
    )


def total(values):
    for bit in (1, 2, 4):
        values = values + exchange(values, bit)
    for bit in (1, 2):
        values = values + lax.ppermute(values, "mp", [(i, i ^ bit) for i in range(4)])
    return values


def fast(
    layer_input,
    out_grad,
    norm_attn,
    query_norm,
    key_norm,
    w_query,
    key_matrix,
    value_matrix,
    w_output,
    norm_mlp,
    w_gate,
    w_up,
    w_down,
):
    bf16, f32 = jnp.bfloat16, jnp.float32
    device = lax.axis_index("dp")
    core = device & 1
    place = jnp.reshape(device >> 1, (1,)).astype(jnp.int32)
    core_index = jnp.reshape(core, (1,)).astype(jnp.int32)
    crossing = core != (lax.axis_index("mp") & 1)
    planes = 4
    rows = layer_input.shape[0]
    width = layer_input.shape[1]
    units = w_gate.shape[1] // 8
    array = jax.ShapeDtypeStruct

    query_cols = w_query.shape[1] // 2
    key_cols = key_matrix.shape[1] // 2

    def heads_of(which):
        return jnp.concatenate(
            [
                pick(w_query, which, query_cols, 1),
                pick(key_matrix, which, key_cols, 1),
                pick(value_matrix, which, key_cols, 1),
            ],
            1,
        )

    qkv_pair = in_order(heads_of(core), exchange(heads_of(1 - core), 1), core)
    out_rows = w_output.shape[0] // 2
    out_pair = in_order(
        pick(w_output, core, out_rows, 0),
        exchange(pick(w_output, 1 - core, out_rows, 0), 1),
        core,
        1,
    )
    qkv_z = lax.all_gather(qkv_pair, "mp", axis=1, tiled=True)
    out_z = lax.all_gather(out_pair, "mp", axis=0, tiled=True)

    pieces = jnp.concatenate(
        [w.reshape(8, units, w.shape[1]) for w in (w_gate.T, w_up.T, w_down)], 1
    )
    feed_own = lax.all_to_all(pieces, "dp", 0, 0)
    feed_own = jnp.swapaxes(feed_own, 0, 1).reshape(3 * units, width)

    inputs = jnp.where(crossing, swap_halves(layer_input), layer_input)
    cotangent = jnp.where(crossing, swap_halves(out_grad), out_grad)

    qkv_z = after(qkv_z, feed_own)
    qkv_chips = gather_weights(qkv_z)
    out_z = after(out_z, qkv_chips)
    out_chips = gather_weights(out_z)
    gate_up = lax.all_gather(feed_own[: 2 * units], "mp", axis=0)
    down = lax.all_gather(feed_own[2 * units :], "mp", axis=0)

    gain_one, gain_two = norm_attn[None, :], norm_mlp[None, :]
    gain_query, gain_key = query_norm[None, :], key_norm[None, :]
    (normed,) = tile_call(
        first_norm_kernel,
        place,
        [(inputs, "rows"), (gain_one, 1)],
        [(array((rows, width), bf16), "rows")],
        4,
    )
    normed_other = exchange(normed, 1)
    cosines, sines = wide_tables(2 * rows)
    proj, query_rot, key_rot, value_low, attended, log_total = attend(
        core_index,
        normed,
        normed_other,
        qkv_chips,
        cosines,
        sines,
        gain_query,
        gain_key,
        planes,
        query_cols,
    )
    branch_own, branch_other = columns(place, attended, out_chips, False)
    middle, tokens_low, tokens_high = tile_call(
        middle_kernel,
        place,
        [(inputs, "rows"), (branch_own, "rows"), (exchange(branch_other, 1), "rows"), (gain_two, 1)],
        [
            (array((rows, width), f32), "rows"),
            (array((rows // 2, width), bf16), "low"),
            (array((rows // 2, width), bf16), "high"),
        ],
        14,
    )

    grads_low, grads_high = after(
        (cotangent[: rows // 2], cotangent[rows // 2 :]), (out_chips[1], out_chips[2])
    )
    grads_near = gather_near(grads_low, grads_high)
    tokens_near = gather_near(tokens_low, tokens_high)
    tokens_far = gather_far(tokens_near)
    grads_far = gather_far(after(grads_near, tokens_near))

    def quarters(low, high, near, far):
        halves = [[low, high], near[:2], near[2:], far]
        return [[(half, 0) for half in both_cores(pair)] for pair in halves]

    token_blocks = quarters(tokens_low, tokens_high, tokens_near, tokens_far)
    grad_blocks = quarters(grads_low, grads_high, grads_near, grads_far)
    kept = None
    outs, twos = [], []
    for k in range(4):
        made = feed(k, kept, token_blocks[k], grad_blocks[k], gate_up, down)
        kept, out_tiles, two_tiles = made[:5], made[5:9], made[9:]
        outs.append(out_tiles)
        twos.append([add_low(two_tiles[n], exchange(two_tiles[n + 2], 1)) for n in range(2)])
    all_tokens, all_grads, all_hidden, all_gate, all_up = kept

    def collect(blocks):
        (own, over_x, over_y, corner) = blocks
        x_high = exchange(over_x[1], 2)
        y_low = exchange(over_y[0], 4)
        low = exchange(corner[0], 4)
        high = exchange(corner[1], 2)
        x_low = exchange(add_low(over_x[0], low), 2)
        y_high = exchange(add_low(over_y[1], high), 4)
        return [own[0], own[1], x_low, x_high, y_low, y_high]

    two_parts = collect(twos)
    gate_weight_grad = dot_first(all_gate, all_tokens).astype(bf16)
    up_weight_grad = dot_first(all_up, all_tokens).astype(bf16)
    down_grad = dot_first(all_hidden, all_grads).astype(bf16)
    outs = after(outs, two_parts)
    out_parts = collect(
        [[add_low(tiles[n], exchange(tiles[n + 2], 1)) for n in range(2)] for tiles in outs]
    )
    halves = ("low", "high") * 3
    middle_grad, branch, gain_two_part = tile_call(
        middle_back_kernel,
        place,
        [(middle, "rows"), (cotangent, "rows"), *zip(two_parts, halves), (gain_two, 1)],
        [
            (array((rows, width), f32), "rows"),
            (array((rows, width), bf16), "rows"),
            (array((8, width), f32), 8),
        ],
        18,
    )

    def over_z(grad):
        return lax.psum_scatter(grad, "mp", scatter_dimension=0, tiled=True)

    def unspread(own):
        pieces = jnp.swapaxes(own.reshape(own.shape[0], 8, -1), 0, 1)
        return lax.all_to_all(pieces, "dp", 0, 0)

    gate_up_own = unspread(
        jnp.concatenate([over_z(gate_weight_grad), over_z(up_weight_grad)], 0)
    )
    gate_own = gate_up_own[:, :units].reshape(8 * units, -1).T.astype(f32)
    up_own = gate_up_own[:, units:].reshape(8 * units, -1).T.astype(f32)
    down_own = unspread(over_z(down_grad)).reshape(8 * units, -1).astype(f32)

    branch_pair = exchange(branch, 1)
    proj_grad, head_gains = attend_back(
        core_index,
        branch,
        branch_pair,
        out_chips,
        cosines,
        sines,
        gain_query,
        gain_key,
        (proj, query_rot, key_rot, value_low, log_total),
        planes,
        query_cols,
    )

    def chip_grads(left, right, along):
        blocks = []
        for k in range(4):
            pair = []
            for n in range(2):
                if along == 0:
                    part = left.shape[1] // 8
                    first = left[:, (2 * k + n) * part : (2 * k + n + 1) * part]
                    pair.append(dot_first(first, right))
                else:
                    part, depth = right.shape[1] // 4, left.shape[1] // 2
                    first = left[:, n * depth : (n + 1) * depth]
                    pair.append(dot_first(first, right[:, k * part : (k + 1) * part]))
            blocks.append([half.astype(bf16) for half in pair])
        return blocks

    def gathered(parts):
        own_low, own_high, x_low, x_high, y_low, y_high = [p.astype(f32) for p in parts]
        return jnp.concatenate(
            [own_low + x_low + y_low, own_high + x_high + y_high], 0
        ).astype(bf16)

    branch_all = jnp.concatenate([branch, branch_pair], 0)
    out_sum = over_z(gathered(collect(chip_grads(attended, branch_all, 1))))
    normed_all = jnp.concatenate([normed, normed_other], 0)
    one_own, one_other = columns(place, proj_grad, qkv_chips, True)
    qkv_sum = lax.psum_scatter(
        gathered(collect(chip_grads(normed_all, proj_grad, 0))),
        "mp",
        scatter_dimension=1,
        tiled=True,
    )
    input_grad, rounded_grad, gain_one_part = tile_call(
        input_back_kernel,
        place,
        [
            (inputs, "rows"),
            (middle_grad, "rows"),
            (one_own, "rows"),
            (exchange(one_other, 1), "rows"),
            (gain_one, 1),
        ],
        [
            (array((rows, width), f32), "rows"),
            (array((rows, width), bf16), "rows"),
            (array((8, width), f32), 8),
        ],
        18,
    )
    (layer_output,) = tile_call(
        output_kernel,
        place,
        [(middle, "rows"), *zip(out_parts, halves)],
        [(array((rows, width), bf16), "rows")],
        12,
    )
    pair_rows = qkv_sum.shape[0] // 2
    qkv_other = exchange(pick(qkv_sum, 1 - core, pair_rows, 0), 1)
    qkv_own = pick(qkv_sum, core, pair_rows, 0)

    def both(start, stop):
        return in_order(qkv_own[:, start:stop], qkv_other[:, start:stop], core, 1).astype(f32)

    pair_cols = out_sum.shape[1] // 2
    out_other = exchange(pick(out_sum, 1 - core, pair_cols, 1), 1)
    out_own = pick(out_sum, core, pair_cols, 1)
    gain_sums = total(
        jnp.concatenate(
            [
                jnp.sum(gain_one_part, 0),
                jnp.sum(head_gains[:8], 0),
                jnp.sum(head_gains[8:], 0),
                jnp.sum(gain_two_part, 0),
            ]
        )
    )
    return (
        jnp.where(crossing, swap_halves(layer_output), layer_output),
        jnp.where(crossing, swap_halves(rounded_grad).astype(f32), input_grad),
        gain_sums[:width],
        gain_sums[width : width + HEAD_SIZE],
        gain_sums[width + HEAD_SIZE : width + 2 * HEAD_SIZE],
        both(0, query_cols),
        both(query_cols, query_cols + key_cols),
        both(query_cols + key_cols, query_cols + 2 * key_cols),
        in_order(out_own, out_other, core, 0).astype(f32),
        gain_sums[width + 2 * HEAD_SIZE :],
        gate_own,
        up_own,
        down_own,
    )


def solution(mesh):
    in_specs = (
        P(("dp", "mp"), None),
        P(("dp", "mp"), None),
        P(),
        P(),
        P(),
        P("dp", "mp"),
        P("dp", "mp"),
        P("dp", "mp"),
        P("mp", "dp"),
        P(),
        P("dp", "mp"),
        P("dp", "mp"),
        P("mp", "dp"),
    )
    out_specs = (
        P(("dp", "mp"), None),
        P(("dp", "mp"), None),
        P(),
        P(),
        P(),
        P("dp", "mp"),
        P("dp", "mp"),
        P("dp", "mp"),
        P("mp", "dp"),
        P(),
        P("dp", "mp"),
        P("dp", "mp"),
        P("mp", "dp"),
    )
    whole_sequences = dict(mesh.shape) == {"dp": 8, "mp": 4}
    local = fast if whole_sequences else generic
    return jax.shard_map(local, mesh=mesh, in_specs=in_specs, out_specs=out_specs, check_vma=False)
```

```python
import functools

import jax
import jax.numpy as jnp
from jax import lax
from jax.experimental import pallas as pl
from jax.experimental.pallas import tpu as pltpu
from jax.sharding import PartitionSpec as P

HEAD_SIZE = 128
SEQUENCE_LENGTH = 1024


EPSILON = 1e-06
THETA = 1000000.0


def norm_rows(values, gain):
    factor = lax.rsqrt(jnp.mean(values * values, -1, keepdims=True) + EPSILON)
    return (values * factor * gain, factor)


def norm_back(values, factor, gain, upstream):
    scaled = upstream * gain
    inner = jnp.mean(scaled * values, -1, keepdims=True)
    return factor * scaled - values * (factor * factor * factor) * inner


def tables(length, width):
    half_width = width // 2
    frequencies = THETA ** (-(jnp.arange(half_width, dtype=jnp.float32) * 2.0 / width))
    angles = jnp.arange(length, dtype=jnp.float32)[:, None] * frequencies[None, :]
    return (jnp.cos(angles), jnp.sin(angles))


def rotate(values, cosine_table, sine_table):
    half_width = values.shape[-1] // 2
    first_half = values[..., :half_width]
    second_half = values[..., half_width:]
    cosine_part = cosine_table[:, None, :]
    sine_part = sine_table[:, None, :]
    return jnp.concatenate(
        [
            first_half * cosine_part - second_half * sine_part,
            second_half * cosine_part + first_half * sine_part,
        ],
        -1,
    )


def rotate_back(grads, cosine_table, sine_table):
    half_width = grads.shape[-1] // 2
    first_half = grads[..., :half_width]
    second_half = grads[..., half_width:]
    cosine_part = cosine_table[:, None, :]
    sine_part = sine_table[:, None, :]
    return jnp.concatenate(
        [
            first_half * cosine_part + second_half * sine_part,
            second_half * cosine_part - first_half * sine_part,
        ],
        -1,
    )


def matmul(left, right):
    return jnp.dot(left, right, preferred_element_type=jnp.float32)


def dot_last(left, right):
    return lax.dot_general(
        left, right, (((1,), (1,)), ((), ())), preferred_element_type=jnp.float32
    )


def dot_first(left, right):
    return lax.dot_general(
        left, right, (((0,), (0,)), ((), ())), preferred_element_type=jnp.float32
    )


def masked_scores(query_block, keys, start, block_rows, scale):
    raw = (
        jnp.einsum("qhgd,khd->hgqk", query_block, keys, preferred_element_type=jnp.float32) * scale
    )
    query_places = start + jnp.arange(block_rows)[:, None]
    key_places = jnp.arange(keys.shape[0])[None, :]
    return jnp.where(key_places <= query_places, raw, -jnp.inf)


def generic(
    layer_input,
    out_grad,
    norm_attn,
    query_norm,
    key_norm,
    w_query,
    key_matrix,
    value_matrix,
    w_output,
    norm_mlp,
    w_gate,
    w_up,
    w_down,
):
    inputs = layer_input.astype(jnp.float32)
    query_full, key_full, value_full, output_full = (
        lax.all_gather(w_query, "dp", axis=0, tiled=True),
        lax.all_gather(key_matrix, "dp", axis=0, tiled=True),
        lax.all_gather(value_matrix, "dp", axis=0, tiled=True),
        lax.all_gather(w_output, "dp", axis=1, tiled=True),
    )
    first_normed, factor_one = norm_rows(inputs, norm_attn)
    normed_all = lax.all_gather(first_normed.astype(jnp.bfloat16), "mp", axis=0, tiled=True)
    total_rows = normed_all.shape[0]
    sequence_batch = total_rows // SEQUENCE_LENGTH
    query_heads = query_full.shape[1] // HEAD_SIZE
    shared_heads = key_full.shape[1] // HEAD_SIZE
    heads_per_group = query_heads // shared_heads
    query_proj = matmul(normed_all, query_full).reshape(
        sequence_batch, SEQUENCE_LENGTH, query_heads, HEAD_SIZE
    )
    key_projected = matmul(normed_all, key_full).reshape(
        sequence_batch, SEQUENCE_LENGTH, shared_heads, HEAD_SIZE
    )
    value_low = (
        matmul(normed_all, value_full)
        .astype(jnp.bfloat16)
        .reshape(sequence_batch, SEQUENCE_LENGTH, shared_heads, HEAD_SIZE)
    )
    cosine_table, sine_table = tables(SEQUENCE_LENGTH, HEAD_SIZE)
    query_normed, query_factor = norm_rows(query_proj, query_norm)
    query_rotated = rotate(query_normed, cosine_table, sine_table).astype(jnp.bfloat16)
    query_rotated = query_rotated.reshape(
        sequence_batch, SEQUENCE_LENGTH, shared_heads, heads_per_group, HEAD_SIZE
    )
    key_normed, key_factor = norm_rows(key_projected, key_norm)
    key_rot = rotate(key_normed, cosine_table, sine_table).astype(jnp.bfloat16)
    block_rows = min(512, SEQUENCE_LENGTH)
    block_count = SEQUENCE_LENGTH // block_rows
    scale = HEAD_SIZE ** (-0.5)
    attended_pieces = []
    log_totals = []
    for seq_index in range(sequence_batch):
        for block_index in range(block_count):
            start = block_index * block_rows
            query_block = query_rotated[seq_index, start : start + block_rows]
            scores = masked_scores(query_block, key_rot[seq_index], start, block_rows, scale)
            largest = jnp.max(scores, -1, keepdims=True)
            expanded = jnp.exp(scores - largest)
            summed = jnp.sum(expanded, -1, keepdims=True)
            probs_low = (expanded / summed).astype(jnp.bfloat16)
            block_out = jnp.einsum(
                "hgqk,khd->qhgd",
                probs_low,
                value_low[seq_index],
                preferred_element_type=jnp.float32,
            )
            attended_pieces.append(block_out.reshape(block_rows, query_heads * HEAD_SIZE))
            log_totals.append(largest + jnp.log(summed))
    attended = jnp.concatenate(attended_pieces, 0).astype(jnp.bfloat16)
    attn_sum = lax.psum_scatter(
        matmul(attended, output_full), "mp", scatter_dimension=0, tiled=True
    )
    middle = inputs + attn_sum
    gate_full, up_full, down_full = (
        lax.all_gather(w_gate, "dp", axis=0, tiled=True),
        lax.all_gather(w_up, "dp", axis=0, tiled=True),
        lax.all_gather(w_down, "dp", axis=1, tiled=True),
    )
    normed_two, factor_two = norm_rows(middle, norm_mlp)
    normed_two_all = lax.all_gather(normed_two.astype(jnp.bfloat16), "mp", axis=0, tiled=True)
    gate_value = matmul(normed_two_all, gate_full)
    up_value = matmul(normed_two_all, up_full)
    hidden_low = (jax.nn.silu(gate_value) * up_value).astype(jnp.bfloat16)
    mlp_sum = lax.psum_scatter(
        matmul(hidden_low, down_full).astype(jnp.bfloat16), "mp", scatter_dimension=0, tiled=True
    ).astype(jnp.float32)
    layer_output = (middle + mlp_sum).astype(jnp.bfloat16)
    grad_rows = lax.all_gather(out_grad, "mp", axis=0, tiled=True)
    gate_back, up_back, down_back = (
        lax.all_gather(w_gate, "dp", axis=0, tiled=True),
        lax.all_gather(w_up, "dp", axis=0, tiled=True),
        lax.all_gather(w_down, "dp", axis=1, tiled=True),
    )
    hidden_grad = dot_last(grad_rows, down_back)
    down_grad = dot_first(hidden_low, grad_rows)
    sigmoid_gate = jax.nn.sigmoid(gate_value)
    gate_grad = (
        hidden_grad * up_value * sigmoid_gate * (1.0 + gate_value * (1.0 - sigmoid_gate))
    ).astype(jnp.bfloat16)
    up_grad = (hidden_grad * gate_value * sigmoid_gate).astype(jnp.bfloat16)
    gate_weight_grad = dot_first(normed_two_all, gate_grad)
    up_weight_grad = dot_first(normed_two_all, up_grad)
    two_grad = lax.psum_scatter(
        dot_last(gate_grad, gate_back) + dot_last(up_grad, up_back),
        "mp",
        scatter_dimension=0,
        tiled=True,
    )
    gain_two_grad = jnp.sum(two_grad * middle * factor_two, 0)
    middle_grad = out_grad.astype(jnp.float32) + norm_back(middle, factor_two, norm_mlp, two_grad)
    mlp_grads = (
        lax.psum_scatter(
            gate_weight_grad.astype(jnp.bfloat16), "dp", scatter_dimension=0, tiled=True
        ).astype(jnp.float32),
        lax.psum_scatter(
            up_weight_grad.astype(jnp.bfloat16), "dp", scatter_dimension=0, tiled=True
        ).astype(jnp.float32),
        lax.psum_scatter(
            down_grad.astype(jnp.bfloat16), "dp", scatter_dimension=1, tiled=True
        ).astype(jnp.float32),
    )
    branch_all = lax.all_gather(middle_grad.astype(jnp.bfloat16), "mp", axis=0, tiled=True)
    output_weight_grad = dot_first(attended, branch_all)
    attended_grad = dot_last(branch_all, output_full).astype(jnp.bfloat16)
    attended_grad = attended_grad.reshape(
        sequence_batch, SEQUENCE_LENGTH, shared_heads, heads_per_group, HEAD_SIZE
    )
    query_grad_seqs = []
    key_grad_seqs = []
    value_grad_seqs = []
    for seq_index in range(sequence_batch):
        key_running = jnp.zeros((SEQUENCE_LENGTH, shared_heads, HEAD_SIZE), jnp.float32)
        value_running = jnp.zeros((SEQUENCE_LENGTH, shared_heads, HEAD_SIZE), jnp.float32)
        query_blocks = []
        for block_index in range(block_count):
            start = block_index * block_rows
            query_block = query_rotated[seq_index, start : start + block_rows]
            scores = masked_scores(query_block, key_rot[seq_index], start, block_rows, scale)
            probs_full = jnp.exp(scores - log_totals[seq_index * block_count + block_index])
            probs_low = probs_full.astype(jnp.bfloat16)
            grad_block = attended_grad[seq_index, start : start + block_rows]
            prob_grad = jnp.einsum(
                "qhgd,khd->hgqk",
                grad_block,
                value_low[seq_index],
                preferred_element_type=jnp.float32,
            )
            row_inner = jnp.sum(probs_full * prob_grad, -1, keepdims=True)
            score_grad = (probs_full * (prob_grad - row_inner)).astype(jnp.bfloat16)
            query_blocks.append(
                jnp.einsum(
                    "hgqk,khd->qhgd",
                    score_grad,
                    key_rot[seq_index],
                    preferred_element_type=jnp.float32,
                )
                * scale
            )
            key_running = (
                key_running
                + jnp.einsum(
                    "hgqk,qhgd->khd", score_grad, query_block, preferred_element_type=jnp.float32
                )
                * scale
            )
            value_running = value_running + jnp.einsum(
                "hgqk,qhgd->khd", probs_low, grad_block, preferred_element_type=jnp.float32
            )
        query_grad_seqs.append(jnp.concatenate(query_blocks, 0))
        key_grad_seqs.append(key_running)
        value_grad_seqs.append(value_running)
    rot_query_grad = jnp.stack(query_grad_seqs, 0).reshape(
        sequence_batch, SEQUENCE_LENGTH, query_heads, HEAD_SIZE
    )
    rot_key_grad = jnp.stack(key_grad_seqs, 0)
    value_grad = (
        jnp.stack(value_grad_seqs, 0)
        .reshape(total_rows, shared_heads * HEAD_SIZE)
        .astype(jnp.bfloat16)
    )
    query_normed_grad = rotate_back(rot_query_grad, cosine_table, sine_table)
    query_gain_grad = jnp.sum(query_normed_grad * query_proj * query_factor, (0, 1, 2))
    query_grad = norm_back(query_proj, query_factor, query_norm, query_normed_grad)
    query_grad = query_grad.reshape(total_rows, query_heads * HEAD_SIZE).astype(jnp.bfloat16)
    key_normed_grad = rotate_back(rot_key_grad, cosine_table, sine_table)
    key_gain_grad = jnp.sum(key_normed_grad * key_projected * key_factor, (0, 1, 2))
    key_grad = norm_back(key_projected, key_factor, key_norm, key_normed_grad)
    key_grad = key_grad.reshape(total_rows, shared_heads * HEAD_SIZE).astype(jnp.bfloat16)
    query_weight_grad = dot_first(normed_all, query_grad)
    key_weight_grad = dot_first(normed_all, key_grad)
    value_weight_grad = dot_first(normed_all, value_grad)
    one_partial = (
        dot_last(query_grad, query_full)
        + dot_last(key_grad, key_full)
        + dot_last(value_grad, value_full)
    )
    one_grad = lax.psum_scatter(
        one_partial.astype(jnp.bfloat16), "mp", scatter_dimension=0, tiled=True
    ).astype(jnp.float32)
    gain_one_grad = jnp.sum(one_grad * inputs * factor_one, 0)
    input_grad = middle_grad + norm_back(inputs, factor_one, norm_attn, one_grad)
    attn_grads = (
        lax.psum_scatter(
            query_weight_grad.astype(jnp.bfloat16), "dp", scatter_dimension=0, tiled=True
        ).astype(jnp.float32),
        lax.psum_scatter(
            key_weight_grad.astype(jnp.bfloat16), "dp", scatter_dimension=0, tiled=True
        ).astype(jnp.float32),
        lax.psum_scatter(
            value_weight_grad.astype(jnp.bfloat16), "dp", scatter_dimension=0, tiled=True
        ).astype(jnp.float32),
        lax.psum_scatter(
            output_weight_grad.astype(jnp.bfloat16), "dp", scatter_dimension=1, tiled=True
        ).astype(jnp.float32),
    )
    gain_sums = lax.psum(
        (gain_one_grad, query_gain_grad, key_gain_grad, gain_two_grad), ("dp", "mp")
    )
    return (
        layer_output,
        input_grad,
        gain_sums[0],
        gain_sums[1],
        gain_sums[2],
        attn_grads[0],
        attn_grads[1],
        attn_grads[2],
        attn_grads[3],
        gain_sums[3],
        mlp_grads[0],
        mlp_grads[1],
        mlp_grads[2],
    )


ROW_BLOCK = 256


def wide_tables(length):
    cosine_table, sine_table = tables(length, HEAD_SIZE)
    return (
        jnp.concatenate([cosine_table, cosine_table], 1),
        jnp.concatenate([-sine_table, sine_table], 1),
    )


def turn(values, cosines, sines):
    return values * cosines + pltpu.roll(values, HEAD_SIZE // 2, 1) * sines


def turn_back(values, cosines, sines):
    return values * cosines - pltpu.roll(values, HEAD_SIZE // 2, 1) * sines


def causal(rows):
    query_places = lax.broadcasted_iota(jnp.int32, (rows, rows), 0)
    key_places = lax.broadcasted_iota(jnp.int32, (rows, rows), 1)
    return key_places <= query_places


def attend_kernel(
    core, own, other, w0, w1, w2, w3_low, w3_high, cosines, sines, query_gain, key_gain,
    proj, query_rot, key_rot, value, attended, log_total,
):
    half = own.shape[0]
    length = 2 * half
    scale = HEAD_SIZE ** (-0.5)
    query_cols = query_rot.shape[1]
    heads = query_cols // HEAD_SIZE
    for h in range(2):
        here = core[0] == h
        rows = slice(h * half, (h + 1) * half)
        block = None
        start = 0
        for weight in (w0, w1, w2, w3_low, w3_high):
            cols = slice(start, start + weight.shape[0])
            start = cols.stop
            tokens = jnp.where(here, own[:, cols], other[:, cols])
            term = matmul(tokens, weight[...])
            block = term if block is None else block + term
        proj[rows, :] = block
        cos_rows, sin_rows = cosines[rows, :], sines[rows, :]
        for head in range(heads):
            cols = slice(head * HEAD_SIZE, (head + 1) * HEAD_SIZE)
            normed, _ = norm_rows(block[:, cols], query_gain[...])
            query_rot[rows, cols] = turn(normed, cos_rows, sin_rows).astype(jnp.bfloat16)
        cols = slice(query_cols, query_cols + HEAD_SIZE)
        normed, _ = norm_rows(block[:, cols], key_gain[...])
        key_rot[rows, :] = turn(normed, cos_rows, sin_rows).astype(jnp.bfloat16)
        value[rows, :] = block[:, query_cols + HEAD_SIZE :].astype(jnp.bfloat16)
    allowed = causal(ROW_BLOCK)

    def place(start):
        return pl.ds(pl.multiple_of((start + core[0] * half) % length, ROW_BLOCK), ROW_BLOCK)

    lane = lax.broadcasted_iota(jnp.int32, (ROW_BLOCK, HEAD_SIZE), 1)
    for start in range(0, length, ROW_BLOCK):
        rows = slice(start, start + ROW_BLOCK)
        logs = jnp.zeros((ROW_BLOCK, HEAD_SIZE), jnp.float32)
        for head in range(heads):
            cols = slice(head * HEAD_SIZE, (head + 1) * HEAD_SIZE)
            query = query_rot[rows, cols]
            scores = [jnp.where(allowed, dot_last(query, key_rot[rows, :]) * scale, -jnp.inf)]
            if start:
                scores.append(dot_last(query, key_rot[:start, :]) * scale)
            largest = functools.reduce(
                jnp.maximum, [jnp.max(s, -1, keepdims=True) for s in scores]
            )
            expanded = [jnp.exp(s - largest) for s in scores]
            summed = sum(jnp.sum(e, -1, keepdims=True) for e in expanded)
            out = matmul(expanded[0].astype(jnp.bfloat16), value[rows, :])
            if start:
                out = out + matmul(expanded[1].astype(jnp.bfloat16), value[:start, :])
            attended[place(start), cols] = (out / summed).astype(jnp.bfloat16)
            logs = jnp.where(lane == head, largest + jnp.log(summed), logs)
        log_total[rows, :] = logs


def attend(core, own, other, weights, cosines, sines, query_gain, key_gain, planes, query_cols):
    half, width = own.shape
    length = 2 * half
    cols = weights[0].shape[1]
    group = cols // planes
    whole = lambda shape: pl.BlockSpec(shape, lambda g, core: (0, 0))
    column = lambda rows, width: pl.BlockSpec((rows, width), lambda g, core: (0, g))
    shape = jax.ShapeDtypeStruct
    return pl.pallas_call(
        attend_kernel,
        grid_spec=pltpu.PrefetchScalarGridSpec(
            num_scalar_prefetch=1,
            grid=(planes,),
            in_specs=[whole((half, width))] * 2
            + [column(weight.shape[0], group) for weight in weights]
            + [whole((length, HEAD_SIZE))] * 2
            + [whole((1, HEAD_SIZE))] * 2,
            out_specs=[
                column(length, group),
                column(length, query_cols),
                column(length, HEAD_SIZE),
                column(length, HEAD_SIZE),
                column(length, query_cols),
                column(length, HEAD_SIZE),
            ],
        ),
        out_shape=[
            shape((length, cols), jnp.float32),
            shape((length, planes * query_cols), jnp.bfloat16),
            shape((length, planes * HEAD_SIZE), jnp.bfloat16),
            shape((length, planes * HEAD_SIZE), jnp.bfloat16),
            shape((length, planes * query_cols), jnp.bfloat16),
            shape((length, planes * HEAD_SIZE), jnp.float32),
        ],
        compiler_params=pltpu.CompilerParams(vmem_limit_bytes=56 * 2**20),
        cost_estimate=pl.CostEstimate(
            flops=2 * length * width * cols + 3 * planes * query_cols * length**2,
            bytes_accessed=30 * 2**20,
            transcendentals=planes * 2 * length**2,
        ),
    )(core, own, other, *weights, cosines, sines, query_gain, key_gain)


def attend_back_kernel(
    core, own, other, o0, o1, o2, o3_low, o3_high, cosines, sines, query_gain, key_gain,
    proj, query_rot, key_rot, value, log_total,
    proj_grad, gain_grads, grad, key_total, value_total,
):
    half = own.shape[0]
    length = 2 * half
    part = o0.shape[1]
    scale = HEAD_SIZE ** (-0.5)
    query_cols = query_rot.shape[1]
    heads = query_cols // HEAD_SIZE

    @pl.when(pl.program_id(0) == 0)
    def _():
        gain_grads[...] = jnp.zeros_like(gain_grads)

    low = pl.program_id(0) < pl.num_programs(0) // 2
    corner = jnp.where(low, o3_low[...], o3_high[...])
    for h in range(2):
        here = core[0] == h
        block = None
        for k, weight in enumerate((o0[...], o1[...], o2[...], corner)):
            cols = slice(k * part, (k + 1) * part)
            tokens = jnp.where(here, own[:, cols], other[:, cols])
            term = dot_last(tokens, weight)
            block = term if block is None else block + term
        grad[h * half : (h + 1) * half, :] = block.astype(jnp.bfloat16)
    key_total[...] = jnp.zeros_like(key_total)
    value_total[...] = jnp.zeros_like(value_total)
    allowed = causal(ROW_BLOCK)

    def fold(values):
        return jnp.sum(values.reshape(-1, 8, HEAD_SIZE), 0)

    def place(start):
        return pl.ds(pl.multiple_of((start + core[0] * half) % length, ROW_BLOCK), ROW_BLOCK)

    for start in range(0, length, ROW_BLOCK):
        rows = slice(start, start + ROW_BLOCK)
        for head in range(heads):
            cols = slice(head * HEAD_SIZE, (head + 1) * HEAD_SIZE)
            query = query_rot[rows, cols]
            upstream = grad[rows, cols]
            logs = log_total[rows, head : head + 1]
            spans = [rows] + ([slice(0, start)] if start else [])
            probs, prob_grads = [], []
            for n, span in enumerate(spans):
                raw = dot_last(query, key_rot[span, :]) * scale
                if n == 0:
                    raw = jnp.where(allowed, raw, -jnp.inf)
                probs.append(jnp.exp(raw - logs))
                prob_grads.append(dot_last(upstream, value[span, :]))
            inner = sum(jnp.sum(p * d, -1, keepdims=True) for p, d in zip(probs, prob_grads))
            query_back = None
            for span, p, d in zip(spans, probs, prob_grads):
                score_grad = (p * (d - inner)).astype(jnp.bfloat16)
                term = matmul(score_grad, key_rot[span, :])
                query_back = term if query_back is None else query_back + term
                key_total[span, :] += dot_first(score_grad, query)
                value_total[span, :] += dot_first(p.astype(jnp.bfloat16), upstream)
            normed_grad = turn_back(query_back * scale, cosines[rows, :], sines[rows, :])
            values = proj[rows, cols]
            _, factor = norm_rows(values, query_gain[...])
            gain_grads[:8, :] += fold(normed_grad * values * factor)
            back = norm_back(values, factor, query_gain[...], normed_grad)
            proj_grad[place(start), cols] = back.astype(jnp.bfloat16)
    for start in range(0, length, ROW_BLOCK):
        rows = slice(start, start + ROW_BLOCK)
        cols = slice(query_cols, query_cols + HEAD_SIZE)
        normed_grad = turn_back(key_total[rows, :] * scale, cosines[rows, :], sines[rows, :])
        values = proj[rows, cols]
        _, factor = norm_rows(values, key_gain[...])
        gain_grads[8:, :] += fold(normed_grad * values * factor)
        back = norm_back(values, factor, key_gain[...], normed_grad)
        proj_grad[place(start), cols] = back.astype(jnp.bfloat16)
        proj_grad[place(start), query_cols + HEAD_SIZE :] = value_total[rows, :].astype(
            jnp.bfloat16
        )


def attend_back(
    core, own, other, weights, cosines, sines, query_gain, key_gain, saved, planes, query_cols
):
    half, width = own.shape
    length = 2 * half
    part = weights[0].shape[1]
    proj, query_rot, key_rot, value, log_total = saved
    cols = proj.shape[1]
    group = cols // planes
    whole = lambda shape: pl.BlockSpec(shape, lambda g, core: (0, 0))
    column = lambda rows, width: pl.BlockSpec((rows, width), lambda g, core: (0, g))
    shape = jax.ShapeDtypeStruct
    return pl.pallas_call(
        attend_back_kernel,
        grid_spec=pltpu.PrefetchScalarGridSpec(
            num_scalar_prefetch=1,
            grid=(planes,),
            in_specs=[whole((half, width))] * 2
            + [pl.BlockSpec((query_cols, part), lambda g, core: (g, 0))] * 3
            + [
                pl.BlockSpec((query_cols, part), lambda g, core: (jnp.minimum(g, 1), 0)),
                pl.BlockSpec((query_cols, part), lambda g, core: (jnp.maximum(g - 2, 0), 0)),
            ]
            + [whole((length, HEAD_SIZE))] * 2
            + [whole((1, HEAD_SIZE))] * 2
            + [
                column(length, group),
                column(length, query_cols),
                column(length, HEAD_SIZE),
                column(length, HEAD_SIZE),
                column(length, HEAD_SIZE),
            ],
            out_specs=[column(length, group), whole((16, HEAD_SIZE))],
            scratch_shapes=[
                pltpu.VMEM((length, query_cols), jnp.bfloat16),
                pltpu.VMEM((length, HEAD_SIZE), jnp.float32),
                pltpu.VMEM((length, HEAD_SIZE), jnp.float32),
            ],
        ),
        out_shape=[
            shape((length, cols), jnp.bfloat16),
            shape((16, HEAD_SIZE), jnp.float32),
        ],
        compiler_params=pltpu.CompilerParams(vmem_limit_bytes=56 * 2**20),
        cost_estimate=pl.CostEstimate(
            flops=length * width * cols + 8 * planes * query_cols * length**2,
            bytes_accessed=30 * 2**20,
            transcendentals=planes * 2 * length**2,
        ),
    )(core, own, other, *weights, cosines, sines, query_gain, key_gain, *saved)


MESH = pl.DeviceIdType.MESH


def neighbours():
    me = lax.axis_index("dp")
    x, y = (me // 2) % 2, me // 4
    return me, me + 2 - 4 * x, me + 4 - 8 * y


def greet(others):
    barrier = pltpu.get_barrier_semaphore()
    for other in others:
        pl.semaphore_signal(barrier, inc=1, device_id={"dp": other}, device_id_type=MESH)
    pl.semaphore_wait(barrier, len(others))


def column_places(width):
    me = lax.axis_index("dp")
    core, x, y = me % 2, (me // 2) % 2, me // 4
    block = 256
    places = []
    for n in range(width // block):
        here = core if n < 4 else 1 - core
        far_x = 1 - x if n % 2 else x
        far_y = 1 - y if (n // 2) % 2 else y
        start = (4 * far_y + 2 * far_x + here) * block
        places.append(pl.ds(pl.multiple_of(start, block), block))
    return places


def split_columns(target, values):
    for n, cols in enumerate(column_places(values.shape[1])):
        target[:, n * 256 : (n + 1) * 256] = values[:, cols]


def merge_columns(target, sums):
    for n, cols in enumerate(column_places(sums.shape[1])):
        target[:, cols] = sums[:, n * 256 : (n + 1) * 256].astype(target.dtype)


def both_halves(left, own, other):
    half = own.shape[1]
    return dot_last(left[:, :half], own[...]) + dot_last(left[:, half:], other[...])


def hidden_kernel(
    x_tokens_out, y_tokens_out, x_grads_out, y_grads_out,
    own_tokens, x_tokens, y_tokens, own_grads, x_grads, y_grads,
    gate_own, gate_other, up_own, up_other,
    all_tokens, all_grads, hidden, gate_slope, up_slope,
    far_tokens, far_grads, send, receive,
):
    block, chunk = pl.program_id(0), pl.program_id(1)
    _, over_x, over_y = neighbours()
    half = far_tokens.shape[0] // 2
    low, high = pl.ds(0, half), pl.ds(half, half)
    copies = [
        pltpu.make_async_remote_copy(
            src_ref=source.at[rows],
            dst_ref=target.at[rows],
            send_sem=send.at[n],
            recv_sem=receive.at[n],
            device_id={"dp": other},
            device_id_type=MESH,
        )
        for n, (source, target, rows, other) in enumerate(
            (
                (x_tokens_out, far_tokens, low, over_y),
                (y_tokens_out, far_tokens, high, over_x),
                (x_grads_out, far_grads, low, over_y),
                (y_grads_out, far_grads, high, over_x),
            )
        )
    ]

    @pl.when((block == 0) & (chunk == 0))
    def _():
        greet((over_x, over_y))
        for transfer in copies:
            transfer.start()

    parts = ((own_tokens, own_grads), (x_tokens, x_grads), (y_tokens, y_grads), (far_tokens, far_grads))
    for n, (tokens, grads) in enumerate(parts):

        @pl.when((block == n) & (chunk == 0))
        def _():
            if n == 3:
                for transfer in copies:
                    transfer.wait_recv()
            split_columns(all_tokens, tokens)
            split_columns(all_grads, grads)

    values = all_tokens[...]
    gate = both_halves(values, gate_own, gate_other)
    up = both_halves(values, up_own, up_other)
    sigmoid_gate = 1.0 / (1.0 + jnp.exp(-gate))
    silu = gate * sigmoid_gate
    hidden[...] = (silu * up).astype(jnp.bfloat16)
    gate_slope[...] = (up * sigmoid_gate * (1.0 + gate * (1.0 - sigmoid_gate))).astype(
        jnp.bfloat16
    )
    up_slope[...] = silu.astype(jnp.bfloat16)

    @pl.when((block == 3) & (chunk == pl.num_programs(1) - 1))
    def _():
        for transfer in copies:
            transfer.wait_send()


def gather_hidden(tokens, grads, weights):
    rows, width = tokens[0].shape
    hidden_count, half = weights[0].shape
    chunk = 512
    spec = pl.BlockSpec
    shape = jax.ShapeDtypeStruct
    outside = spec(memory_space=pl.ANY)
    whole = spec((rows, width), lambda b, c: (0, 0), pipeline_mode=pl.Buffered(1))
    bf16 = jnp.bfloat16
    return pl.pallas_call(
        hidden_kernel,
        grid=(4, hidden_count // chunk),
        in_specs=[outside] * 4 + [whole] * 6 + [spec((chunk, half), lambda b, c: (c, 0))] * 4,
        out_specs=[spec((rows, width), lambda b, c: (b, 0))] * 2
        + [spec((rows, chunk), lambda b, c: (b, c))] * 3,
        out_shape=[shape((4 * rows, width), bf16)] * 2 + [shape((4 * rows, hidden_count), bf16)] * 3,
        scratch_shapes=[pltpu.VMEM((rows, width), bf16)] * 2
        + [pltpu.SemaphoreType.DMA((4,)), pltpu.SemaphoreType.DMA((4,))],
        compiler_params=pltpu.CompilerParams(
            collective_id=1, has_side_effects=True, vmem_limit_bytes=60 * 2**20
        ),
        cost_estimate=pl.CostEstimate(
            flops=16 * rows * width * hidden_count,
            bytes_accessed=60 * 2**20,
            transcendentals=4 * rows * hidden_count,
        ),
    )(*tokens[1:], *grads[1:], *tokens, *grads, *weights)


def reduce_copies(corner, send_x, send_y, got_corner, got_x, got_y, send, receive):
    _, over_x, over_y = neighbours()
    half = corner.shape[0] // 2
    low, high = pl.ds(0, half), pl.ds(half, half)
    plan = [
        (corner.at[low], got_corner.at[low], over_y),
        (corner.at[high], got_corner.at[high], over_x),
        (send_y.at[low], got_y.at[low], over_y),
        (send_y.at[high], got_y.at[high], over_y),
        (send_x.at[high], got_x.at[high], over_x),
        (send_x.at[low], got_x.at[low], over_x),
    ]
    return [
        pltpu.make_async_remote_copy(
            src_ref=source,
            dst_ref=target,
            send_sem=send.at[n],
            recv_sem=receive.at[n],
            device_id={"dp": other},
            device_id_type=MESH,
        )
        for n, (source, target, other) in enumerate(plan)
    ]


def corner_copies(corner, got_corner, send, receive, first):
    _, over_x, over_y = neighbours()
    half = corner.shape[0] // 2
    return [
        pltpu.make_async_remote_copy(
            src_ref=corner.at[rows],
            dst_ref=got_corner.at[rows],
            send_sem=send.at[first + n],
            recv_sem=receive.at[first + n],
            device_id={"dp": other},
            device_id_type=MESH,
        )
        for n, (rows, other) in enumerate(
            ((pl.ds(0, half), over_y), (pl.ds(half, half), over_x))
        )
    ]


def add_into(target, rows, other):
    total_rows = target[rows, :].astype(jnp.float32) + other[rows, :].astype(jnp.float32)
    target[rows, :] = total_rows.astype(target.dtype)


def feed_back_kernel(
    grads, hidden, gate_slope, up_slope,
    gate_own, gate_other, up_own, up_other, down_own, down_other,
    gate_grad, up_grad, out_own, out_x, out_y, two_grad,
    out_sum, two_sum, out_corner, keep_x, keep_y, got_out, local, corner, send_x, send_y, got_corner, got_x, got_y, send, receive,
):
    turn_index, chunk = pl.program_id(0), pl.program_id(1)
    last = chunk == pl.num_programs(1) - 1
    rows = grads.shape[0]
    low, high = slice(0, rows // 2), slice(rows // 2, rows)
    copies = reduce_copies(corner, send_x, send_y, got_corner, got_x, got_y, send, receive)
    copies += corner_copies(out_corner, got_out, send, receive, len(copies))
    writes = [
        pltpu.make_async_copy(source, target, local.at[n])
        for n, (source, target) in enumerate(
            ((keep_y, out_y), (keep_x, out_x), (out_corner, out_own))
        )
    ]

    @pl.when((turn_index == 0) & (chunk == 0))
    def _():
        _, over_x, over_y = neighbours()
        greet((over_x, over_y))

    @pl.when(chunk == 0)
    def _():
        out_sum[...] = jnp.zeros_like(out_sum)
        two_sum[...] = jnp.zeros_like(two_sum)

    hidden_grad = both_halves(grads[...], down_own, down_other)
    gate_back = (hidden_grad * gate_slope[...].astype(jnp.float32)).astype(jnp.bfloat16)
    up_back = (hidden_grad * up_slope[...].astype(jnp.float32)).astype(jnp.bfloat16)
    gate_grad[...] = gate_back
    up_grad[...] = up_back
    active = hidden[...]
    half = down_own.shape[1]
    for n, (gate, up, down) in enumerate(
        ((gate_own, up_own, down_own), (gate_other, up_other, down_other))
    ):
        for part in range(0, half, 512):
            cols = slice(part, part + 512)
            place = slice(n * half + part, n * half + part + 512)
            out_sum[:, place] += matmul(active, down[:, cols])
            two_sum[:, place] += matmul(gate_back, gate[:, cols]) + matmul(up_back, up[:, cols])

    @pl.when(last & (turn_index == 0))
    def _():
        merge_columns(corner, two_sum)
        copies[0].start()
        copies[1].start()
        merge_columns(out_corner, out_sum)
        copies[6].start()
        copies[7].start()

    @pl.when(last & (turn_index == 1))
    def _():
        merge_columns(send_y, two_sum)
        copies[2].start()
        merge_columns(keep_y, out_sum)

    @pl.when((chunk == 0) & (turn_index == 2))
    def _():
        copies[1].wait_recv()
        add_into(send_y, high, got_corner)
        copies[3].start()

    @pl.when(last & (turn_index == 2))
    def _():
        merge_columns(send_x, two_sum)
        copies[4].start()
        copies[0].wait_recv()
        add_into(send_x, low, got_corner)
        copies[5].start()
        merge_columns(keep_x, out_sum)
        copies[7].wait_recv()
        add_into(keep_y, high, got_out)
        writes[0].start()

    @pl.when(last & (turn_index == 3))
    def _():
        copies[6].wait_recv()
        add_into(keep_x, low, got_out)
        writes[1].start()
        copies[6].wait_send()
        copies[7].wait_send()
        merge_columns(out_corner, out_sum)
        writes[2].start()
        merge_columns(two_grad, two_sum)
        copies[2].wait_recv()
        copies[3].wait_recv()
        two_grad[...] += got_y[...].astype(jnp.float32)
        copies[4].wait_recv()
        copies[5].wait_recv()
        two_grad[...] += got_x[...].astype(jnp.float32)
        for transfer in copies[:6]:
            transfer.wait_send()
        for write in writes:
            write.wait()


def feed_back(grads, saved, weights):
    rows, width = grads.shape[0] // 4, grads.shape[1]
    hidden_count, half = weights[0].shape
    chunk = 512
    spec = pl.BlockSpec
    shape = jax.ShapeDtypeStruct
    bf16, f32 = jnp.bfloat16, jnp.float32
    block = lambda q, c: (3 - q, 0)
    piece = lambda q, c: (3 - q, c)
    return pl.pallas_call(
        feed_back_kernel,
        grid=(4, hidden_count // chunk),
        in_specs=[spec((rows, width), block)]
        + [spec((rows, chunk), piece)] * 3
        + [spec((chunk, half), lambda q, c: (c, 0))] * 6,
        out_specs=[spec((rows, chunk), piece)] * 2
        + [spec(memory_space=pl.ANY)] * 3
        + [spec((rows, width), lambda q, c: (0, 0))],
        out_shape=[shape((4 * rows, hidden_count), bf16)] * 2
        + [shape((rows, width), bf16)] * 3
        + [shape((rows, width), f32)],
        scratch_shapes=[pltpu.VMEM((rows, width), f32)] * 2
        + [pltpu.VMEM((rows, width), bf16)] * 4
        + [pltpu.SemaphoreType.DMA((3,))]
        + [pltpu.VMEM((rows, width), bf16)] * 6
        + [pltpu.SemaphoreType.DMA((8,)), pltpu.SemaphoreType.DMA((8,))],
        compiler_params=pltpu.CompilerParams(
            collective_id=2, has_side_effects=True, vmem_limit_bytes=62 * 2**20
        ),
        cost_estimate=pl.CostEstimate(
            flops=32 * rows * width * hidden_count,
            bytes_accessed=80 * 2**20,
            transcendentals=0,
        ),
    )(grads, *saved, *weights)


def outer_kernel(extra, left_own, left_other, right_own, right_other, *refs):
    weights = refs[:extra]
    total_out, *spread = refs[extra : extra + (3 if extra else 1)]
    own, corner, send_x, send_y, got_corner, got_x, got_y, send, receive = refs[-9:]
    step = pl.program_id(0)
    half = own.shape[0] // 2
    low, high = slice(0, half), slice(half, 2 * half)
    copies = reduce_copies(corner, send_x, send_y, got_corner, got_x, got_y, send, receive)

    @pl.when(step == 0)
    def _():
        _, over_x, over_y = neighbours()
        greet((over_x, over_y))

    @pl.when(step < 8)
    def _():
        result = dot_first(left_own[...], right_own[...]) + dot_first(
            left_other[...], right_other[...]
        )
        order = (corner, corner, send_y, send_y, send_x, send_x, own, own)
        starts = (0, 1, 2, None, None, 4, None, None)
        for n, (target, first) in enumerate(zip(order, starts)):

            @pl.when(step == n)
            def _():
                target[high if n % 2 else low, :] = result.astype(target.dtype)
                if first is not None:
                    copies[first].start()

    for n, weight in enumerate(weights):

        @pl.when(step == 8 + n)
        def _():
            me = lax.axis_index("dp")
            x, y = (me // 2) % 2, me // 4
            k = min(n, 3)
            far_x = 1 - x if k % 2 else x
            far_y = 1 - y if k // 2 else y
            part = 512
            start = (2 * far_y + far_x) * part + (part // 2 if n == 4 else 0)
            cols = pl.ds(pl.multiple_of(start, 256), weight.shape[0])
            spread[0][:, cols] = dot_last(right_own[...], weight[...])
            spread[1][:, cols] = dot_last(right_other[...], weight[...]).astype(jnp.bfloat16)

    last = pl.num_programs(0) - 1

    @pl.when(step == min(9, 7 + extra))
    def _():
        copies[1].wait_recv()
        add_into(send_y, high, got_corner)
        copies[3].start()
        copies[0].wait_recv()
        add_into(send_x, low, got_corner)
        copies[5].start()

    @pl.when(step == last)
    def _():
        for n in (2, 4, 3, 5):
            copies[n].wait_recv()
        total_out[...] = (
            own[...] + got_x[...].astype(jnp.float32) + got_y[...].astype(jnp.float32)
        ).astype(total_out.dtype)
        for transfer in copies:
            transfer.wait_send()


def outer(lefts, rights, by_left, collective_id, weights=()):
    rows = 512
    wide = lefts[0][0].shape[1]
    right_wide = rights[0][0].shape[1]
    turn_of = lambda s: 6 - 2 * (jnp.minimum(s, 7) // 2) + jnp.minimum(s, 7) % 2
    if by_left:
        size = (wide // 8, right_wide)
        left_size = (rows, wide // 8)
        place_left = lambda row: lambda s: (row, turn_of(s))
        place_right = lambda row: lambda s: (row, 0)
    else:
        size = (wide // 2, right_wide // 4)
        left_size = (rows, wide // 2)
        place_left = lambda row: lambda s: (row, s % 2)
        place_right = lambda row: lambda s: (row, 3 - s // 2)
    both = (2 * size[0], size[1])
    spec, shape = pl.BlockSpec, jax.ShapeDtypeStruct
    out_specs = [spec(both, lambda s: (0, 0))]
    out_shape = [shape(both, jnp.bfloat16)]
    if weights:
        out_specs += [spec((rows, wide), lambda s: (0, 0))] * 2
        out_shape += [shape((rows, wide), jnp.float32), shape((rows, wide), jnp.bfloat16)]
    made = pl.pallas_call(
        functools.partial(outer_kernel, len(weights)),
        grid=(8 + len(weights),),
        in_specs=[spec(left_size, place_left(row)) for _, row in lefts]
        + [spec((rows, size[1]), place_right(row)) for _, row in rights]
        + [
            spec(weight.shape, lambda s: (0, 0), pipeline_mode=pl.Buffered(1))
            for weight in weights
        ],
        out_specs=out_specs,
        out_shape=out_shape,
        scratch_shapes=[pltpu.VMEM(both, jnp.float32)]
        + [pltpu.VMEM(both, jnp.bfloat16)] * 6
        + [pltpu.SemaphoreType.DMA((6,)), pltpu.SemaphoreType.DMA((6,))],
        compiler_params=pltpu.CompilerParams(
            collective_id=collective_id, has_side_effects=True, vmem_limit_bytes=60 * 2**20
        ),
        cost_estimate=pl.CostEstimate(
            flops=4 * rows * wide * right_wide, bytes_accessed=16 * 2**20, transcendentals=0
        ),
    )(*[array for array, _ in (*lefts, *rights)], *weights)
    return made if weights else made[0]


def columns_kernel(transposed, place, left, w0, w1, w2, w3_low, w3_high, own, other):
    rows = own.shape[0]

    def write(lines, result):
        for ref, kind in ((own, jnp.float32), (other, jnp.bfloat16)):
            start = 0 if ref is own else rows
            ref[...] = result(lines[start : start + rows]).astype(kind)

    for k, weight in enumerate((w0, w1, w2)):

        @pl.when(pl.program_id(0) == k)
        def _():
            step = dot_last if transposed else matmul
            write(left, lambda lines: step(lines, weight[...]))

    @pl.when(pl.program_id(0) == 3)
    def _():
        if transposed:
            write(
                left,
                lambda lines: jnp.concatenate(
                    [dot_last(lines, w3_low[...]), dot_last(lines, w3_high[...])], 1
                ),
            )
        else:
            middle = w3_low.shape[0]
            write(
                left,
                lambda lines: matmul(lines[:, :middle], w3_low[...])
                + matmul(lines[:, middle:], w3_high[...]),
            )


def columns(place, left, weights, transposed):
    length, depth = left.shape
    rows = length // 2
    part = weights[0].shape[0 if transposed else 1]
    width = 4 * part
    whole = lambda array: pl.BlockSpec(array.shape, lambda k, place: (0, 0))
    block = pl.BlockSpec((rows, part), lambda k, place: (0, k ^ place[0]))
    shape = jax.ShapeDtypeStruct
    return pl.pallas_call(
        functools.partial(columns_kernel, transposed),
        grid_spec=pltpu.PrefetchScalarGridSpec(
            num_scalar_prefetch=1,
            grid=(4,),
            in_specs=[whole(array) for array in (left, *weights)],
            out_specs=[block, block],
        ),
        out_shape=[shape((rows, width), jnp.float32), shape((rows, width), jnp.bfloat16)],
        compiler_params=pltpu.CompilerParams(vmem_limit_bytes=56 * 2**20),
        cost_estimate=pl.CostEstimate(
            flops=2 * length * depth * width, bytes_accessed=20 * 2**20, transcendentals=0
        ),
    )(place, left, *weights)


def tile_call(kernel, place, ins, outs, kept):
    width = 2048
    tile = 256

    def spec(cut, columns):
        if cut == "rows":
            return pl.BlockSpec((tile, columns), lambda t, place: (t, 0))
        if cut == "low" or cut == "high":
            return pl.BlockSpec((tile, columns), lambda t, place: (0, 0))
        return pl.BlockSpec((cut, columns), lambda t, place: (0, 0))

    return pl.pallas_call(
        kernel,
        grid_spec=pltpu.PrefetchScalarGridSpec(
            num_scalar_prefetch=1,
            grid=(2,),
            in_specs=[spec(cut, array.shape[1]) for array, cut in ins],
            out_specs=[spec(cut, shape.shape[1]) for shape, cut in outs],
        ),
        out_shape=[shape for shape, _ in outs],
        compiler_params=pltpu.CompilerParams(vmem_limit_bytes=56 * 2**20),
        cost_estimate=pl.CostEstimate(
            flops=20 * 2**20, bytes_accessed=kept * 2**20, transcendentals=0
        ),
    )(place, *[array for array, _ in ins])


def choose(low_ref, high_ref):
    return jnp.where(pl.program_id(0) == 0, low_ref[...], high_ref[...]).astype(jnp.float32)


def add_gain(gain_ref, values):
    @pl.when(pl.program_id(0) == 0)
    def _():
        gain_ref[...] = jnp.zeros_like(gain_ref)

    gain_ref[...] += jnp.sum(values.reshape(-1, 8, values.shape[1]), 0)


def relabelled(ref, values, place):
    width = values.shape[1] // 4
    for k in range(4):
        start = pl.multiple_of((place[0] ^ k) * width, width)
        ref[:, pl.ds(start, width)] = values[:, k * width : (k + 1) * width]


def first_norm_kernel(place, inputs, gain, normed):
    values, _ = norm_rows(inputs[...].astype(jnp.float32), gain[...])
    relabelled(normed, values.astype(jnp.bfloat16), place)


def middle_kernel(place, inputs, own, other, gain, middle, normed):
    values = inputs[...].astype(jnp.float32) + own[...] + other[...].astype(jnp.float32)
    middle[...] = values
    normed[...] = norm_rows(values, gain[...])[0].astype(jnp.bfloat16)


def middle_back_kernel(
    place, middle, cotangent, two, gain, middle_grad, branch, gain_grad
):
    two_grad = two[...]
    values = middle[...]
    _, factor = norm_rows(values, gain[...])
    add_gain(gain_grad, two_grad * values * factor)
    grads = cotangent[...].astype(jnp.float32) + norm_back(values, factor, gain[...], two_grad)
    middle_grad[...] = grads
    relabelled(branch, grads.astype(jnp.bfloat16), place)


def input_back_kernel(
    place, inputs, middle_grad, own, other, gain, input_grad, rounded, gain_grad
):
    one_grad = own[...] + other[...].astype(jnp.float32)
    values = inputs[...].astype(jnp.float32)
    _, factor = norm_rows(values, gain[...])
    add_gain(gain_grad, one_grad * values * factor)
    grads = middle_grad[...] + norm_back(values, factor, gain[...], one_grad)
    input_grad[...] = grads
    rounded[...] = grads.astype(jnp.bfloat16)


def output_kernel(place, middle, own, over_x, over_y, output):
    parts = [part[...].astype(jnp.float32) for part in (own, over_x, over_y)]
    output[...] = (middle[...] + parts[0] + parts[1] + parts[2]).astype(jnp.bfloat16)


def exchange(values, bit):
    return lax.ppermute(values, "dp", [(i, i ^ bit) for i in range(8)])


def swap_halves(values):
    pairs = []
    for i in range(8):
        for m in range(4):
            if (i & 1) != (m & 1):
                pairs.append((i * 4 + m, (i ^ 1) * 4 + (m ^ 1)))
    return lax.ppermute(values, ("dp", "mp"), pairs)


def after(values, earlier):
    return lax.optimization_barrier((values, earlier))[0]


def gather_near(block):
    return [exchange(block, 2), exchange(block, 4)]


def gather_far(near):
    half = near[0].shape[0] // 2
    return [exchange(near[0][:half], 4), exchange(near[1][half:], 2)]


def add_low(left, right):
    return (left.astype(jnp.float32) + right.astype(jnp.float32)).astype(jnp.bfloat16)


def pick(values, index, width, axis):
    return lax.dynamic_slice_in_dim(values, index * width, width, axis)


def in_order(own, other, core, axis=0):
    return jnp.where(
        core == 0,
        jnp.concatenate([own, other], axis),
        jnp.concatenate([other, own], axis),
    )


def total(values):
    for bit in (1, 2, 4):
        values = values + exchange(values, bit)
    for bit in (1, 2):
        values = values + lax.ppermute(values, "mp", [(i, i ^ bit) for i in range(4)])
    return values


def fast(
    layer_input,
    out_grad,
    norm_attn,
    query_norm,
    key_norm,
    w_query,
    key_matrix,
    value_matrix,
    w_output,
    norm_mlp,
    w_gate,
    w_up,
    w_down,
):
    bf16, f32 = jnp.bfloat16, jnp.float32
    device = lax.axis_index("dp")
    core = device & 1
    place = jnp.reshape(device >> 1, (1,)).astype(jnp.int32)
    core_index = jnp.reshape(core, (1,)).astype(jnp.int32)
    crossing = core != (lax.axis_index("mp") & 1)
    planes = 4
    rows = layer_input.shape[0]
    width = layer_input.shape[1]
    units = w_gate.shape[1] // planes
    array = jax.ShapeDtypeStruct

    query_cols = w_query.shape[1] // 2
    key_cols = key_matrix.shape[1] // 2

    def heads_of(which):
        return jnp.concatenate(
            [
                pick(w_query, which, query_cols, 1),
                pick(key_matrix, which, key_cols, 1),
                pick(value_matrix, which, key_cols, 1),
            ],
            1,
        )

    qkv_pair = in_order(heads_of(core), exchange(heads_of(1 - core), 1), core)
    out_rows = w_output.shape[0] // 2
    out_pair = in_order(
        pick(w_output, core, out_rows, 0),
        exchange(pick(w_output, 1 - core, out_rows, 0), 1),
        core,
        1,
    )
    qkv_z = lax.all_gather(qkv_pair, "mp", axis=1, tiled=True)
    pieces = jnp.concatenate(
        [w.reshape(planes, units, w.shape[1]) for w in (w_gate.T, w_up.T, w_down)], 1
    )

    def piece_for(k):
        return pick(pieces, place[0] ^ k, 1, 0)[0]

    feed_own = jnp.concatenate(
        [piece_for(0)] + [exchange(piece_for(k), 2 * k) for k in (1, 2, 3)], 1
    )

    qkv_z = after(qkv_z, feed_own)
    qkv_near = gather_near(qkv_z)
    moved = swap_halves(after(layer_input, qkv_z))
    moved_grad = swap_halves(after(out_grad, qkv_z))
    out_z = lax.all_gather(
        after(out_pair, (moved, moved_grad, qkv_near)), "mp", axis=0, tiled=True
    )

    qkv_chips = [qkv_z, *qkv_near, *gather_far(qkv_near)]
    inputs = jnp.where(crossing, moved, layer_input)
    cotangent = jnp.where(crossing, moved_grad, out_grad)

    out_near = gather_near(after(out_z, qkv_chips))
    feed_own = after(feed_own, (out_z, qkv_chips))
    gate_half, up_half, down_half = [
        lax.all_gather(feed_own[n * units : (n + 1) * units], "mp", axis=0, tiled=True)
        for n in range(3)
    ]

    gain_one, gain_two = norm_attn[None, :], norm_mlp[None, :]
    gain_query, gain_key = query_norm[None, :], key_norm[None, :]
    (normed,) = tile_call(
        first_norm_kernel,
        place,
        [(inputs, "rows"), (gain_one, 1)],
        [(array((rows, width), bf16), "rows")],
        4,
    )
    normed_other = after(exchange(normed, 1), (out_z, cotangent))
    cosines, sines = wide_tables(2 * rows)
    proj, query_rot, key_rot, value_low, attended, log_total = attend(
        core_index,
        normed,
        normed_other,
        qkv_chips,
        cosines,
        sines,
        gain_query,
        gain_key,
        planes,
        query_cols,
    )
    out_near = after(out_near, attended)
    out_chips = [out_z, *out_near, *gather_far(out_near)]
    grads_near = gather_near(after(cotangent, qkv_chips))
    branch_own, branch_other = columns(place, attended, out_chips, False)
    middle, tokens = tile_call(
        middle_kernel,
        place,
        [(inputs, "rows"), (branch_own, "rows"), (after(exchange(branch_other, 1), grads_near), "rows"), (gain_two, 1)],
        [
            (array((rows, width), f32), "rows"),
            (array((rows, width), bf16), "rows"),
        ],
        14,
    )

    gate_half = after(gate_half, attended)
    up_half = after(up_half, tokens)
    gate_w, up_w = [[half, exchange(half, 1)] for half in (gate_half, up_half)]
    tokens_near = gather_near(tokens)
    all_tokens, all_grads, all_hidden, gate_slope, up_slope = gather_hidden(
        [tokens, *tokens_near], [cotangent, *grads_near], [*gate_w, *up_w]
    )
    down_half = after(down_half, tokens_near)
    down_w = [down_half, exchange(down_half, 1)]

    def over_z(grad):
        return lax.psum_scatter(grad, "mp", scatter_dimension=0, tiled=True)

    def weight_grad(left, right):
        half = right.shape[1] // 2
        other = exchange(dot_first(left, right[:, half:]).astype(bf16), 1)
        return (dot_first(left, right[:, :half]) + other.astype(f32)).astype(bf16)

    down_local = weight_grad(all_hidden, all_grads)
    down_sum = over_z(down_local)
    all_gate, all_up, out_own, out_x, out_y, two_grad = feed_back(
        after(all_grads, down_local),
        [all_hidden, gate_slope, up_slope],
        [*gate_w, *up_w, *down_w],
    )
    half = width // 2
    gate_other = dot_first(all_gate, all_tokens[:, half:]).astype(bf16)
    up_other = dot_first(all_up, all_tokens[:, half:]).astype(bf16)
    all_gate, all_up = after((all_gate, all_up), (gate_other, up_other))

    def own_half(left, other):
        own = dot_first(left, all_tokens[:, :half])
        return (own + exchange(other, 1).astype(f32)).astype(bf16)

    gate_local = own_half(all_gate, gate_other)
    up_local = own_half(all_up, up_other)
    gate_sum, up_sum = over_z(gate_local), over_z(up_local)
    middle_grad, branch, gain_two_part = tile_call(
        middle_back_kernel,
        place,
        [(middle, "rows"), (cotangent, "rows"), (two_grad, "rows"), (gain_two, 1)],
        [
            (array((rows, width), f32), "rows"),
            (array((rows, width), bf16), "rows"),
            (array((8, width), f32), 8),
        ],
        18,
    )

    def unspread(own):
        cols = own.shape[1] // planes
        got = [own[:, :cols]] + [
            exchange(own[:, k * cols : (k + 1) * cols], 2 * k) for k in (1, 2, 3)
        ]
        return jnp.concatenate(got, 1), cols

    def chips_in_order(got, cols, rows):
        return jnp.concatenate([pick(got[rows], place[0] ^ k, cols, 1) for k in range(planes)], 0)

    gate_up_got, cols = unspread(jnp.concatenate([gate_sum, up_sum], 0))
    gate_own = chips_in_order(gate_up_got, cols, slice(0, units)).T.astype(f32)
    up_own = chips_in_order(gate_up_got, cols, slice(units, 2 * units)).T.astype(f32)
    down_got, cols = unspread(down_sum)
    down_own = chips_in_order(down_got, cols, slice(0, units)).astype(f32)

    branch_pair = after(exchange(branch, 1), (gate_local, up_local))
    out_parts = [out_own, exchange(after(out_x, branch_pair), 2), exchange(after(out_y, branch_pair), 4)]
    proj_grad, head_gains = attend_back(
        core_index,
        branch,
        branch_pair,
        out_chips,
        cosines,
        sines,
        gain_query,
        gain_key,
        (proj, query_rot, key_rot, value_low, log_total),
        planes,
        query_cols,
    )

    out_parts = after(out_parts, proj_grad)
    (layer_output,) = tile_call(
        output_kernel,
        place,
        [(middle, "rows")] + [(part, "rows") for part in out_parts],
        [(array((rows, width), bf16), "rows")],
        12,
    )
    proj_grad = after(proj_grad, (layer_output, down_own))
    qkv_local, one_own, one_other = outer(
        [(normed, 0), (normed_other, 0)], [(proj_grad, 0), (proj_grad, 1)], True, 3, qkv_chips
    )
    qkv_sum = lax.psum_scatter(qkv_local, "mp", scatter_dimension=1, tiled=True)
    output_moved = swap_halves(layer_output)
    attended = after(attended, (qkv_local, output_moved, gate_sum, up_sum))
    out_local = outer([(attended, 0), (attended, 1)], [(branch, 0), (branch_pair, 0)], False, 4)
    out_sum = over_z(after(out_local, qkv_sum))
    input_grad, rounded_grad, gain_one_part = tile_call(
        input_back_kernel,
        place,
        [
            (inputs, "rows"),
            (middle_grad, "rows"),
            (one_own, "rows"),
            (exchange(one_other, 1), "rows"),
            (gain_one, 1),
        ],
        [
            (array((rows, width), f32), "rows"),
            (array((rows, width), bf16), "rows"),
            (array((8, width), f32), 8),
        ],
        18,
    )
    gain_sums = total(
        after(jnp.concatenate(
            [
                jnp.sum(gain_one_part, 0),
                jnp.sum(head_gains[:8], 0),
                jnp.sum(head_gains[8:], 0),
                jnp.sum(gain_two_part, 0),
            ]
        ), out_local)
    )
    pair_rows = qkv_sum.shape[0] // 2
    qkv_other = exchange(pick(qkv_sum, 1 - core, pair_rows, 0), 1)
    qkv_own = pick(qkv_sum, core, pair_rows, 0)

    def both(start, stop):
        return in_order(qkv_own[:, start:stop], qkv_other[:, start:stop], core, 1).astype(f32)

    pair_cols = out_sum.shape[1] // 2
    out_other = exchange(pick(out_sum, 1 - core, pair_cols, 1), 1)
    out_own = pick(out_sum, core, pair_cols, 1)
    return (
        jnp.where(crossing, output_moved, layer_output),
        jnp.where(crossing, swap_halves(rounded_grad).astype(f32), input_grad),
        gain_sums[:width],
        gain_sums[width : width + HEAD_SIZE],
        gain_sums[width + HEAD_SIZE : width + 2 * HEAD_SIZE],
        both(0, query_cols),
        both(query_cols, query_cols + key_cols),
        both(query_cols + key_cols, query_cols + 2 * key_cols),
        in_order(out_own, out_other, core, 0).astype(f32),
        gain_sums[width + 2 * HEAD_SIZE :],
        gate_own,
        up_own,
        down_own,
    )


def solution(mesh):
    in_specs = (
        P(("dp", "mp"), None),
        P(("dp", "mp"), None),
        P(),
        P(),
        P(),
        P("dp", "mp"),
        P("dp", "mp"),
        P("dp", "mp"),
        P("mp", "dp"),
        P(),
        P("dp", "mp"),
        P("dp", "mp"),
        P("mp", "dp"),
    )
    out_specs = (
        P(("dp", "mp"), None),
        P(("dp", "mp"), None),
        P(),
        P(),
        P(),
        P("dp", "mp"),
        P("dp", "mp"),
        P("dp", "mp"),
        P("mp", "dp"),
        P(),
        P("dp", "mp"),
        P("dp", "mp"),
        P("mp", "dp"),
    )
    whole_sequences = dict(mesh.shape) == {"dp": 8, "mp": 4}
    local = fast if whole_sequences else generic
    return jax.shard_map(local, mesh=mesh, in_specs=in_specs, out_specs=out_specs, check_vma=False)
```

```python
import functools

import jax
import jax.numpy as jnp
from jax import lax
from jax.experimental import pallas as pl
from jax.experimental.pallas import tpu as pltpu
from jax.sharding import PartitionSpec as P

HEAD_SIZE = 128
SEQUENCE_LENGTH = 1024


EPSILON = 1e-06
THETA = 1000000.0


def norm_rows(values, gain):
    factor = lax.rsqrt(jnp.mean(values * values, -1, keepdims=True) + EPSILON)
    return (values * factor * gain, factor)


def norm_back(values, factor, gain, upstream):
    scaled = upstream * gain
    inner = jnp.mean(scaled * values, -1, keepdims=True)
    return factor * scaled - values * (factor * factor * factor) * inner


def tables(length, width):
    half_width = width // 2
    frequencies = THETA ** (-(jnp.arange(half_width, dtype=jnp.float32) * 2.0 / width))
    angles = jnp.arange(length, dtype=jnp.float32)[:, None] * frequencies[None, :]
    return (jnp.cos(angles), jnp.sin(angles))


def rotate(values, cosine_table, sine_table):
    half_width = values.shape[-1] // 2
    first_half = values[..., :half_width]
    second_half = values[..., half_width:]
    cosine_part = cosine_table[:, None, :]
    sine_part = sine_table[:, None, :]
    return jnp.concatenate(
        [
            first_half * cosine_part - second_half * sine_part,
            second_half * cosine_part + first_half * sine_part,
        ],
        -1,
    )


def rotate_back(grads, cosine_table, sine_table):
    half_width = grads.shape[-1] // 2
    first_half = grads[..., :half_width]
    second_half = grads[..., half_width:]
    cosine_part = cosine_table[:, None, :]
    sine_part = sine_table[:, None, :]
    return jnp.concatenate(
        [
            first_half * cosine_part + second_half * sine_part,
            second_half * cosine_part - first_half * sine_part,
        ],
        -1,
    )


def matmul(left, right):
    return jnp.dot(left, right, preferred_element_type=jnp.float32)


def dot_last(left, right):
    return lax.dot_general(
        left, right, (((1,), (1,)), ((), ())), preferred_element_type=jnp.float32
    )


def dot_first(left, right):
    return lax.dot_general(
        left, right, (((0,), (0,)), ((), ())), preferred_element_type=jnp.float32
    )


def masked_scores(query_block, keys, start, block_rows, scale):
    raw = (
        jnp.einsum("qhgd,khd->hgqk", query_block, keys, preferred_element_type=jnp.float32) * scale
    )
    query_places = start + jnp.arange(block_rows)[:, None]
    key_places = jnp.arange(keys.shape[0])[None, :]
    return jnp.where(key_places <= query_places, raw, -jnp.inf)


def generic(
    layer_input,
    out_grad,
    norm_attn,
    query_norm,
    key_norm,
    w_query,
    key_matrix,
    value_matrix,
    w_output,
    norm_mlp,
    w_gate,
    w_up,
    w_down,
):
    inputs = layer_input.astype(jnp.float32)
    query_full, key_full, value_full, output_full = (
        lax.all_gather(w_query, "dp", axis=0, tiled=True),
        lax.all_gather(key_matrix, "dp", axis=0, tiled=True),
        lax.all_gather(value_matrix, "dp", axis=0, tiled=True),
        lax.all_gather(w_output, "dp", axis=1, tiled=True),
    )
    first_normed, factor_one = norm_rows(inputs, norm_attn)
    normed_all = lax.all_gather(first_normed.astype(jnp.bfloat16), "mp", axis=0, tiled=True)
    total_rows = normed_all.shape[0]
    sequence_batch = total_rows // SEQUENCE_LENGTH
    query_heads = query_full.shape[1] // HEAD_SIZE
    shared_heads = key_full.shape[1] // HEAD_SIZE
    heads_per_group = query_heads // shared_heads
    query_proj = matmul(normed_all, query_full).reshape(
        sequence_batch, SEQUENCE_LENGTH, query_heads, HEAD_SIZE
    )
    key_projected = matmul(normed_all, key_full).reshape(
        sequence_batch, SEQUENCE_LENGTH, shared_heads, HEAD_SIZE
    )
    value_low = (
        matmul(normed_all, value_full)
        .astype(jnp.bfloat16)
        .reshape(sequence_batch, SEQUENCE_LENGTH, shared_heads, HEAD_SIZE)
    )
    cosine_table, sine_table = tables(SEQUENCE_LENGTH, HEAD_SIZE)
    query_normed, query_factor = norm_rows(query_proj, query_norm)
    query_rotated = rotate(query_normed, cosine_table, sine_table).astype(jnp.bfloat16)
    query_rotated = query_rotated.reshape(
        sequence_batch, SEQUENCE_LENGTH, shared_heads, heads_per_group, HEAD_SIZE
    )
    key_normed, key_factor = norm_rows(key_projected, key_norm)
    key_rot = rotate(key_normed, cosine_table, sine_table).astype(jnp.bfloat16)
    block_rows = min(512, SEQUENCE_LENGTH)
    block_count = SEQUENCE_LENGTH // block_rows
    scale = HEAD_SIZE ** (-0.5)
    attended_pieces = []
    log_totals = []
    for seq_index in range(sequence_batch):
        for block_index in range(block_count):
            start = block_index * block_rows
            query_block = query_rotated[seq_index, start : start + block_rows]
            scores = masked_scores(query_block, key_rot[seq_index], start, block_rows, scale)
            largest = jnp.max(scores, -1, keepdims=True)
            expanded = jnp.exp(scores - largest)
            summed = jnp.sum(expanded, -1, keepdims=True)
            probs_low = (expanded / summed).astype(jnp.bfloat16)
            block_out = jnp.einsum(
                "hgqk,khd->qhgd",
                probs_low,
                value_low[seq_index],
                preferred_element_type=jnp.float32,
            )
            attended_pieces.append(block_out.reshape(block_rows, query_heads * HEAD_SIZE))
            log_totals.append(largest + jnp.log(summed))
    attended = jnp.concatenate(attended_pieces, 0).astype(jnp.bfloat16)
    attn_sum = lax.psum_scatter(
        matmul(attended, output_full), "mp", scatter_dimension=0, tiled=True
    )
    middle = inputs + attn_sum
    gate_full, up_full, down_full = (
        lax.all_gather(w_gate, "dp", axis=0, tiled=True),
        lax.all_gather(w_up, "dp", axis=0, tiled=True),
        lax.all_gather(w_down, "dp", axis=1, tiled=True),
    )
    normed_two, factor_two = norm_rows(middle, norm_mlp)
    normed_two_all = lax.all_gather(normed_two.astype(jnp.bfloat16), "mp", axis=0, tiled=True)
    gate_value = matmul(normed_two_all, gate_full)
    up_value = matmul(normed_two_all, up_full)
    hidden_low = (jax.nn.silu(gate_value) * up_value).astype(jnp.bfloat16)
    mlp_sum = lax.psum_scatter(
        matmul(hidden_low, down_full).astype(jnp.bfloat16), "mp", scatter_dimension=0, tiled=True
    ).astype(jnp.float32)
    layer_output = (middle + mlp_sum).astype(jnp.bfloat16)
    grad_rows = lax.all_gather(out_grad, "mp", axis=0, tiled=True)
    gate_back, up_back, down_back = (
        lax.all_gather(w_gate, "dp", axis=0, tiled=True),
        lax.all_gather(w_up, "dp", axis=0, tiled=True),
        lax.all_gather(w_down, "dp", axis=1, tiled=True),
    )
    hidden_grad = dot_last(grad_rows, down_back)
    down_grad = dot_first(hidden_low, grad_rows)
    sigmoid_gate = jax.nn.sigmoid(gate_value)
    gate_grad = (
        hidden_grad * up_value * sigmoid_gate * (1.0 + gate_value * (1.0 - sigmoid_gate))
    ).astype(jnp.bfloat16)
    up_grad = (hidden_grad * gate_value * sigmoid_gate).astype(jnp.bfloat16)
    gate_weight_grad = dot_first(normed_two_all, gate_grad)
    up_weight_grad = dot_first(normed_two_all, up_grad)
    two_grad = lax.psum_scatter(
        dot_last(gate_grad, gate_back) + dot_last(up_grad, up_back),
        "mp",
        scatter_dimension=0,
        tiled=True,
    )
    gain_two_grad = jnp.sum(two_grad * middle * factor_two, 0)
    middle_grad = out_grad.astype(jnp.float32) + norm_back(middle, factor_two, norm_mlp, two_grad)
    mlp_grads = (
        lax.psum_scatter(
            gate_weight_grad.astype(jnp.bfloat16), "dp", scatter_dimension=0, tiled=True
        ).astype(jnp.float32),
        lax.psum_scatter(
            up_weight_grad.astype(jnp.bfloat16), "dp", scatter_dimension=0, tiled=True
        ).astype(jnp.float32),
        lax.psum_scatter(
            down_grad.astype(jnp.bfloat16), "dp", scatter_dimension=1, tiled=True
        ).astype(jnp.float32),
    )
    branch_all = lax.all_gather(middle_grad.astype(jnp.bfloat16), "mp", axis=0, tiled=True)
    output_weight_grad = dot_first(attended, branch_all)
    attended_grad = dot_last(branch_all, output_full).astype(jnp.bfloat16)
    attended_grad = attended_grad.reshape(
        sequence_batch, SEQUENCE_LENGTH, shared_heads, heads_per_group, HEAD_SIZE
    )
    query_grad_seqs = []
    key_grad_seqs = []
    value_grad_seqs = []
    for seq_index in range(sequence_batch):
        key_running = jnp.zeros((SEQUENCE_LENGTH, shared_heads, HEAD_SIZE), jnp.float32)
        value_running = jnp.zeros((SEQUENCE_LENGTH, shared_heads, HEAD_SIZE), jnp.float32)
        query_blocks = []
        for block_index in range(block_count):
            start = block_index * block_rows
            query_block = query_rotated[seq_index, start : start + block_rows]
            scores = masked_scores(query_block, key_rot[seq_index], start, block_rows, scale)
            probs_full = jnp.exp(scores - log_totals[seq_index * block_count + block_index])
            probs_low = probs_full.astype(jnp.bfloat16)
            grad_block = attended_grad[seq_index, start : start + block_rows]
            prob_grad = jnp.einsum(
                "qhgd,khd->hgqk",
                grad_block,
                value_low[seq_index],
                preferred_element_type=jnp.float32,
            )
            row_inner = jnp.sum(probs_full * prob_grad, -1, keepdims=True)
            score_grad = (probs_full * (prob_grad - row_inner)).astype(jnp.bfloat16)
            query_blocks.append(
                jnp.einsum(
                    "hgqk,khd->qhgd",
                    score_grad,
                    key_rot[seq_index],
                    preferred_element_type=jnp.float32,
                )
                * scale
            )
            key_running = (
                key_running
                + jnp.einsum(
                    "hgqk,qhgd->khd", score_grad, query_block, preferred_element_type=jnp.float32
                )
                * scale
            )
            value_running = value_running + jnp.einsum(
                "hgqk,qhgd->khd", probs_low, grad_block, preferred_element_type=jnp.float32
            )
        query_grad_seqs.append(jnp.concatenate(query_blocks, 0))
        key_grad_seqs.append(key_running)
        value_grad_seqs.append(value_running)
    rot_query_grad = jnp.stack(query_grad_seqs, 0).reshape(
        sequence_batch, SEQUENCE_LENGTH, query_heads, HEAD_SIZE
    )
    rot_key_grad = jnp.stack(key_grad_seqs, 0)
    value_grad = (
        jnp.stack(value_grad_seqs, 0)
        .reshape(total_rows, shared_heads * HEAD_SIZE)
        .astype(jnp.bfloat16)
    )
    query_normed_grad = rotate_back(rot_query_grad, cosine_table, sine_table)
    query_gain_grad = jnp.sum(query_normed_grad * query_proj * query_factor, (0, 1, 2))
    query_grad = norm_back(query_proj, query_factor, query_norm, query_normed_grad)
    query_grad = query_grad.reshape(total_rows, query_heads * HEAD_SIZE).astype(jnp.bfloat16)
    key_normed_grad = rotate_back(rot_key_grad, cosine_table, sine_table)
    key_gain_grad = jnp.sum(key_normed_grad * key_projected * key_factor, (0, 1, 2))
    key_grad = norm_back(key_projected, key_factor, key_norm, key_normed_grad)
    key_grad = key_grad.reshape(total_rows, shared_heads * HEAD_SIZE).astype(jnp.bfloat16)
    query_weight_grad = dot_first(normed_all, query_grad)
    key_weight_grad = dot_first(normed_all, key_grad)
    value_weight_grad = dot_first(normed_all, value_grad)
    one_partial = (
        dot_last(query_grad, query_full)
        + dot_last(key_grad, key_full)
        + dot_last(value_grad, value_full)
    )
    one_grad = lax.psum_scatter(
        one_partial.astype(jnp.bfloat16), "mp", scatter_dimension=0, tiled=True
    ).astype(jnp.float32)
    gain_one_grad = jnp.sum(one_grad * inputs * factor_one, 0)
    input_grad = middle_grad + norm_back(inputs, factor_one, norm_attn, one_grad)
    attn_grads = (
        lax.psum_scatter(
            query_weight_grad.astype(jnp.bfloat16), "dp", scatter_dimension=0, tiled=True
        ).astype(jnp.float32),
        lax.psum_scatter(
            key_weight_grad.astype(jnp.bfloat16), "dp", scatter_dimension=0, tiled=True
        ).astype(jnp.float32),
        lax.psum_scatter(
            value_weight_grad.astype(jnp.bfloat16), "dp", scatter_dimension=0, tiled=True
        ).astype(jnp.float32),
        lax.psum_scatter(
            output_weight_grad.astype(jnp.bfloat16), "dp", scatter_dimension=1, tiled=True
        ).astype(jnp.float32),
    )
    gain_sums = lax.psum(
        (gain_one_grad, query_gain_grad, key_gain_grad, gain_two_grad), ("dp", "mp")
    )
    return (
        layer_output,
        input_grad,
        gain_sums[0],
        gain_sums[1],
        gain_sums[2],
        attn_grads[0],
        attn_grads[1],
        attn_grads[2],
        attn_grads[3],
        gain_sums[3],
        mlp_grads[0],
        mlp_grads[1],
        mlp_grads[2],
    )


ROW_BLOCK = 256


def wide_tables(length):
    cosine_table, sine_table = tables(length, HEAD_SIZE)
    return (
        jnp.concatenate([cosine_table, cosine_table], 1),
        jnp.concatenate([-sine_table, sine_table], 1),
    )


def turn(values, cosines, sines):
    return values * cosines + pltpu.roll(values, HEAD_SIZE // 2, 1) * sines


def turn_back(values, cosines, sines):
    return values * cosines - pltpu.roll(values, HEAD_SIZE // 2, 1) * sines


def causal(rows):
    query_places = lax.broadcasted_iota(jnp.int32, (rows, rows), 0)
    key_places = lax.broadcasted_iota(jnp.int32, (rows, rows), 1)
    return key_places <= query_places


def attend_kernel(
    core, own, other, w0, w1, w2, w3_low, w3_high, cosines, sines, query_gain, key_gain,
    proj, query_rot, key_rot, value, attended, log_total,
):
    half = own.shape[0]
    length = 2 * half
    scale = HEAD_SIZE ** (-0.5)
    query_cols = query_rot.shape[1]
    heads = query_cols // HEAD_SIZE
    for h in range(2):
        here = core[0] == h
        rows = slice(h * half, (h + 1) * half)
        block = None
        start = 0
        for weight in (w0, w1, w2, w3_low, w3_high):
            cols = slice(start, start + weight.shape[0])
            start = cols.stop
            tokens = jnp.where(here, own[:, cols], other[:, cols])
            term = matmul(tokens, weight[...])
            block = term if block is None else block + term
        proj[rows, :] = block
        cos_rows, sin_rows = cosines[rows, :], sines[rows, :]
        for head in range(heads):
            cols = slice(head * HEAD_SIZE, (head + 1) * HEAD_SIZE)
            normed, _ = norm_rows(block[:, cols], query_gain[...])
            query_rot[rows, cols] = turn(normed, cos_rows, sin_rows).astype(jnp.bfloat16)
        cols = slice(query_cols, query_cols + HEAD_SIZE)
        normed, _ = norm_rows(block[:, cols], key_gain[...])
        key_rot[rows, :] = turn(normed, cos_rows, sin_rows).astype(jnp.bfloat16)
        value[rows, :] = block[:, query_cols + HEAD_SIZE :].astype(jnp.bfloat16)
    allowed = causal(ROW_BLOCK)

    def place(start):
        return pl.ds(pl.multiple_of((start + core[0] * half) % length, ROW_BLOCK), ROW_BLOCK)

    lane = lax.broadcasted_iota(jnp.int32, (ROW_BLOCK, HEAD_SIZE), 1)
    for start in range(0, length, ROW_BLOCK):
        rows = slice(start, start + ROW_BLOCK)
        logs = jnp.zeros((ROW_BLOCK, HEAD_SIZE), jnp.float32)
        for head in range(heads):
            cols = slice(head * HEAD_SIZE, (head + 1) * HEAD_SIZE)
            query = query_rot[rows, cols]
            scores = [jnp.where(allowed, dot_last(query, key_rot[rows, :]) * scale, -jnp.inf)]
            if start:
                scores.append(dot_last(query, key_rot[:start, :]) * scale)
            largest = functools.reduce(
                jnp.maximum, [jnp.max(s, -1, keepdims=True) for s in scores]
            )
            expanded = [jnp.exp(s - largest) for s in scores]
            summed = sum(jnp.sum(e, -1, keepdims=True) for e in expanded)
            out = matmul(expanded[0].astype(jnp.bfloat16), value[rows, :])
            if start:
                out = out + matmul(expanded[1].astype(jnp.bfloat16), value[:start, :])
            attended[place(start), cols] = (out / summed).astype(jnp.bfloat16)
            logs = jnp.where(lane == head, largest + jnp.log(summed), logs)
        log_total[rows, :] = logs


def attend(core, own, other, weights, cosines, sines, query_gain, key_gain, planes, query_cols):
    half, width = own.shape
    length = 2 * half
    cols = weights[0].shape[1]
    group = cols // planes
    whole = lambda shape: pl.BlockSpec(shape, lambda g, core: (0, 0))
    column = lambda rows, width: pl.BlockSpec((rows, width), lambda g, core: (0, g))
    shape = jax.ShapeDtypeStruct
    return pl.pallas_call(
        attend_kernel,
        grid_spec=pltpu.PrefetchScalarGridSpec(
            num_scalar_prefetch=1,
            grid=(planes,),
            in_specs=[whole((half, width))] * 2
            + [column(weight.shape[0], group) for weight in weights]
            + [whole((length, HEAD_SIZE))] * 2
            + [whole((1, HEAD_SIZE))] * 2,
            out_specs=[
                column(length, group),
                column(length, query_cols),
                column(length, HEAD_SIZE),
                column(length, HEAD_SIZE),
                column(length, query_cols),
                column(length, HEAD_SIZE),
            ],
        ),
        out_shape=[
            shape((length, cols), jnp.float32),
            shape((length, planes * query_cols), jnp.bfloat16),
            shape((length, planes * HEAD_SIZE), jnp.bfloat16),
            shape((length, planes * HEAD_SIZE), jnp.bfloat16),
            shape((length, planes * query_cols), jnp.bfloat16),
            shape((length, planes * HEAD_SIZE), jnp.float32),
        ],
        compiler_params=pltpu.CompilerParams(vmem_limit_bytes=56 * 2**20),
        cost_estimate=pl.CostEstimate(flops=1, bytes_accessed=1, transcendentals=0),
    )(core, own, other, *weights, cosines, sines, query_gain, key_gain)


def attend_back_kernel(
    core, own, other, o0, o1, o2, o3_low, o3_high, cosines, sines, query_gain, key_gain,
    proj, query_rot, key_rot, value, log_total,
    proj_grad, gain_grads, grad, key_total, value_total,
):
    half = own.shape[0]
    length = 2 * half
    part = o0.shape[1]
    scale = HEAD_SIZE ** (-0.5)
    query_cols = query_rot.shape[1]
    heads = query_cols // HEAD_SIZE

    @pl.when(pl.program_id(0) == 0)
    def _():
        gain_grads[...] = jnp.zeros_like(gain_grads)

    low = pl.program_id(0) < pl.num_programs(0) // 2
    corner = jnp.where(low, o3_low[...], o3_high[...])
    for h in range(2):
        here = core[0] == h
        block = None
        for k, weight in enumerate((o0[...], o1[...], o2[...], corner)):
            cols = slice(k * part, (k + 1) * part)
            tokens = jnp.where(here, own[:, cols], other[:, cols])
            term = dot_last(tokens, weight)
            block = term if block is None else block + term
        grad[h * half : (h + 1) * half, :] = block.astype(jnp.bfloat16)
    key_total[...] = jnp.zeros_like(key_total)
    value_total[...] = jnp.zeros_like(value_total)
    allowed = causal(ROW_BLOCK)

    def fold(values):
        return jnp.sum(values.reshape(-1, 8, HEAD_SIZE), 0)

    def place(start):
        return pl.ds(pl.multiple_of((start + core[0] * half) % length, ROW_BLOCK), ROW_BLOCK)

    for start in range(0, length, ROW_BLOCK):
        rows = slice(start, start + ROW_BLOCK)
        for head in range(heads):
            cols = slice(head * HEAD_SIZE, (head + 1) * HEAD_SIZE)
            query = query_rot[rows, cols]
            upstream = grad[rows, cols]
            logs = log_total[rows, head : head + 1]
            spans = [rows] + ([slice(0, start)] if start else [])
            probs, prob_grads = [], []
            for n, span in enumerate(spans):
                raw = dot_last(query, key_rot[span, :]) * scale
                if n == 0:
                    raw = jnp.where(allowed, raw, -jnp.inf)
                probs.append(jnp.exp(raw - logs))
                prob_grads.append(dot_last(upstream, value[span, :]))
            inner = sum(jnp.sum(p * d, -1, keepdims=True) for p, d in zip(probs, prob_grads))
            query_back = None
            for span, p, d in zip(spans, probs, prob_grads):
                score_grad = (p * (d - inner)).astype(jnp.bfloat16)
                term = matmul(score_grad, key_rot[span, :])
                query_back = term if query_back is None else query_back + term
                key_total[span, :] += dot_first(score_grad, query)
                value_total[span, :] += dot_first(p.astype(jnp.bfloat16), upstream)
            normed_grad = turn_back(query_back * scale, cosines[rows, :], sines[rows, :])
            values = proj[rows, cols]
            _, factor = norm_rows(values, query_gain[...])
            gain_grads[:8, :] += fold(normed_grad * values * factor)
            back = norm_back(values, factor, query_gain[...], normed_grad)
            proj_grad[place(start), cols] = back.astype(jnp.bfloat16)
    for start in range(0, length, ROW_BLOCK):
        rows = slice(start, start + ROW_BLOCK)
        cols = slice(query_cols, query_cols + HEAD_SIZE)
        normed_grad = turn_back(key_total[rows, :] * scale, cosines[rows, :], sines[rows, :])
        values = proj[rows, cols]
        _, factor = norm_rows(values, key_gain[...])
        gain_grads[8:, :] += fold(normed_grad * values * factor)
        back = norm_back(values, factor, key_gain[...], normed_grad)
        proj_grad[place(start), cols] = back.astype(jnp.bfloat16)
        proj_grad[place(start), query_cols + HEAD_SIZE :] = value_total[rows, :].astype(
            jnp.bfloat16
        )


def attend_back(
    core, own, other, weights, cosines, sines, query_gain, key_gain, saved, planes, query_cols
):
    half, width = own.shape
    length = 2 * half
    part = weights[0].shape[1]
    proj, query_rot, key_rot, value, log_total = saved
    cols = proj.shape[1]
    group = cols // planes
    whole = lambda shape: pl.BlockSpec(shape, lambda g, core: (0, 0))
    column = lambda rows, width: pl.BlockSpec((rows, width), lambda g, core: (0, g))
    shape = jax.ShapeDtypeStruct
    return pl.pallas_call(
        attend_back_kernel,
        grid_spec=pltpu.PrefetchScalarGridSpec(
            num_scalar_prefetch=1,
            grid=(planes,),
            in_specs=[whole((half, width))] * 2
            + [pl.BlockSpec((query_cols, part), lambda g, core: (g, 0))] * 3
            + [
                pl.BlockSpec((query_cols, part), lambda g, core: (jnp.minimum(g, 1), 0)),
                pl.BlockSpec((query_cols, part), lambda g, core: (jnp.maximum(g - 2, 0), 0)),
            ]
            + [whole((length, HEAD_SIZE))] * 2
            + [whole((1, HEAD_SIZE))] * 2
            + [
                column(length, group),
                column(length, query_cols),
                column(length, HEAD_SIZE),
                column(length, HEAD_SIZE),
                column(length, HEAD_SIZE),
            ],
            out_specs=[column(length, group), whole((16, HEAD_SIZE))],
            scratch_shapes=[
                pltpu.VMEM((length, query_cols), jnp.bfloat16),
                pltpu.VMEM((length, HEAD_SIZE), jnp.float32),
                pltpu.VMEM((length, HEAD_SIZE), jnp.float32),
            ],
        ),
        out_shape=[
            shape((length, cols), jnp.bfloat16),
            shape((16, HEAD_SIZE), jnp.float32),
        ],
        compiler_params=pltpu.CompilerParams(vmem_limit_bytes=56 * 2**20),
        cost_estimate=pl.CostEstimate(flops=1, bytes_accessed=1, transcendentals=0),
    )(core, own, other, *weights, cosines, sines, query_gain, key_gain, *saved)


MESH = pl.DeviceIdType.MESH


def neighbours():
    me = lax.axis_index("dp")
    x, y = (me // 2) % 2, me // 4
    return me, me + 2 - 4 * x, me + 4 - 8 * y


def greet(others):
    barrier = pltpu.get_barrier_semaphore()
    for other in others:
        pl.semaphore_signal(barrier, inc=1, device_id={"dp": other}, device_id_type=MESH)
    pl.semaphore_wait(barrier, len(others))


def column_places(width):
    me = lax.axis_index("dp")
    core, x, y = me % 2, (me // 2) % 2, me // 4
    block = 256
    places = []
    for n in range(width // block):
        here = core if n < 4 else 1 - core
        far_x = 1 - x if n % 2 else x
        far_y = 1 - y if (n // 2) % 2 else y
        start = (4 * far_y + 2 * far_x + here) * block
        places.append(pl.ds(pl.multiple_of(start, block), block))
    return places


def split_columns(target, values):
    for n, cols in enumerate(column_places(values.shape[1])):
        target[:, n * 256 : (n + 1) * 256] = values[:, cols]


def merge_columns(target, sums):
    for n, cols in enumerate(column_places(sums.shape[1])):
        target[:, cols] = sums[:, n * 256 : (n + 1) * 256].astype(target.dtype)


def both_halves(left, own, other):
    half = own.shape[1]
    return dot_last(left[:, :half], own[...]) + dot_last(left[:, half:], other[...])


def hidden_kernel(
    x_tokens_out, y_tokens_out, x_grads_out, y_grads_out,
    own_tokens, x_tokens, y_tokens, own_grads, x_grads, y_grads,
    gate_own, gate_other, up_own, up_other,
    all_tokens, all_grads, hidden, gate_slope, up_slope,
    far_tokens, far_grads, send, receive,
):
    block, chunk = pl.program_id(0), pl.program_id(1)
    _, over_x, over_y = neighbours()
    half = far_tokens.shape[0] // 2
    low, high = pl.ds(0, half), pl.ds(half, half)
    copies = [
        pltpu.make_async_remote_copy(
            src_ref=source.at[rows],
            dst_ref=target.at[rows],
            send_sem=send.at[n],
            recv_sem=receive.at[n],
            device_id={"dp": other},
            device_id_type=MESH,
        )
        for n, (source, target, rows, other) in enumerate(
            (
                (x_tokens_out, far_tokens, low, over_y),
                (y_tokens_out, far_tokens, high, over_x),
                (x_grads_out, far_grads, low, over_y),
                (y_grads_out, far_grads, high, over_x),
            )
        )
    ]

    @pl.when((block == 0) & (chunk == 0))
    def _():
        greet((over_x, over_y))
        for transfer in copies:
            transfer.start()

    parts = ((own_tokens, own_grads), (x_tokens, x_grads), (y_tokens, y_grads), (far_tokens, far_grads))
    for n, (tokens, grads) in enumerate(parts):

        @pl.when((block == n) & (chunk == 0))
        def _():
            if n == 3:
                for transfer in copies:
                    transfer.wait_recv()
            split_columns(all_tokens, tokens)
            split_columns(all_grads, grads)

    values = all_tokens[...]
    gate = both_halves(values, gate_own, gate_other)
    up = both_halves(values, up_own, up_other)
    sigmoid_gate = 1.0 / (1.0 + jnp.exp(-gate))
    silu = gate * sigmoid_gate
    hidden[...] = (silu * up).astype(jnp.bfloat16)
    gate_slope[...] = (up * sigmoid_gate * (1.0 + gate * (1.0 - sigmoid_gate))).astype(
        jnp.bfloat16
    )
    up_slope[...] = silu.astype(jnp.bfloat16)

    @pl.when((block == 3) & (chunk == pl.num_programs(1) - 1))
    def _():
        for transfer in copies:
            transfer.wait_send()


def gather_hidden(tokens, grads, weights):
    rows, width = tokens[0].shape
    _, hidden_count, half = weights[0].shape
    chunk = 512
    spec = pl.BlockSpec
    shape = jax.ShapeDtypeStruct
    outside = spec(memory_space=pl.ANY)
    whole = spec((rows, width), lambda b, c: (0, 0), pipeline_mode=pl.Buffered(1))
    bf16 = jnp.bfloat16
    return pl.pallas_call(
        hidden_kernel,
        grid=(4, hidden_count // chunk),
        in_specs=[outside] * 4 + [whole] * 6
        + [spec((None, chunk, half), lambda b, c, n=n: (n, c, 0)) for n in (0, 0, 1, 1)],
        out_specs=[spec((rows, width), lambda b, c: (b, 0))] * 2
        + [spec((rows, chunk), lambda b, c: (b, c))] * 3,
        out_shape=[shape((4 * rows, width), bf16)] * 2 + [shape((4 * rows, hidden_count), bf16)] * 3,
        scratch_shapes=[pltpu.VMEM((rows, width), bf16)] * 2
        + [pltpu.SemaphoreType.DMA((4,)), pltpu.SemaphoreType.DMA((4,))],
        compiler_params=pltpu.CompilerParams(
            collective_id=1, has_side_effects=True, vmem_limit_bytes=60 * 2**20
        ),
        cost_estimate=pl.CostEstimate(flops=1, bytes_accessed=1, transcendentals=0),
    )(*tokens[1:], *grads[1:], *tokens, *grads, *weights, *weights)


def reduce_copies(corner, send_x, send_y, got_corner, got_x, got_y, send, receive):
    _, over_x, over_y = neighbours()
    half = corner.shape[0] // 2
    low, high = pl.ds(0, half), pl.ds(half, half)
    plan = [
        (corner.at[low], got_corner.at[low], over_y),
        (corner.at[high], got_corner.at[high], over_x),
        (send_y.at[low], got_y.at[low], over_y),
        (send_y.at[high], got_y.at[high], over_y),
        (send_x.at[high], got_x.at[high], over_x),
        (send_x.at[low], got_x.at[low], over_x),
    ]
    return [
        pltpu.make_async_remote_copy(
            src_ref=source,
            dst_ref=target,
            send_sem=send.at[n],
            recv_sem=receive.at[n],
            device_id={"dp": other},
            device_id_type=MESH,
        )
        for n, (source, target, other) in enumerate(plan)
    ]


def corner_copies(corner, got_corner, send, receive, first):
    _, over_x, over_y = neighbours()
    half = corner.shape[0] // 2
    return [
        pltpu.make_async_remote_copy(
            src_ref=corner.at[rows],
            dst_ref=got_corner.at[rows],
            send_sem=send.at[first + n],
            recv_sem=receive.at[first + n],
            device_id={"dp": other},
            device_id_type=MESH,
        )
        for n, (rows, other) in enumerate(
            ((pl.ds(0, half), over_y), (pl.ds(half, half), over_x))
        )
    ]


def add_into(target, rows, other):
    total_rows = target[rows, :].astype(jnp.float32) + other[rows, :].astype(jnp.float32)
    target[rows, :] = total_rows.astype(target.dtype)


def feed_back_kernel(
    grads, hidden, gate_slope, up_slope,
    gate_own, gate_other, up_own, up_other, down_own, down_other,
    gate_grad, up_grad, out_own, out_x, out_y, two_grad,
    out_sum, two_sum, out_corner, keep_x, keep_y, got_out, local, corner, send_x, send_y, got_corner, got_x, got_y, send, receive,
):
    turn_index, chunk = pl.program_id(0), pl.program_id(1)
    last = chunk == pl.num_programs(1) - 1
    rows = grads.shape[0]
    low, high = slice(0, rows // 2), slice(rows // 2, rows)
    copies = reduce_copies(corner, send_x, send_y, got_corner, got_x, got_y, send, receive)
    copies += corner_copies(out_corner, got_out, send, receive, len(copies))
    writes = [
        pltpu.make_async_copy(source, target, local.at[n])
        for n, (source, target) in enumerate(
            ((keep_y, out_y), (keep_x, out_x), (out_corner, out_own))
        )
    ]

    @pl.when((turn_index == 0) & (chunk == 0))
    def _():
        _, over_x, over_y = neighbours()
        greet((over_x, over_y))

    @pl.when(chunk == 0)
    def _():
        out_sum[...] = jnp.zeros_like(out_sum)
        two_sum[...] = jnp.zeros_like(two_sum)

    hidden_grad = both_halves(grads[...], down_own, down_other)
    gate_back = (hidden_grad * gate_slope[...].astype(jnp.float32)).astype(jnp.bfloat16)
    up_back = (hidden_grad * up_slope[...].astype(jnp.float32)).astype(jnp.bfloat16)
    gate_grad[...] = gate_back
    up_grad[...] = up_back
    active = hidden[...]
    half = down_own.shape[1]
    for n, (gate, up, down) in enumerate(
        ((gate_own, up_own, down_own), (gate_other, up_other, down_other))
    ):
        for part in range(0, half, 512):
            cols = slice(part, part + 512)
            place = slice(n * half + part, n * half + part + 512)
            out_sum[:, place] += matmul(active, down[:, cols])
            two_sum[:, place] += matmul(gate_back, gate[:, cols]) + matmul(up_back, up[:, cols])

    @pl.when(last & (turn_index == 0))
    def _():
        merge_columns(corner, two_sum)
        copies[0].start()
        copies[1].start()
        merge_columns(out_corner, out_sum)
        copies[6].start()
        copies[7].start()

    @pl.when(last & (turn_index == 1))
    def _():
        merge_columns(send_y, two_sum)
        copies[2].start()
        merge_columns(keep_y, out_sum)

    @pl.when((chunk == 0) & (turn_index == 2))
    def _():
        copies[1].wait_recv()
        add_into(send_y, high, got_corner)
        copies[3].start()

    @pl.when(last & (turn_index == 2))
    def _():
        merge_columns(send_x, two_sum)
        copies[4].start()
        copies[0].wait_recv()
        add_into(send_x, low, got_corner)
        copies[5].start()
        merge_columns(keep_x, out_sum)
        copies[7].wait_recv()
        add_into(keep_y, high, got_out)
        writes[0].start()

    @pl.when(last & (turn_index == 3))
    def _():
        copies[6].wait_recv()
        add_into(keep_x, low, got_out)
        writes[1].start()
        copies[6].wait_send()
        copies[7].wait_send()
        merge_columns(out_corner, out_sum)
        writes[2].start()
        merge_columns(two_grad, two_sum)
        copies[2].wait_recv()
        copies[3].wait_recv()
        two_grad[...] += got_y[...].astype(jnp.float32)
        copies[4].wait_recv()
        copies[5].wait_recv()
        two_grad[...] += got_x[...].astype(jnp.float32)
        for transfer in copies[:6]:
            transfer.wait_send()
        for write in writes:
            write.wait()


def feed_back(grads, saved, weights, down):
    rows, width = grads.shape[0] // 4, grads.shape[1]
    _, hidden_count, half = weights[0].shape
    chunk = 512
    spec = pl.BlockSpec
    shape = jax.ShapeDtypeStruct
    bf16, f32 = jnp.bfloat16, jnp.float32
    block = lambda q, c: (3 - q, 0)
    piece = lambda q, c: (3 - q, c)
    return pl.pallas_call(
        feed_back_kernel,
        grid=(4, hidden_count // chunk),
        in_specs=[spec((rows, width), block)]
        + [spec((rows, chunk), piece)] * 3
        + [spec((None, chunk, half), lambda q, c, n=n: (n, c, 0)) for n in (0, 0, 1, 1)]
        + [spec((chunk, half), lambda q, c: (c, 0))] * 2,
        out_specs=[spec((rows, chunk), piece)] * 2
        + [spec(memory_space=pl.ANY)] * 3
        + [spec((rows, width), lambda q, c: (0, 0))],
        out_shape=[shape((4 * rows, hidden_count), bf16)] * 2
        + [shape((rows, width), bf16)] * 3
        + [shape((rows, width), f32)],
        scratch_shapes=[pltpu.VMEM((rows, width), f32)] * 2
        + [pltpu.VMEM((rows, width), bf16)] * 4
        + [pltpu.SemaphoreType.DMA((3,))]
        + [pltpu.VMEM((rows, width), bf16)] * 6
        + [pltpu.SemaphoreType.DMA((8,)), pltpu.SemaphoreType.DMA((8,))],
        compiler_params=pltpu.CompilerParams(
            collective_id=2, has_side_effects=True, vmem_limit_bytes=62 * 2**20
        ),
        cost_estimate=pl.CostEstimate(flops=1, bytes_accessed=1, transcendentals=0),
    )(grads, *saved, *weights, *weights, *down)


def is_crossing():
    return (lax.axis_index("dp") + lax.axis_index("mp")) % 2 == 1


def crossing_partner():
    me, z = lax.axis_index("dp"), lax.axis_index("mp")
    return {"dp": me + 1 - 2 * (me % 2), "mp": z + 1 - 2 * (z % 2)}


def crossing_copy(source, target, send, receive):
    return pltpu.make_async_remote_copy(
        src_ref=source,
        dst_ref=target,
        send_sem=send.at[0],
        recv_sem=receive.at[0],
        device_id=crossing_partner(),
        device_id_type=MESH,
    )


def outer_kernel(extra, left_own, left_other, right_own, right_other, *refs):
    weights = refs[:extra]
    if extra:
        layer, total_out, *spread, layer_out = refs[extra : extra + 5]
        cross = crossing_copy(layer, layer_out, refs[-3], refs[-2])
        stay = pltpu.make_async_copy(layer, layer_out, refs[-1].at[0])
        crossing = is_crossing()
        refs = refs[:-3]
    else:
        total_out = refs[0]
    own, corner, send_x, send_y, got_corner, got_x, got_y, send, receive = refs[-9:]
    step = pl.program_id(0)
    half = own.shape[0] // 2
    low, high = slice(0, half), slice(half, 2 * half)
    copies = reduce_copies(corner, send_x, send_y, got_corner, got_x, got_y, send, receive)

    if not extra:

        @pl.when(step == 0)
        def _():
            _, over_x, over_y = neighbours()
            greet((over_x, over_y))

    else:

        @pl.when((step == 0) & crossing)
        def _():
            _, over_x, over_y = neighbours()
            partner = crossing_partner()
            barrier = pltpu.get_barrier_semaphore()
            for other in (over_x, over_y):
                pl.semaphore_signal(barrier, inc=1, device_id={"dp": other}, device_id_type=MESH)
            pl.semaphore_signal(barrier, inc=1, device_id=partner, device_id_type=MESH)
            pl.semaphore_wait(barrier, 3)
            cross.start()

        @pl.when((step == 0) & jnp.logical_not(crossing))
        def _():
            _, over_x, over_y = neighbours()
            greet((over_x, over_y))
            stay.start()

    @pl.when(step < 8)
    def _():
        result = dot_first(left_own[...], right_own[...]) + dot_first(
            left_other[...], right_other[...]
        )
        order = (corner, corner, send_y, send_y, send_x, send_x, own, own)
        starts = (0, 1, 2, None, None, 4, None, None)
        for n, (target, first) in enumerate(zip(order, starts)):

            @pl.when(step == n)
            def _():
                target[high if n % 2 else low, :] = result.astype(target.dtype)
                if first is not None:
                    copies[first].start()

    for n, weight in enumerate(weights):

        @pl.when(step == 8 + n)
        def _():
            me = lax.axis_index("dp")
            x, y = (me // 2) % 2, me // 4
            k = min(n, 3)
            far_x = 1 - x if k % 2 else x
            far_y = 1 - y if k // 2 else y
            part = 512
            start = (2 * far_y + far_x) * part + (part // 2 if n == 4 else 0)
            cols = pl.ds(pl.multiple_of(start, 256), weight.shape[0])
            spread[0][:, cols] = dot_last(right_own[...], weight[...])
            spread[1][:, cols] = dot_last(right_other[...], weight[...]).astype(jnp.bfloat16)

    last = pl.num_programs(0) - 1

    @pl.when(step == min(9, 7 + extra))
    def _():
        copies[1].wait_recv()
        add_into(send_y, high, got_corner)
        copies[3].start()
        copies[0].wait_recv()
        add_into(send_x, low, got_corner)
        copies[5].start()

    @pl.when(step == last)
    def _():
        for n in (2, 4, 3, 5):
            copies[n].wait_recv()
        total_out[...] = (
            own[...] + got_x[...].astype(jnp.float32) + got_y[...].astype(jnp.float32)
        ).astype(total_out.dtype)
        for transfer in copies:
            transfer.wait_send()

    if extra:

        @pl.when((step == last) & crossing)
        def _():
            cross.wait()

        @pl.when((step == last) & jnp.logical_not(crossing))
        def _():
            stay.wait()


def outer(lefts, rights, by_left, collective_id, weights=(), layer=None):
    rows = 512
    wide = lefts[0][0].shape[1]
    right_wide = rights[0][0].shape[1]
    turn_of = lambda s: 6 - 2 * (jnp.minimum(s, 7) // 2) + jnp.minimum(s, 7) % 2
    if by_left:
        size = (wide // 8, right_wide)
        left_size = (rows, wide // 8)
        place_left = lambda row: lambda s: (row, turn_of(s))
        place_right = lambda row: lambda s: (row, 0)
    else:
        size = (wide // 2, right_wide // 4)
        left_size = (rows, wide // 2)
        place_left = lambda row: lambda s: (row, s % 2)
        place_right = lambda row: lambda s: (row, 3 - s // 2)
    both = (2 * size[0], size[1])
    spec, shape = pl.BlockSpec, jax.ShapeDtypeStruct
    out_specs = [spec(both, lambda s: (0, 0))]
    out_shape = [shape(both, jnp.bfloat16)]
    if weights:
        out_specs += [spec((rows, wide), lambda s: (0, 0))] * 2
        out_shape += [shape((rows, wide), jnp.float32), shape((rows, wide), jnp.bfloat16)]
        out_specs += [spec(memory_space=pl.ANY)]
        out_shape += [shape(layer.shape, layer.dtype)]
    made = pl.pallas_call(
        functools.partial(outer_kernel, len(weights)),
        grid=(8 + len(weights),),
        in_specs=[spec(left_size, place_left(row)) for _, row in lefts]
        + [spec((rows, size[1]), place_right(row)) for _, row in rights]
        + [
            spec(weight.shape, lambda s: (0, 0), pipeline_mode=pl.Buffered(1))
            for weight in weights
        ]
        + ([spec(memory_space=pl.ANY)] if weights else []),
        out_specs=out_specs,
        out_shape=out_shape,
        scratch_shapes=[pltpu.VMEM(both, jnp.float32)]
        + [pltpu.VMEM(both, jnp.bfloat16)] * 6
        + [pltpu.SemaphoreType.DMA((6,)), pltpu.SemaphoreType.DMA((6,))]
        + ([pltpu.SemaphoreType.DMA((1,))] * 3 if weights else []),
        compiler_params=pltpu.CompilerParams(
            collective_id=collective_id, has_side_effects=True, vmem_limit_bytes=60 * 2**20
        ),
        cost_estimate=pl.CostEstimate(flops=1, bytes_accessed=1, transcendentals=0),
    )(*[array for array, _ in (*lefts, *rights)], *weights, *([layer] if weights else []))
    return made if weights else made[0]


def columns_kernel(transposed, place, left, w0, w1, w2, w3_low, w3_high, own, other):
    rows = own.shape[0]

    def write(lines, result):
        for ref, kind in ((own, jnp.float32), (other, jnp.bfloat16)):
            start = 0 if ref is own else rows
            ref[...] = result(lines[start : start + rows]).astype(kind)

    for k, weight in enumerate((w0, w1, w2)):

        @pl.when(pl.program_id(0) == k)
        def _():
            step = dot_last if transposed else matmul
            write(left, lambda lines: step(lines, weight[...]))

    @pl.when(pl.program_id(0) == 3)
    def _():
        if transposed:
            write(
                left,
                lambda lines: jnp.concatenate(
                    [dot_last(lines, w3_low[...]), dot_last(lines, w3_high[...])], 1
                ),
            )
        else:
            middle = w3_low.shape[0]
            write(
                left,
                lambda lines: matmul(lines[:, :middle], w3_low[...])
                + matmul(lines[:, middle:], w3_high[...]),
            )


def columns(place, left, weights, transposed):
    length, depth = left.shape
    rows = length // 2
    part = weights[0].shape[0 if transposed else 1]
    width = 4 * part
    whole = lambda array: pl.BlockSpec(array.shape, lambda k, place: (0, 0))
    block = pl.BlockSpec((rows, part), lambda k, place: (0, k ^ place[0]))
    shape = jax.ShapeDtypeStruct
    return pl.pallas_call(
        functools.partial(columns_kernel, transposed),
        grid_spec=pltpu.PrefetchScalarGridSpec(
            num_scalar_prefetch=1,
            grid=(4,),
            in_specs=[whole(array) for array in (left, *weights)],
            out_specs=[block, block],
        ),
        out_shape=[shape((rows, width), jnp.float32), shape((rows, width), jnp.bfloat16)],
        compiler_params=pltpu.CompilerParams(vmem_limit_bytes=56 * 2**20),
        cost_estimate=pl.CostEstimate(flops=1, bytes_accessed=1, transcendentals=0),
    )(place, left, *weights)


def tile_call(kernel, place, ins, outs, kept):
    width = 2048
    tile = 256

    def spec(cut, columns):
        if cut == "rows":
            return pl.BlockSpec((tile, columns), lambda t, place: (t, 0))
        if cut == "low" or cut == "high":
            return pl.BlockSpec((tile, columns), lambda t, place: (0, 0))
        return pl.BlockSpec((cut, columns), lambda t, place: (0, 0))

    return pl.pallas_call(
        kernel,
        grid_spec=pltpu.PrefetchScalarGridSpec(
            num_scalar_prefetch=1,
            grid=(2,),
            in_specs=[spec(cut, array.shape[1]) for array, cut in ins],
            out_specs=[spec(cut, shape.shape[1]) for shape, cut in outs],
        ),
        out_shape=[shape for shape, _ in outs],
        compiler_params=pltpu.CompilerParams(vmem_limit_bytes=56 * 2**20),
        cost_estimate=pl.CostEstimate(flops=1, bytes_accessed=1, transcendentals=0),
    )(place, *[array for array, _ in ins])


def choose(low_ref, high_ref):
    return jnp.where(pl.program_id(0) == 0, low_ref[...], high_ref[...]).astype(jnp.float32)


def add_gain(gain_ref, values):
    @pl.when(pl.program_id(0) == 0)
    def _():
        gain_ref[...] = jnp.zeros_like(gain_ref)

    gain_ref[...] += jnp.sum(values.reshape(-1, 8, values.shape[1]), 0)


def relabelled(ref, values, place):
    width = values.shape[1] // 4
    for k in range(4):
        start = pl.multiple_of((place[0] ^ k) * width, width)
        ref[:, pl.ds(start, width)] = values[:, k * width : (k + 1) * width]


def first_norm_kernel(place, inputs, gain, normed):
    values, _ = norm_rows(inputs[...].astype(jnp.float32), gain[...])
    relabelled(normed, values.astype(jnp.bfloat16), place)


def middle_kernel(place, inputs, own, other, gain, middle, normed):
    values = inputs[...].astype(jnp.float32) + own[...] + other[...].astype(jnp.float32)
    middle[...] = values
    normed[...] = norm_rows(values, gain[...])[0].astype(jnp.bfloat16)


def middle_back_kernel(
    place, middle, cotangent, two, gain, middle_grad, branch, gain_grad
):
    two_grad = two[...]
    values = middle[...]
    _, factor = norm_rows(values, gain[...])
    add_gain(gain_grad, two_grad * values * factor)
    grads = cotangent[...].astype(jnp.float32) + norm_back(values, factor, gain[...], two_grad)
    middle_grad[...] = grads
    relabelled(branch, grads.astype(jnp.bfloat16), place)


def input_back_kernel(
    place, inputs, middle_grad, own, other, gain, input_grad, rounded, gain_grad
):
    one_grad = own[...] + other[...].astype(jnp.float32)
    values = inputs[...].astype(jnp.float32)
    _, factor = norm_rows(values, gain[...])
    add_gain(gain_grad, one_grad * values * factor)
    grads = middle_grad[...] + norm_back(values, factor, gain[...], one_grad)
    input_grad[...] = grads
    rounded[...] = grads.astype(jnp.bfloat16)


def output_kernel(place, middle, own, over_x, over_y, output):
    parts = [part[...].astype(jnp.float32) for part in (own, over_x, over_y)]
    output[...] = (middle[...] + parts[0] + parts[1] + parts[2]).astype(jnp.bfloat16)


def exchange(values, bit):
    return lax.ppermute(values, "dp", [(i, i ^ bit) for i in range(8)])


def swap_halves(values):
    pairs = []
    for i in range(8):
        for m in range(4):
            if (i & 1) != (m & 1):
                pairs.append((i * 4 + m, (i ^ 1) * 4 + (m ^ 1)))
    return lax.ppermute(values, ("dp", "mp"), pairs)


def after(values, earlier):
    return lax.optimization_barrier((values, earlier))[0]


def gather_near(block):
    return [exchange(block, 2), exchange(block, 4)]


def gather_far(near):
    half = near[0].shape[0] // 2
    return [exchange(near[0][:half], 4), exchange(near[1][half:], 2)]


def add_low(left, right):
    return (left.astype(jnp.float32) + right.astype(jnp.float32)).astype(jnp.bfloat16)


def pick(values, index, width, axis):
    return lax.dynamic_slice_in_dim(values, index * width, width, axis)


def in_order(own, other, core, axis=0):
    return jnp.where(
        core == 0,
        jnp.concatenate([own, other], axis),
        jnp.concatenate([other, own], axis),
    )


def total_plane(values):
    for bit in (1, 2, 4):
        values = values + exchange(values, bit)
    return values


def total_z(values):
    others = [lax.ppermute(values, "mp", [(i, i ^ bit) for i in range(4)]) for bit in (1, 2, 3)]
    return (values + others[0]) + (others[1] + others[2])


def fast(
    layer_input,
    out_grad,
    norm_attn,
    query_norm,
    key_norm,
    w_query,
    key_matrix,
    value_matrix,
    w_output,
    norm_mlp,
    w_gate,
    w_up,
    w_down,
):
    bf16, f32 = jnp.bfloat16, jnp.float32
    device = lax.axis_index("dp")
    core = device & 1
    place = jnp.reshape(device >> 1, (1,)).astype(jnp.int32)
    core_index = jnp.reshape(core, (1,)).astype(jnp.int32)
    crossing = core != (lax.axis_index("mp") & 1)
    planes = 4
    rows = layer_input.shape[0]
    width = layer_input.shape[1]
    units = w_gate.shape[1] // planes
    array = jax.ShapeDtypeStruct

    query_cols = w_query.shape[1] // 2
    key_cols = key_matrix.shape[1] // 2

    def heads_of(which):
        return jnp.concatenate(
            [
                pick(w_query, which, query_cols, 1),
                pick(key_matrix, which, key_cols, 1),
                pick(value_matrix, which, key_cols, 1),
            ],
            1,
        )

    qkv_pair = in_order(heads_of(core), exchange(heads_of(1 - core), 1), core)
    out_rows = w_output.shape[0] // 2
    out_pair = in_order(
        pick(w_output, core, out_rows, 0),
        exchange(pick(w_output, 1 - core, out_rows, 0), 1),
        core,
        1,
    )
    qkv_z = lax.all_gather(qkv_pair, "mp", axis=1, tiled=True)
    pieces = jnp.concatenate(
        [w.reshape(planes, units, w.shape[1]) for w in (w_gate.T, w_up.T, w_down)], 1
    )

    def piece_for(k):
        return pick(pieces, place[0] ^ k, 1, 0)[0]

    feed_own = jnp.concatenate(
        [piece_for(0)] + [exchange(piece_for(k), 2 * k) for k in (1, 2, 3)], 1
    )

    qkv_z = after(qkv_z, feed_own)
    qkv_near = gather_near(qkv_z)
    moved = swap_halves(after(layer_input, qkv_z))
    moved_grad = swap_halves(after(out_grad, qkv_z))
    out_z = lax.all_gather(
        after(out_pair, (moved, moved_grad, qkv_near)), "mp", axis=0, tiled=True
    )

    inputs = jnp.where(crossing, moved, layer_input)
    cotangent = jnp.where(crossing, moved_grad, out_grad)

    gain_one, gain_two = norm_attn[None, :], norm_mlp[None, :]
    gain_query, gain_key = query_norm[None, :], key_norm[None, :]
    (normed,) = tile_call(
        first_norm_kernel,
        place,
        [(inputs, "rows"), (gain_one, 1)],
        [(array((rows, width), bf16), "rows")],
        4,
    )
    cosines, sines = wide_tables(2 * rows)
    qkv_chips = [
        qkv_z,
        *qkv_near,
        *gather_far(after(qkv_near, (normed, cosines, sines, cotangent))),
    ]
    out_near = gather_near(after(out_z, qkv_chips))
    feed_own = after(feed_own, (out_z, qkv_chips))
    gate_up_half = lax.all_gather(
        feed_own[: 2 * units].reshape(2, units, width // 2), "mp", axis=1, tiled=True
    )
    down_half = lax.all_gather(feed_own[2 * units :], "mp", axis=0, tiled=True)
    normed_other = after(exchange(normed, 1), out_z)
    proj, query_rot, key_rot, value_low, attended, log_total = attend(
        core_index,
        normed,
        normed_other,
        qkv_chips,
        cosines,
        sines,
        gain_query,
        gain_key,
        planes,
        query_cols,
    )
    out_near = after(out_near, attended)
    out_chips = [out_z, *out_near, *gather_far(out_near)]
    grads_near = gather_near(after(cotangent, qkv_chips))
    branch_own, branch_other = columns(place, attended, out_chips, False)
    middle, tokens = tile_call(
        middle_kernel,
        place,
        [(inputs, "rows"), (branch_own, "rows"), (after(exchange(branch_other, 1), grads_near), "rows"), (gain_two, 1)],
        [
            (array((rows, width), f32), "rows"),
            (array((rows, width), bf16), "rows"),
        ],
        14,
    )

    tokens_near = gather_near(tokens)
    gate_up_w = [gate_up_half, exchange(after(gate_up_half, tokens), 1)]
    all_tokens, all_grads, all_hidden, gate_slope, up_slope = gather_hidden(
        [tokens, *tokens_near], [cotangent, *grads_near], gate_up_w
    )
    down_half = after(down_half, all_hidden)
    down_w = [down_half, exchange(down_half, 1)]

    def over_z(grad):
        return lax.psum_scatter(grad, "mp", scatter_dimension=0, tiled=True)

    half = width // 2
    down_other = dot_first(all_hidden, all_grads[:, half:]).astype(bf16)
    all_gate, all_up, out_own, out_x, out_y, two_grad = feed_back(
        after(all_grads, down_other),
        [all_hidden, gate_slope, up_slope],
        gate_up_w,
        down_w,
    )
    gate_other = dot_first(all_gate, all_tokens[:, half:]).astype(bf16)
    up_other = dot_first(all_up, all_tokens[:, half:]).astype(bf16)
    all_gate, all_up = after((all_gate, all_up), (gate_other, up_other))

    def own_half(left, right, other):
        own = dot_first(left, right[:, :half])
        return (own + exchange(other, 1).astype(f32)).astype(bf16)

    down_local = own_half(after(all_hidden, two_grad), all_grads, down_other)
    down_sum = over_z(down_local)
    gate_local = own_half(all_gate, all_tokens, gate_other)
    up_local = own_half(all_up, all_tokens, up_other)
    gate_sum, up_sum = over_z(gate_local), over_z(up_local)
    middle_grad, branch, gain_two_part = tile_call(
        middle_back_kernel,
        place,
        [(middle, "rows"), (cotangent, "rows"), (two_grad, "rows"), (gain_two, 1)],
        [
            (array((rows, width), f32), "rows"),
            (array((rows, width), bf16), "rows"),
            (array((8, width), f32), 8),
        ],
        18,
    )

    def unspread(own):
        cols = own.shape[1] // planes
        got = [own[:, :cols]] + [
            exchange(own[:, k * cols : (k + 1) * cols], 2 * k) for k in (1, 2, 3)
        ]
        return jnp.concatenate(got, 1), cols

    def chips_in_order(got, cols, rows):
        return jnp.concatenate([pick(got[rows], place[0] ^ k, cols, 1) for k in range(planes)], 0)

    down_got, cols = unspread(down_sum)
    down_own = chips_in_order(down_got, cols, slice(0, units)).astype(f32)

    branch_pair = after(exchange(branch, 1), (gate_local, up_local, down_local))
    out_parts = [out_own, exchange(out_x, 2), exchange(out_y, 4)]
    proj_grad, head_gains = attend_back(
        core_index,
        branch,
        branch_pair,
        out_chips,
        cosines,
        sines,
        gain_query,
        gain_key,
        (proj, query_rot, key_rot, value_low, log_total),
        planes,
        query_cols,
    )

    out_parts = after(out_parts, proj_grad)
    (layer_output,) = tile_call(
        output_kernel,
        place,
        [(middle, "rows")] + [(part, "rows") for part in out_parts],
        [(array((rows, width), bf16), "rows")],
        12,
    )
    attended = after(attended, (proj_grad, out_parts))
    out_local = outer([(attended, 0), (attended, 1)], [(branch, 0), (branch_pair, 0)], False, 4)
    out_sum = over_z(out_local)
    proj_grad = after(proj_grad, (down_own, gate_sum, out_local))
    qkv_local, one_own, one_other, output_moved = outer(
        [(normed, 0), (normed_other, 0)],
        [(proj_grad, 0), (proj_grad, 1)],
        True,
        3,
        qkv_chips,
        layer_output,
    )
    qkv_local = after(qkv_local, (up_sum, out_sum))
    qkv_sum = lax.psum_scatter(qkv_local, "mp", scatter_dimension=1, tiled=True)
    input_grad, rounded_grad, gain_one_part = tile_call(
        input_back_kernel,
        place,
        [
            (inputs, "rows"),
            (middle_grad, "rows"),
            (one_own, "rows"),
            (exchange(one_other, 1), "rows"),
            (gain_one, 1),
        ],
        [
            (array((rows, width), f32), "rows"),
            (array((rows, width), bf16), "rows"),
            (array((8, width), f32), 8),
        ],
        18,
    )
    gate_up_got, cols = unspread(
        after(jnp.concatenate([gate_sum, up_sum], 0), rounded_grad)
    )
    gate_own = chips_in_order(gate_up_got, cols, slice(0, units)).T.astype(f32)
    up_own = chips_in_order(gate_up_got, cols, slice(units, 2 * units)).T.astype(f32)
    gain_sums = total_plane(
        after(jnp.concatenate(
            [
                jnp.sum(gain_one_part, 0),
                jnp.sum(head_gains[:8], 0),
                jnp.sum(head_gains[8:], 0),
                jnp.sum(gain_two_part, 0),
            ]
        ), qkv_local)
    )
    grad_moved = swap_halves(rounded_grad)
    gain_sums = total_z(after(gain_sums, (gate_own, up_own, grad_moved)))
    pair_rows = qkv_sum.shape[0] // 2
    qkv_other = exchange(pick(qkv_sum, 1 - core, pair_rows, 0), 1)
    qkv_own = pick(qkv_sum, core, pair_rows, 0)

    def both(start, stop):
        return in_order(qkv_own[:, start:stop], qkv_other[:, start:stop], core, 1).astype(f32)

    pair_cols = out_sum.shape[1] // 2
    out_other = exchange(pick(out_sum, 1 - core, pair_cols, 1), 1)
    out_own = pick(out_sum, core, pair_cols, 1)
    return (
        output_moved,
        jnp.where(crossing, grad_moved.astype(f32), input_grad),
        gain_sums[:width],
        gain_sums[width : width + HEAD_SIZE],
        gain_sums[width + HEAD_SIZE : width + 2 * HEAD_SIZE],
        both(0, query_cols),
        both(query_cols, query_cols + key_cols),
        both(query_cols + key_cols, query_cols + 2 * key_cols),
        in_order(out_own, out_other, core, 0).astype(f32),
        gain_sums[width + 2 * HEAD_SIZE :],
        gate_own,
        up_own,
        down_own,
    )


def solution(mesh):
    in_specs = (
        P(("dp", "mp"), None),
        P(("dp", "mp"), None),
        P(),
        P(),
        P(),
        P("dp", "mp"),
        P("dp", "mp"),
        P("dp", "mp"),
        P("mp", "dp"),
        P(),
        P("dp", "mp"),
        P("dp", "mp"),
        P("mp", "dp"),
    )
    out_specs = (
        P(("dp", "mp"), None),
        P(("dp", "mp"), None),
        P(),
        P(),
        P(),
        P("dp", "mp"),
        P("dp", "mp"),
        P("dp", "mp"),
        P("mp", "dp"),
        P(),
        P("dp", "mp"),
        P("dp", "mp"),
        P("mp", "dp"),
    )
    whole_sequences = dict(mesh.shape) == {"dp": 8, "mp": 4}
    local = fast if whole_sequences else generic
    return jax.shard_map(local, mesh=mesh, in_specs=in_specs, out_specs=out_specs, check_vma=False)
```

```python
import functools

import jax
import jax.numpy as jnp
from jax import lax
from jax.experimental import pallas as pl
from jax.experimental.pallas import tpu as pltpu
from jax.sharding import PartitionSpec as P

HEAD_SIZE = 128
SEQUENCE_LENGTH = 1024


EPSILON = 1e-06
THETA = 1000000.0


def norm_rows(values, gain):
    factor = lax.rsqrt(jnp.mean(values * values, -1, keepdims=True) + EPSILON)
    return (values * factor * gain, factor)


def norm_back(values, factor, gain, upstream):
    scaled = upstream * gain
    inner = jnp.mean(scaled * values, -1, keepdims=True)
    return factor * scaled - values * (factor * factor * factor) * inner


def tables(length, width):
    half_width = width // 2
    frequencies = THETA ** (-(jnp.arange(half_width, dtype=jnp.float32) * 2.0 / width))
    angles = jnp.arange(length, dtype=jnp.float32)[:, None] * frequencies[None, :]
    return (jnp.cos(angles), jnp.sin(angles))


def rotate(values, cosine_table, sine_table):
    half_width = values.shape[-1] // 2
    first_half = values[..., :half_width]
    second_half = values[..., half_width:]
    cosine_part = cosine_table[:, None, :]
    sine_part = sine_table[:, None, :]
    return jnp.concatenate(
        [
            first_half * cosine_part - second_half * sine_part,
            second_half * cosine_part + first_half * sine_part,
        ],
        -1,
    )


def rotate_back(grads, cosine_table, sine_table):
    half_width = grads.shape[-1] // 2
    first_half = grads[..., :half_width]
    second_half = grads[..., half_width:]
    cosine_part = cosine_table[:, None, :]
    sine_part = sine_table[:, None, :]
    return jnp.concatenate(
        [
            first_half * cosine_part + second_half * sine_part,
            second_half * cosine_part - first_half * sine_part,
        ],
        -1,
    )


def matmul(left, right):
    return jnp.dot(left, right, preferred_element_type=jnp.float32)


def dot_last(left, right):
    return lax.dot_general(
        left, right, (((1,), (1,)), ((), ())), preferred_element_type=jnp.float32
    )


def dot_first(left, right):
    return lax.dot_general(
        left, right, (((0,), (0,)), ((), ())), preferred_element_type=jnp.float32
    )


def masked_scores(query_block, keys, start, block_rows, scale):
    raw = (
        jnp.einsum("qhgd,khd->hgqk", query_block, keys, preferred_element_type=jnp.float32) * scale
    )
    query_places = start + jnp.arange(block_rows)[:, None]
    key_places = jnp.arange(keys.shape[0])[None, :]
    return jnp.where(key_places <= query_places, raw, -jnp.inf)


def generic(
    layer_input,
    out_grad,
    norm_attn,
    query_norm,
    key_norm,
    w_query,
    key_matrix,
    value_matrix,
    w_output,
    norm_mlp,
    w_gate,
    w_up,
    w_down,
):
    inputs = layer_input.astype(jnp.float32)
    query_full, key_full, value_full, output_full = (
        lax.all_gather(w_query, "dp", axis=0, tiled=True),
        lax.all_gather(key_matrix, "dp", axis=0, tiled=True),
        lax.all_gather(value_matrix, "dp", axis=0, tiled=True),
        lax.all_gather(w_output, "dp", axis=1, tiled=True),
    )
    first_normed, factor_one = norm_rows(inputs, norm_attn)
    normed_all = lax.all_gather(first_normed.astype(jnp.bfloat16), "mp", axis=0, tiled=True)
    total_rows = normed_all.shape[0]
    sequence_batch = total_rows // SEQUENCE_LENGTH
    query_heads = query_full.shape[1] // HEAD_SIZE
    shared_heads = key_full.shape[1] // HEAD_SIZE
    heads_per_group = query_heads // shared_heads
    query_proj = matmul(normed_all, query_full).reshape(
        sequence_batch, SEQUENCE_LENGTH, query_heads, HEAD_SIZE
    )
    key_projected = matmul(normed_all, key_full).reshape(
        sequence_batch, SEQUENCE_LENGTH, shared_heads, HEAD_SIZE
    )
    value_low = (
        matmul(normed_all, value_full)
        .astype(jnp.bfloat16)
        .reshape(sequence_batch, SEQUENCE_LENGTH, shared_heads, HEAD_SIZE)
    )
    cosine_table, sine_table = tables(SEQUENCE_LENGTH, HEAD_SIZE)
    query_normed, query_factor = norm_rows(query_proj, query_norm)
    query_rotated = rotate(query_normed, cosine_table, sine_table).astype(jnp.bfloat16)
    query_rotated = query_rotated.reshape(
        sequence_batch, SEQUENCE_LENGTH, shared_heads, heads_per_group, HEAD_SIZE
    )
    key_normed, key_factor = norm_rows(key_projected, key_norm)
    key_rot = rotate(key_normed, cosine_table, sine_table).astype(jnp.bfloat16)
    block_rows = min(512, SEQUENCE_LENGTH)
    block_count = SEQUENCE_LENGTH // block_rows
    scale = HEAD_SIZE ** (-0.5)
    attended_pieces = []
    log_totals = []
    for seq_index in range(sequence_batch):
        for block_index in range(block_count):
            start = block_index * block_rows
            query_block = query_rotated[seq_index, start : start + block_rows]
            scores = masked_scores(query_block, key_rot[seq_index], start, block_rows, scale)
            largest = jnp.max(scores, -1, keepdims=True)
            expanded = jnp.exp(scores - largest)
            summed = jnp.sum(expanded, -1, keepdims=True)
            probs_low = (expanded / summed).astype(jnp.bfloat16)
            block_out = jnp.einsum(
                "hgqk,khd->qhgd",
                probs_low,
                value_low[seq_index],
                preferred_element_type=jnp.float32,
            )
            attended_pieces.append(block_out.reshape(block_rows, query_heads * HEAD_SIZE))
            log_totals.append(largest + jnp.log(summed))
    attended = jnp.concatenate(attended_pieces, 0).astype(jnp.bfloat16)
    attn_sum = lax.psum_scatter(
        matmul(attended, output_full), "mp", scatter_dimension=0, tiled=True
    )
    middle = inputs + attn_sum
    gate_full, up_full, down_full = (
        lax.all_gather(w_gate, "dp", axis=0, tiled=True),
        lax.all_gather(w_up, "dp", axis=0, tiled=True),
        lax.all_gather(w_down, "dp", axis=1, tiled=True),
    )
    normed_two, factor_two = norm_rows(middle, norm_mlp)
    normed_two_all = lax.all_gather(normed_two.astype(jnp.bfloat16), "mp", axis=0, tiled=True)
    gate_value = matmul(normed_two_all, gate_full)
    up_value = matmul(normed_two_all, up_full)
    hidden_low = (jax.nn.silu(gate_value) * up_value).astype(jnp.bfloat16)
    mlp_sum = lax.psum_scatter(
        matmul(hidden_low, down_full).astype(jnp.bfloat16), "mp", scatter_dimension=0, tiled=True
    ).astype(jnp.float32)
    layer_output = (middle + mlp_sum).astype(jnp.bfloat16)
    grad_rows = lax.all_gather(out_grad, "mp", axis=0, tiled=True)
    gate_back, up_back, down_back = (
        lax.all_gather(w_gate, "dp", axis=0, tiled=True),
        lax.all_gather(w_up, "dp", axis=0, tiled=True),
        lax.all_gather(w_down, "dp", axis=1, tiled=True),
    )
    hidden_grad = dot_last(grad_rows, down_back)
    down_grad = dot_first(hidden_low, grad_rows)
    sigmoid_gate = jax.nn.sigmoid(gate_value)
    gate_grad = (
        hidden_grad * up_value * sigmoid_gate * (1.0 + gate_value * (1.0 - sigmoid_gate))
    ).astype(jnp.bfloat16)
    up_grad = (hidden_grad * gate_value * sigmoid_gate).astype(jnp.bfloat16)
    gate_weight_grad = dot_first(normed_two_all, gate_grad)
    up_weight_grad = dot_first(normed_two_all, up_grad)
    two_grad = lax.psum_scatter(
        dot_last(gate_grad, gate_back) + dot_last(up_grad, up_back),
        "mp",
        scatter_dimension=0,
        tiled=True,
    )
    gain_two_grad = jnp.sum(two_grad * middle * factor_two, 0)
    middle_grad = out_grad.astype(jnp.float32) + norm_back(middle, factor_two, norm_mlp, two_grad)
    mlp_grads = (
        lax.psum_scatter(
            gate_weight_grad.astype(jnp.bfloat16), "dp", scatter_dimension=0, tiled=True
        ).astype(jnp.float32),
        lax.psum_scatter(
            up_weight_grad.astype(jnp.bfloat16), "dp", scatter_dimension=0, tiled=True
        ).astype(jnp.float32),
        lax.psum_scatter(
            down_grad.astype(jnp.bfloat16), "dp", scatter_dimension=1, tiled=True
        ).astype(jnp.float32),
    )
    branch_all = lax.all_gather(middle_grad.astype(jnp.bfloat16), "mp", axis=0, tiled=True)
    output_weight_grad = dot_first(attended, branch_all)
    attended_grad = dot_last(branch_all, output_full).astype(jnp.bfloat16)
    attended_grad = attended_grad.reshape(
        sequence_batch, SEQUENCE_LENGTH, shared_heads, heads_per_group, HEAD_SIZE
    )
    query_grad_seqs = []
    key_grad_seqs = []
    value_grad_seqs = []
    for seq_index in range(sequence_batch):
        key_running = jnp.zeros((SEQUENCE_LENGTH, shared_heads, HEAD_SIZE), jnp.float32)
        value_running = jnp.zeros((SEQUENCE_LENGTH, shared_heads, HEAD_SIZE), jnp.float32)
        query_blocks = []
        for block_index in range(block_count):
            start = block_index * block_rows
            query_block = query_rotated[seq_index, start : start + block_rows]
            scores = masked_scores(query_block, key_rot[seq_index], start, block_rows, scale)
            probs_full = jnp.exp(scores - log_totals[seq_index * block_count + block_index])
            probs_low = probs_full.astype(jnp.bfloat16)
            grad_block = attended_grad[seq_index, start : start + block_rows]
            prob_grad = jnp.einsum(
                "qhgd,khd->hgqk",
                grad_block,
                value_low[seq_index],
                preferred_element_type=jnp.float32,
            )
            row_inner = jnp.sum(probs_full * prob_grad, -1, keepdims=True)
            score_grad = (probs_full * (prob_grad - row_inner)).astype(jnp.bfloat16)
            query_blocks.append(
                jnp.einsum(
                    "hgqk,khd->qhgd",
                    score_grad,
                    key_rot[seq_index],
                    preferred_element_type=jnp.float32,
                )
                * scale
            )
            key_running = (
                key_running
                + jnp.einsum(
                    "hgqk,qhgd->khd", score_grad, query_block, preferred_element_type=jnp.float32
                )
                * scale
            )
            value_running = value_running + jnp.einsum(
                "hgqk,qhgd->khd", probs_low, grad_block, preferred_element_type=jnp.float32
            )
        query_grad_seqs.append(jnp.concatenate(query_blocks, 0))
        key_grad_seqs.append(key_running)
        value_grad_seqs.append(value_running)
    rot_query_grad = jnp.stack(query_grad_seqs, 0).reshape(
        sequence_batch, SEQUENCE_LENGTH, query_heads, HEAD_SIZE
    )
    rot_key_grad = jnp.stack(key_grad_seqs, 0)
    value_grad = (
        jnp.stack(value_grad_seqs, 0)
        .reshape(total_rows, shared_heads * HEAD_SIZE)
        .astype(jnp.bfloat16)
    )
    query_normed_grad = rotate_back(rot_query_grad, cosine_table, sine_table)
    query_gain_grad = jnp.sum(query_normed_grad * query_proj * query_factor, (0, 1, 2))
    query_grad = norm_back(query_proj, query_factor, query_norm, query_normed_grad)
    query_grad = query_grad.reshape(total_rows, query_heads * HEAD_SIZE).astype(jnp.bfloat16)
    key_normed_grad = rotate_back(rot_key_grad, cosine_table, sine_table)
    key_gain_grad = jnp.sum(key_normed_grad * key_projected * key_factor, (0, 1, 2))
    key_grad = norm_back(key_projected, key_factor, key_norm, key_normed_grad)
    key_grad = key_grad.reshape(total_rows, shared_heads * HEAD_SIZE).astype(jnp.bfloat16)
    query_weight_grad = dot_first(normed_all, query_grad)
    key_weight_grad = dot_first(normed_all, key_grad)
    value_weight_grad = dot_first(normed_all, value_grad)
    one_partial = (
        dot_last(query_grad, query_full)
        + dot_last(key_grad, key_full)
        + dot_last(value_grad, value_full)
    )
    one_grad = lax.psum_scatter(
        one_partial.astype(jnp.bfloat16), "mp", scatter_dimension=0, tiled=True
    ).astype(jnp.float32)
    gain_one_grad = jnp.sum(one_grad * inputs * factor_one, 0)
    input_grad = middle_grad + norm_back(inputs, factor_one, norm_attn, one_grad)
    attn_grads = (
        lax.psum_scatter(
            query_weight_grad.astype(jnp.bfloat16), "dp", scatter_dimension=0, tiled=True
        ).astype(jnp.float32),
        lax.psum_scatter(
            key_weight_grad.astype(jnp.bfloat16), "dp", scatter_dimension=0, tiled=True
        ).astype(jnp.float32),
        lax.psum_scatter(
            value_weight_grad.astype(jnp.bfloat16), "dp", scatter_dimension=0, tiled=True
        ).astype(jnp.float32),
        lax.psum_scatter(
            output_weight_grad.astype(jnp.bfloat16), "dp", scatter_dimension=1, tiled=True
        ).astype(jnp.float32),
    )
    gain_sums = lax.psum(
        (gain_one_grad, query_gain_grad, key_gain_grad, gain_two_grad), ("dp", "mp")
    )
    return (
        layer_output,
        input_grad,
        gain_sums[0],
        gain_sums[1],
        gain_sums[2],
        attn_grads[0],
        attn_grads[1],
        attn_grads[2],
        attn_grads[3],
        gain_sums[3],
        mlp_grads[0],
        mlp_grads[1],
        mlp_grads[2],
    )


ROW_BLOCK = 256


def wide_tables(length):
    cosine_table, sine_table = tables(length, HEAD_SIZE)
    return (
        jnp.concatenate([cosine_table, cosine_table], 1),
        jnp.concatenate([-sine_table, sine_table], 1),
    )


def turn(values, cosines, sines):
    return values * cosines + pltpu.roll(values, HEAD_SIZE // 2, 1) * sines


def turn_back(values, cosines, sines):
    return values * cosines - pltpu.roll(values, HEAD_SIZE // 2, 1) * sines


def causal(rows):
    query_places = lax.broadcasted_iota(jnp.int32, (rows, rows), 0)
    key_places = lax.broadcasted_iota(jnp.int32, (rows, rows), 1)
    return key_places <= query_places


def attend_kernel(
    core, own, other, w0, w1, w2, w3_low, w3_high, cosines, sines, query_gain, key_gain,
    proj, query_rot, key_rot, value, attended, log_total,
):
    half = own.shape[0]
    length = 2 * half
    scale = HEAD_SIZE ** (-0.5)
    query_cols = query_rot.shape[1]
    heads = query_cols // HEAD_SIZE
    for h in range(2):
        here = core[0] == h
        rows = slice(h * half, (h + 1) * half)
        block = None
        start = 0
        for weight in (w0, w1, w2, w3_low, w3_high):
            cols = slice(start, start + weight.shape[0])
            start = cols.stop
            tokens = jnp.where(here, own[:, cols], other[:, cols])
            term = matmul(tokens, weight[...])
            block = term if block is None else block + term
        proj[rows, :] = block
        cos_rows, sin_rows = cosines[rows, :], sines[rows, :]
        for head in range(heads):
            cols = slice(head * HEAD_SIZE, (head + 1) * HEAD_SIZE)
            normed, _ = norm_rows(block[:, cols], query_gain[...])
            query_rot[rows, cols] = turn(normed, cos_rows, sin_rows).astype(jnp.bfloat16)
        cols = slice(query_cols, query_cols + HEAD_SIZE)
        normed, _ = norm_rows(block[:, cols], key_gain[...])
        key_rot[rows, :] = turn(normed, cos_rows, sin_rows).astype(jnp.bfloat16)
        value[rows, :] = block[:, query_cols + HEAD_SIZE :].astype(jnp.bfloat16)
    allowed = causal(ROW_BLOCK)

    def place(start):
        return pl.ds(pl.multiple_of((start + core[0] * half) % length, ROW_BLOCK), ROW_BLOCK)

    lane = lax.broadcasted_iota(jnp.int32, (ROW_BLOCK, HEAD_SIZE), 1)
    for start in range(0, length, ROW_BLOCK):
        rows = slice(start, start + ROW_BLOCK)
        logs = jnp.zeros((ROW_BLOCK, HEAD_SIZE), jnp.float32)
        for head in range(heads):
            cols = slice(head * HEAD_SIZE, (head + 1) * HEAD_SIZE)
            query = query_rot[rows, cols]
            scores = [jnp.where(allowed, dot_last(query, key_rot[rows, :]) * scale, -jnp.inf)]
            if start:
                scores.append(dot_last(query, key_rot[:start, :]) * scale)
            largest = functools.reduce(
                jnp.maximum, [jnp.max(s, -1, keepdims=True) for s in scores]
            )
            expanded = [jnp.exp(s - largest) for s in scores]
            summed = sum(jnp.sum(e, -1, keepdims=True) for e in expanded)
            out = matmul(expanded[0].astype(jnp.bfloat16), value[rows, :])
            if start:
                out = out + matmul(expanded[1].astype(jnp.bfloat16), value[:start, :])
            attended[place(start), cols] = (out / summed).astype(jnp.bfloat16)
            logs = jnp.where(lane == head, largest + jnp.log(summed), logs)
        log_total[rows, :] = logs


def attend(core, own, other, weights, cosines, sines, query_gain, key_gain, planes, query_cols):
    half, width = own.shape
    length = 2 * half
    cols = weights[0].shape[1]
    group = cols // planes
    whole = lambda shape: pl.BlockSpec(shape, lambda g, core: (0, 0))
    column = lambda rows, width: pl.BlockSpec((rows, width), lambda g, core: (0, g))
    shape = jax.ShapeDtypeStruct
    return pl.pallas_call(
        attend_kernel,
        grid_spec=pltpu.PrefetchScalarGridSpec(
            num_scalar_prefetch=1,
            grid=(planes,),
            in_specs=[whole((half, width))] * 2
            + [column(weight.shape[0], group) for weight in weights]
            + [whole((length, HEAD_SIZE))] * 2
            + [whole((1, HEAD_SIZE))] * 2,
            out_specs=[
                column(length, group),
                column(length, query_cols),
                column(length, HEAD_SIZE),
                column(length, HEAD_SIZE),
                column(length, query_cols),
                column(length, HEAD_SIZE),
            ],
        ),
        out_shape=[
            shape((length, cols), jnp.float32),
            shape((length, planes * query_cols), jnp.bfloat16),
            shape((length, planes * HEAD_SIZE), jnp.bfloat16),
            shape((length, planes * HEAD_SIZE), jnp.bfloat16),
            shape((length, planes * query_cols), jnp.bfloat16),
            shape((length, planes * HEAD_SIZE), jnp.float32),
        ],
        compiler_params=pltpu.CompilerParams(vmem_limit_bytes=56 * 2**20),
        cost_estimate=pl.CostEstimate(flops=1, bytes_accessed=1, transcendentals=0),
    )(core, own, other, *weights, cosines, sines, query_gain, key_gain)


def attend_back_kernel(
    core, own, other, o0, o1, o2, o3_low, o3_high, cosines, sines, query_gain, key_gain,
    proj, query_rot, key_rot, value, log_total,
    proj_grad, gain_grads, grad, key_total, value_total,
):
    half = own.shape[0]
    length = 2 * half
    part = o0.shape[1]
    scale = HEAD_SIZE ** (-0.5)
    query_cols = query_rot.shape[1]
    heads = query_cols // HEAD_SIZE

    @pl.when(pl.program_id(0) == 0)
    def _():
        gain_grads[...] = jnp.zeros_like(gain_grads)

    low = pl.program_id(0) < pl.num_programs(0) // 2
    corner = jnp.where(low, o3_low[...], o3_high[...])
    for h in range(2):
        here = core[0] == h
        block = None
        for k, weight in enumerate((o0[...], o1[...], o2[...], corner)):
            cols = slice(k * part, (k + 1) * part)
            tokens = jnp.where(here, own[:, cols], other[:, cols])
            term = dot_last(tokens, weight)
            block = term if block is None else block + term
        grad[h * half : (h + 1) * half, :] = block.astype(jnp.bfloat16)
    key_total[...] = jnp.zeros_like(key_total)
    value_total[...] = jnp.zeros_like(value_total)
    allowed = causal(ROW_BLOCK)

    def fold(values):
        return jnp.sum(values.reshape(-1, 8, HEAD_SIZE), 0)

    def place(start):
        return pl.ds(pl.multiple_of((start + core[0] * half) % length, ROW_BLOCK), ROW_BLOCK)

    for start in range(0, length, ROW_BLOCK):
        rows = slice(start, start + ROW_BLOCK)
        for head in range(heads):
            cols = slice(head * HEAD_SIZE, (head + 1) * HEAD_SIZE)
            query = query_rot[rows, cols]
            upstream = grad[rows, cols]
            logs = log_total[rows, head : head + 1]
            spans = [rows] + ([slice(0, start)] if start else [])
            probs, prob_grads = [], []
            for n, span in enumerate(spans):
                raw = dot_last(query, key_rot[span, :]) * scale
                if n == 0:
                    raw = jnp.where(allowed, raw, -jnp.inf)
                probs.append(jnp.exp(raw - logs))
                prob_grads.append(dot_last(upstream, value[span, :]))
            inner = sum(jnp.sum(p * d, -1, keepdims=True) for p, d in zip(probs, prob_grads))
            query_back = None
            for span, p, d in zip(spans, probs, prob_grads):
                score_grad = (p * (d - inner)).astype(jnp.bfloat16)
                term = matmul(score_grad, key_rot[span, :])
                query_back = term if query_back is None else query_back + term
                key_total[span, :] += dot_first(score_grad, query)
                value_total[span, :] += dot_first(p.astype(jnp.bfloat16), upstream)
            normed_grad = turn_back(query_back * scale, cosines[rows, :], sines[rows, :])
            values = proj[rows, cols]
            _, factor = norm_rows(values, query_gain[...])
            gain_grads[:8, :] += fold(normed_grad * values * factor)
            back = norm_back(values, factor, query_gain[...], normed_grad)
            proj_grad[place(start), cols] = back.astype(jnp.bfloat16)
    for start in range(0, length, ROW_BLOCK):
        rows = slice(start, start + ROW_BLOCK)
        cols = slice(query_cols, query_cols + HEAD_SIZE)
        normed_grad = turn_back(key_total[rows, :] * scale, cosines[rows, :], sines[rows, :])
        values = proj[rows, cols]
        _, factor = norm_rows(values, key_gain[...])
        gain_grads[8:, :] += fold(normed_grad * values * factor)
        back = norm_back(values, factor, key_gain[...], normed_grad)
        proj_grad[place(start), cols] = back.astype(jnp.bfloat16)
        proj_grad[place(start), query_cols + HEAD_SIZE :] = value_total[rows, :].astype(
            jnp.bfloat16
        )


def attend_back(
    core, own, other, weights, cosines, sines, query_gain, key_gain, saved, planes, query_cols
):
    half, width = own.shape
    length = 2 * half
    part = weights[0].shape[1]
    proj, query_rot, key_rot, value, log_total = saved
    cols = proj.shape[1]
    group = cols // planes
    whole = lambda shape: pl.BlockSpec(shape, lambda g, core: (0, 0))
    column = lambda rows, width: pl.BlockSpec((rows, width), lambda g, core: (0, g))
    shape = jax.ShapeDtypeStruct
    return pl.pallas_call(
        attend_back_kernel,
        grid_spec=pltpu.PrefetchScalarGridSpec(
            num_scalar_prefetch=1,
            grid=(planes,),
            in_specs=[whole((half, width))] * 2
            + [pl.BlockSpec((query_cols, part), lambda g, core: (g, 0))] * 3
            + [
                pl.BlockSpec((query_cols, part), lambda g, core: (jnp.minimum(g, 1), 0)),
                pl.BlockSpec((query_cols, part), lambda g, core: (jnp.maximum(g - 2, 0), 0)),
            ]
            + [whole((length, HEAD_SIZE))] * 2
            + [whole((1, HEAD_SIZE))] * 2
            + [
                column(length, group),
                column(length, query_cols),
                column(length, HEAD_SIZE),
                column(length, HEAD_SIZE),
                column(length, HEAD_SIZE),
            ],
            out_specs=[column(length, group), whole((16, HEAD_SIZE))],
            scratch_shapes=[
                pltpu.VMEM((length, query_cols), jnp.bfloat16),
                pltpu.VMEM((length, HEAD_SIZE), jnp.float32),
                pltpu.VMEM((length, HEAD_SIZE), jnp.float32),
            ],
        ),
        out_shape=[
            shape((length, cols), jnp.bfloat16),
            shape((16, HEAD_SIZE), jnp.float32),
        ],
        compiler_params=pltpu.CompilerParams(vmem_limit_bytes=56 * 2**20),
        cost_estimate=pl.CostEstimate(flops=1, bytes_accessed=1, transcendentals=0),
    )(core, own, other, *weights, cosines, sines, query_gain, key_gain, *saved)


MESH = pl.DeviceIdType.MESH


def neighbours():
    me = lax.axis_index("dp")
    x, y = (me // 2) % 2, me // 4
    return me, me + 2 - 4 * x, me + 4 - 8 * y


def greet(others):
    barrier = pltpu.get_barrier_semaphore()
    for other in others:
        pl.semaphore_signal(barrier, inc=1, device_id={"dp": other}, device_id_type=MESH)
    pl.semaphore_wait(barrier, len(others))


def column_places(width):
    me = lax.axis_index("dp")
    core, x, y = me % 2, (me // 2) % 2, me // 4
    block = 256
    places = []
    for n in range(width // block):
        here = core if n < 4 else 1 - core
        far_x = 1 - x if n % 2 else x
        far_y = 1 - y if (n // 2) % 2 else y
        start = (4 * far_y + 2 * far_x + here) * block
        places.append(pl.ds(pl.multiple_of(start, block), block))
    return places


def split_columns(target, values):
    for n, cols in enumerate(column_places(values.shape[1])):
        target[:, n * 256 : (n + 1) * 256] = values[:, cols]


def merge_columns(target, sums):
    for n, cols in enumerate(column_places(sums.shape[1])):
        target[:, cols] = sums[:, n * 256 : (n + 1) * 256].astype(target.dtype)


def both_halves(left, own, other):
    half = own.shape[1]
    return dot_last(left[:, :half], own[...]) + dot_last(left[:, half:], other[...])


def hidden_kernel(
    x_tokens_out, y_tokens_out, x_grads_out, y_grads_out,
    own_tokens, x_tokens, y_tokens, own_grads, x_grads, y_grads,
    gate_own, gate_other, up_own, up_other,
    all_tokens, all_grads, hidden, gate_slope, up_slope,
    far_tokens, far_grads, send, receive,
):
    block, chunk = pl.program_id(0), pl.program_id(1)
    _, over_x, over_y = neighbours()
    half = far_tokens.shape[0] // 2
    low, high = pl.ds(0, half), pl.ds(half, half)
    copies = [
        pltpu.make_async_remote_copy(
            src_ref=source.at[rows],
            dst_ref=target.at[rows],
            send_sem=send.at[n],
            recv_sem=receive.at[n],
            device_id={"dp": other},
            device_id_type=MESH,
        )
        for n, (source, target, rows, other) in enumerate(
            (
                (x_tokens_out, far_tokens, low, over_y),
                (y_tokens_out, far_tokens, high, over_x),
                (x_grads_out, far_grads, low, over_y),
                (y_grads_out, far_grads, high, over_x),
            )
        )
    ]

    @pl.when((block == 0) & (chunk == 0))
    def _():
        greet((over_x, over_y))
        for transfer in copies:
            transfer.start()

    parts = ((own_tokens, own_grads), (x_tokens, x_grads), (y_tokens, y_grads), (far_tokens, far_grads))
    for n, (tokens, grads) in enumerate(parts):

        @pl.when((block == n) & (chunk == 0))
        def _():
            if n == 3:
                for transfer in copies:
                    transfer.wait_recv()
            split_columns(all_tokens, tokens)
            split_columns(all_grads, grads)

    values = all_tokens[...]
    gate = both_halves(values, gate_own, gate_other)
    up = both_halves(values, up_own, up_other)
    sigmoid_gate = 1.0 / (1.0 + jnp.exp(-gate))
    silu = gate * sigmoid_gate
    hidden[...] = (silu * up).astype(jnp.bfloat16)
    gate_slope[...] = (up * sigmoid_gate * (1.0 + gate * (1.0 - sigmoid_gate))).astype(
        jnp.bfloat16
    )
    up_slope[...] = silu.astype(jnp.bfloat16)

    @pl.when((block == 3) & (chunk == pl.num_programs(1) - 1))
    def _():
        for transfer in copies:
            transfer.wait_send()


def gather_hidden(tokens, grads, weights):
    rows, width = tokens[0].shape
    _, hidden_count, half = weights[0].shape
    chunk = 512
    spec = pl.BlockSpec
    shape = jax.ShapeDtypeStruct
    outside = spec(memory_space=pl.ANY)
    whole = spec((rows, width), lambda b, c: (0, 0), pipeline_mode=pl.Buffered(1))
    bf16 = jnp.bfloat16
    return pl.pallas_call(
        hidden_kernel,
        grid=(4, hidden_count // chunk),
        in_specs=[outside] * 4 + [whole] * 6
        + [spec((None, chunk, half), lambda b, c, n=n: (n, c, 0)) for n in (0, 0, 1, 1)],
        out_specs=[spec((rows, width), lambda b, c: (b, 0))] * 2
        + [spec((rows, chunk), lambda b, c: (b, c))] * 3,
        out_shape=[shape((4 * rows, width), bf16)] * 2 + [shape((4 * rows, hidden_count), bf16)] * 3,
        scratch_shapes=[pltpu.VMEM((rows, width), bf16)] * 2
        + [pltpu.SemaphoreType.DMA((4,)), pltpu.SemaphoreType.DMA((4,))],
        compiler_params=pltpu.CompilerParams(
            collective_id=1, has_side_effects=True, vmem_limit_bytes=60 * 2**20
        ),
        cost_estimate=pl.CostEstimate(flops=1, bytes_accessed=1, transcendentals=0),
    )(*tokens[1:], *grads[1:], *tokens, *grads, *weights, *weights)


def reduce_copies(corner, send_x, send_y, got_corner, got_x, got_y, send, receive):
    _, over_x, over_y = neighbours()
    half = corner.shape[0] // 2
    low, high = pl.ds(0, half), pl.ds(half, half)
    plan = [
        (corner.at[low], got_corner.at[low], over_y),
        (corner.at[high], got_corner.at[high], over_x),
        (send_y.at[low], got_y.at[low], over_y),
        (send_y.at[high], got_y.at[high], over_y),
        (send_x.at[high], got_x.at[high], over_x),
        (send_x.at[low], got_x.at[low], over_x),
    ]
    return [
        pltpu.make_async_remote_copy(
            src_ref=source,
            dst_ref=target,
            send_sem=send.at[n],
            recv_sem=receive.at[n],
            device_id={"dp": other},
            device_id_type=MESH,
        )
        for n, (source, target, other) in enumerate(plan)
    ]


def corner_copies(corner, got_corner, send, receive, first):
    _, over_x, over_y = neighbours()
    half = corner.shape[0] // 2
    return [
        pltpu.make_async_remote_copy(
            src_ref=corner.at[rows],
            dst_ref=got_corner.at[rows],
            send_sem=send.at[first + n],
            recv_sem=receive.at[first + n],
            device_id={"dp": other},
            device_id_type=MESH,
        )
        for n, (rows, other) in enumerate(
            ((pl.ds(0, half), over_y), (pl.ds(half, half), over_x))
        )
    ]


def add_into(target, rows, other):
    total_rows = target[rows, :].astype(jnp.float32) + other[rows, :].astype(jnp.float32)
    target[rows, :] = total_rows.astype(target.dtype)


def feed_back_kernel(
    grads, hidden, gate_slope, up_slope,
    gate_own, gate_other, up_own, up_other, down_own, down_other,
    gate_grad, up_grad, out_own, out_x, out_y, two_grad,
    out_sum, two_sum, out_corner, keep_x, keep_y, got_out, local, corner, send_x, send_y, got_corner, got_x, got_y, send, receive,
):
    turn_index, chunk = pl.program_id(0), pl.program_id(1)
    last = chunk == pl.num_programs(1) - 1
    rows = grads.shape[0]
    low, high = slice(0, rows // 2), slice(rows // 2, rows)
    copies = reduce_copies(corner, send_x, send_y, got_corner, got_x, got_y, send, receive)
    copies += corner_copies(out_corner, got_out, send, receive, len(copies))
    writes = [
        pltpu.make_async_copy(source, target, local.at[n])
        for n, (source, target) in enumerate(
            ((keep_y, out_y), (keep_x, out_x), (out_corner, out_own))
        )
    ]

    @pl.when((turn_index == 0) & (chunk == 0))
    def _():
        _, over_x, over_y = neighbours()
        greet((over_x, over_y))

    @pl.when(chunk == 0)
    def _():
        out_sum[...] = jnp.zeros_like(out_sum)
        two_sum[...] = jnp.zeros_like(two_sum)

    hidden_grad = both_halves(grads[...], down_own, down_other)
    gate_back = (hidden_grad * gate_slope[...].astype(jnp.float32)).astype(jnp.bfloat16)
    up_back = (hidden_grad * up_slope[...].astype(jnp.float32)).astype(jnp.bfloat16)
    gate_grad[...] = gate_back
    up_grad[...] = up_back
    active = hidden[...]
    half = down_own.shape[1]
    for n, (gate, up, down) in enumerate(
        ((gate_own, up_own, down_own), (gate_other, up_other, down_other))
    ):
        for part in range(0, half, 512):
            cols = slice(part, part + 512)
            place = slice(n * half + part, n * half + part + 512)
            out_sum[:, place] += matmul(active, down[:, cols])
            two_sum[:, place] += matmul(gate_back, gate[:, cols]) + matmul(up_back, up[:, cols])

    @pl.when(last & (turn_index == 0))
    def _():
        merge_columns(corner, two_sum)
        copies[0].start()
        copies[1].start()
        merge_columns(out_corner, out_sum)
        copies[6].start()
        copies[7].start()

    @pl.when(last & (turn_index == 1))
    def _():
        merge_columns(send_y, two_sum)
        copies[2].start()
        merge_columns(keep_y, out_sum)

    @pl.when((chunk == 0) & (turn_index == 2))
    def _():
        copies[1].wait_recv()
        add_into(send_y, high, got_corner)
        copies[3].start()

    @pl.when(last & (turn_index == 2))
    def _():
        merge_columns(send_x, two_sum)
        copies[4].start()
        copies[0].wait_recv()
        add_into(send_x, low, got_corner)
        copies[5].start()
        merge_columns(keep_x, out_sum)
        copies[7].wait_recv()
        add_into(keep_y, high, got_out)
        writes[0].start()

    @pl.when(last & (turn_index == 3))
    def _():
        copies[6].wait_recv()
        add_into(keep_x, low, got_out)
        writes[1].start()
        copies[6].wait_send()
        copies[7].wait_send()
        merge_columns(out_corner, out_sum)
        writes[2].start()
        merge_columns(two_grad, two_sum)
        copies[2].wait_recv()
        copies[3].wait_recv()
        two_grad[...] += got_y[...].astype(jnp.float32)
        copies[4].wait_recv()
        copies[5].wait_recv()
        two_grad[...] += got_x[...].astype(jnp.float32)
        for transfer in copies[:6]:
            transfer.wait_send()
        for write in writes:
            write.wait()


def feed_back(grads, saved, weights, down):
    rows, width = grads.shape[0] // 4, grads.shape[1]
    _, hidden_count, half = weights[0].shape
    chunk = 512
    spec = pl.BlockSpec
    shape = jax.ShapeDtypeStruct
    bf16, f32 = jnp.bfloat16, jnp.float32
    block = lambda q, c: (3 - q, 0)
    piece = lambda q, c: (3 - q, c)
    return pl.pallas_call(
        feed_back_kernel,
        grid=(4, hidden_count // chunk),
        in_specs=[spec((rows, width), block)]
        + [spec((rows, chunk), piece)] * 3
        + [spec((None, chunk, half), lambda q, c, n=n: (n, c, 0)) for n in (0, 0, 1, 1)]
        + [spec((chunk, half), lambda q, c: (c, 0))] * 2,
        out_specs=[spec((rows, chunk), piece)] * 2
        + [spec(memory_space=pl.ANY)] * 3
        + [spec((rows, width), lambda q, c: (0, 0))],
        out_shape=[shape((4 * rows, hidden_count), bf16)] * 2
        + [shape((rows, width), bf16)] * 3
        + [shape((rows, width), f32)],
        scratch_shapes=[pltpu.VMEM((rows, width), f32)] * 2
        + [pltpu.VMEM((rows, width), bf16)] * 4
        + [pltpu.SemaphoreType.DMA((3,))]
        + [pltpu.VMEM((rows, width), bf16)] * 6
        + [pltpu.SemaphoreType.DMA((8,)), pltpu.SemaphoreType.DMA((8,))],
        compiler_params=pltpu.CompilerParams(
            collective_id=2, has_side_effects=True, vmem_limit_bytes=62 * 2**20
        ),
        cost_estimate=pl.CostEstimate(flops=1, bytes_accessed=1, transcendentals=0),
    )(grads, *saved, *weights, *weights, *down)


def is_crossing():
    return (lax.axis_index("dp") + lax.axis_index("mp")) % 2 == 1


def crossing_partner():
    me, z = lax.axis_index("dp"), lax.axis_index("mp")
    return {"dp": me + 1 - 2 * (me % 2), "mp": z + 1 - 2 * (z % 2)}


def crossing_copy(source, target, send, receive):
    return pltpu.make_async_remote_copy(
        src_ref=source,
        dst_ref=target,
        send_sem=send.at[0],
        recv_sem=receive.at[0],
        device_id=crossing_partner(),
        device_id_type=MESH,
    )


def core_copy(source, target, send, receive, n, chunk):
    me = lax.axis_index("dp")
    rows = pl.ds(n * chunk, chunk)
    return pltpu.make_async_remote_copy(
        src_ref=source.at[rows],
        dst_ref=target.at[rows],
        send_sem=send.at[n],
        recv_sem=receive.at[n],
        device_id={"dp": me + 1 - 2 * (me % 2)},
        device_id_type=MESH,
    )


def outer_kernel(extra, more, left_own, left_other, right_own, right_other, *refs):
    weights = refs[:extra]
    if extra:
        layer, total_out, *spread, layer_out = refs[extra : extra + 5]
        cross = crossing_copy(layer, layer_out, refs[-3], refs[-2])
        stay = pltpu.make_async_copy(layer, layer_out, refs[-1].at[0])
        crossing = is_crossing()
        refs = refs[:-3]
    elif more:
        product_left, product_right, total_out, product_out = refs[:4]
        product_own, product_send, product_got, product_sent, product_came = refs[-5:]
        refs = refs[:-5]
        chunk = product_left.shape[1]
        exchanges = [
            core_copy(product_send, product_got, product_sent, product_came, n, chunk)
            for n in range(more)
        ]
    else:
        total_out = refs[0]
    own, corner, send_x, send_y, got_corner, got_x, got_y, send, receive = refs[-9:]
    step = pl.program_id(0)
    half = own.shape[0] // 2
    low, high = slice(0, half), slice(half, 2 * half)
    copies = reduce_copies(corner, send_x, send_y, got_corner, got_x, got_y, send, receive)

    if not extra:

        @pl.when(step == 0)
        def _():
            me, over_x, over_y = neighbours()
            greet((over_x, over_y) + ((me + 1 - 2 * (me % 2),) if more else ()))

    else:

        @pl.when((step == 0) & crossing)
        def _():
            _, over_x, over_y = neighbours()
            partner = crossing_partner()
            barrier = pltpu.get_barrier_semaphore()
            for other in (over_x, over_y):
                pl.semaphore_signal(barrier, inc=1, device_id={"dp": other}, device_id_type=MESH)
            pl.semaphore_signal(barrier, inc=1, device_id=partner, device_id_type=MESH)
            pl.semaphore_wait(barrier, 3)
            cross.start()

        @pl.when((step == 0) & jnp.logical_not(crossing))
        def _():
            _, over_x, over_y = neighbours()
            greet((over_x, over_y))
            stay.start()

    @pl.when(step < 8)
    def _():
        result = dot_first(left_own[...], right_own[...]) + dot_first(
            left_other[...], right_other[...]
        )
        order = (corner, corner, send_y, send_y, send_x, send_x, own, own)
        starts = (0, 1, 2, None, None, 4, None, None)
        for n, (target, first) in enumerate(zip(order, starts)):

            @pl.when(step == n)
            def _():
                target[high if n % 2 else low, :] = result.astype(target.dtype)
                if first is not None:
                    copies[first].start()

    for n, weight in enumerate(weights):

        @pl.when(step == 8 + n)
        def _():
            me = lax.axis_index("dp")
            x, y = (me // 2) % 2, me // 4
            k = min(n, 3)
            far_x = 1 - x if k % 2 else x
            far_y = 1 - y if k // 2 else y
            part = 512
            start = (2 * far_y + far_x) * part + (part // 2 if n == 4 else 0)
            cols = pl.ds(pl.multiple_of(start, 256), weight.shape[0])
            spread[0][:, cols] = dot_last(right_own[...], weight[...])
            spread[1][:, cols] = dot_last(right_other[...], weight[...]).astype(jnp.bfloat16)

    if more:

        @pl.when(step >= 8)
        def _():
            product = dot_first(product_left[...], product_right[...])
            middle = product_own.shape[1]
            for n in range(more):

                @pl.when(step == 8 + n)
                def _():
                    rows = slice(n * chunk, (n + 1) * chunk)
                    product_own[rows, :] = product[:, :middle]
                    product_send[rows, :] = product[:, middle:].astype(jnp.bfloat16)
                    exchanges[n].start()

    last = pl.num_programs(0) - 1

    @pl.when(step == min(9, 7 + extra + more))
    def _():
        copies[1].wait_recv()
        add_into(send_y, high, got_corner)
        copies[3].start()
        copies[0].wait_recv()
        add_into(send_x, low, got_corner)
        copies[5].start()

    @pl.when(step == last)
    def _():
        for n in (2, 4, 3, 5):
            copies[n].wait_recv()
        total_out[...] = (
            own[...] + got_x[...].astype(jnp.float32) + got_y[...].astype(jnp.float32)
        ).astype(total_out.dtype)
        for transfer in copies:
            transfer.wait_send()

    if more:

        @pl.when(step == last)
        def _():
            for transfer in exchanges:
                transfer.wait()
            product_out[...] = (
                product_own[...] + product_got[...].astype(jnp.float32)
            ).astype(jnp.bfloat16)

    if extra:

        @pl.when((step == last) & crossing)
        def _():
            cross.wait()

        @pl.when((step == last) & jnp.logical_not(crossing))
        def _():
            stay.wait()


def outer(lefts, rights, by_left, collective_id, weights=(), layer=None, product=None):
    rows = 512
    wide = lefts[0][0].shape[1]
    right_wide = rights[0][0].shape[1]
    turn_of = lambda s: 6 - 2 * (jnp.minimum(s, 7) // 2) + jnp.minimum(s, 7) % 2
    if by_left:
        size = (wide // 8, right_wide)
        left_size = (rows, wide // 8)
        place_left = lambda row: lambda s: (row, turn_of(s))
        place_right = lambda row: lambda s: (row, 0)
    else:
        size = (wide // 2, right_wide // 4)
        left_size = (rows, wide // 2)
        place_left = lambda row: lambda s: (row, jnp.minimum(s, 7) % 2)
        place_right = lambda row: lambda s: (row, 3 - jnp.minimum(s, 7) // 2)
    both = (2 * size[0], size[1])
    spec, shape = pl.BlockSpec, jax.ShapeDtypeStruct
    out_specs = [spec(both, lambda s: (0, 0))]
    out_shape = [shape(both, jnp.bfloat16)]
    if weights:
        out_specs += [spec((rows, wide), lambda s: (0, 0))] * 2
        out_shape += [shape((rows, wide), jnp.float32), shape((rows, wide), jnp.bfloat16)]
        out_specs += [spec(memory_space=pl.ANY)]
        out_shape += [shape(layer.shape, layer.dtype)]
    more, product_specs = 0, []
    if product:
        chunk = 256
        tokens, hidden_count = product[0].shape
        more = hidden_count // chunk
        turn = lambda s: jnp.maximum(s - 8, 0)
        product_specs = [
            spec((tokens, chunk), lambda s: (0, turn(s))),
            spec(product[1].shape, lambda s: (0, 0), pipeline_mode=pl.Buffered(1)),
        ]
        half = product[1].shape[1] // 2
        out_specs += [spec((hidden_count, half), lambda s: (0, 0))]
        out_shape += [shape((hidden_count, half), jnp.bfloat16)]
    made = pl.pallas_call(
        functools.partial(outer_kernel, len(weights), more),
        grid=(8 + len(weights) + more,),
        in_specs=[spec(left_size, place_left(row)) for _, row in lefts]
        + [spec((rows, size[1]), place_right(row)) for _, row in rights]
        + [
            spec(weight.shape, lambda s: (0, 0), pipeline_mode=pl.Buffered(1))
            for weight in weights
        ]
        + ([spec(memory_space=pl.ANY)] if weights else [])
        + product_specs,
        out_specs=out_specs,
        out_shape=out_shape,
        scratch_shapes=[pltpu.VMEM(both, jnp.float32)]
        + [pltpu.VMEM(both, jnp.bfloat16)] * 6
        + [pltpu.SemaphoreType.DMA((6,)), pltpu.SemaphoreType.DMA((6,))]
        + ([pltpu.SemaphoreType.DMA((1,))] * 3 if weights else [])
        + (
            [
                pltpu.VMEM((hidden_count, half), jnp.float32),
                pltpu.VMEM((hidden_count, half), jnp.bfloat16),
                pltpu.VMEM((hidden_count, half), jnp.bfloat16),
                pltpu.SemaphoreType.DMA((more,)),
                pltpu.SemaphoreType.DMA((more,)),
            ]
            if product
            else []
        ),
        compiler_params=pltpu.CompilerParams(
            collective_id=collective_id, has_side_effects=True, vmem_limit_bytes=60 * 2**20
        ),
        cost_estimate=pl.CostEstimate(flops=1, bytes_accessed=1, transcendentals=0),
    )(*[array for array, _ in (*lefts, *rights)], *weights, *([layer] if weights else []), *(product or []))
    return made


def columns_kernel(transposed, place, left, w0, w1, w2, w3_low, w3_high, own, other):
    rows = own.shape[0]

    def write(lines, result):
        for ref, kind in ((own, jnp.float32), (other, jnp.bfloat16)):
            start = 0 if ref is own else rows
            ref[...] = result(lines[start : start + rows]).astype(kind)

    for k, weight in enumerate((w0, w1, w2)):

        @pl.when(pl.program_id(0) == k)
        def _():
            step = dot_last if transposed else matmul
            write(left, lambda lines: step(lines, weight[...]))

    @pl.when(pl.program_id(0) == 3)
    def _():
        if transposed:
            write(
                left,
                lambda lines: jnp.concatenate(
                    [dot_last(lines, w3_low[...]), dot_last(lines, w3_high[...])], 1
                ),
            )
        else:
            middle = w3_low.shape[0]
            write(
                left,
                lambda lines: matmul(lines[:, :middle], w3_low[...])
                + matmul(lines[:, middle:], w3_high[...]),
            )


def columns(place, left, weights, transposed):
    length, depth = left.shape
    rows = length // 2
    part = weights[0].shape[0 if transposed else 1]
    width = 4 * part
    whole = lambda array: pl.BlockSpec(array.shape, lambda k, place: (0, 0))
    block = pl.BlockSpec((rows, part), lambda k, place: (0, k ^ place[0]))
    shape = jax.ShapeDtypeStruct
    return pl.pallas_call(
        functools.partial(columns_kernel, transposed),
        grid_spec=pltpu.PrefetchScalarGridSpec(
            num_scalar_prefetch=1,
            grid=(4,),
            in_specs=[whole(array) for array in (left, *weights)],
            out_specs=[block, block],
        ),
        out_shape=[shape((rows, width), jnp.float32), shape((rows, width), jnp.bfloat16)],
        compiler_params=pltpu.CompilerParams(vmem_limit_bytes=56 * 2**20),
        cost_estimate=pl.CostEstimate(flops=1, bytes_accessed=1, transcendentals=0),
    )(place, left, *weights)


def tile_call(kernel, place, ins, outs, kept):
    width = 2048
    tile = 256

    def spec(cut, columns):
        if cut == "rows":
            return pl.BlockSpec((tile, columns), lambda t, place: (t, 0))
        if cut == "low" or cut == "high":
            return pl.BlockSpec((tile, columns), lambda t, place: (0, 0))
        return pl.BlockSpec((cut, columns), lambda t, place: (0, 0))

    return pl.pallas_call(
        kernel,
        grid_spec=pltpu.PrefetchScalarGridSpec(
            num_scalar_prefetch=1,
            grid=(2,),
            in_specs=[spec(cut, array.shape[1]) for array, cut in ins],
            out_specs=[spec(cut, shape.shape[1]) for shape, cut in outs],
        ),
        out_shape=[shape for shape, _ in outs],
        compiler_params=pltpu.CompilerParams(vmem_limit_bytes=56 * 2**20),
        cost_estimate=pl.CostEstimate(flops=1, bytes_accessed=1, transcendentals=0),
    )(place, *[array for array, _ in ins])


def choose(low_ref, high_ref):
    return jnp.where(pl.program_id(0) == 0, low_ref[...], high_ref[...]).astype(jnp.float32)


def add_gain(gain_ref, values):
    @pl.when(pl.program_id(0) == 0)
    def _():
        gain_ref[...] = jnp.zeros_like(gain_ref)

    gain_ref[...] += jnp.sum(values.reshape(-1, 8, values.shape[1]), 0)


def relabelled(ref, values, place):
    width = values.shape[1] // 4
    for k in range(4):
        start = pl.multiple_of((place[0] ^ k) * width, width)
        ref[:, pl.ds(start, width)] = values[:, k * width : (k + 1) * width]


def first_norm_kernel(place, inputs, gain, normed):
    values, _ = norm_rows(inputs[...].astype(jnp.float32), gain[...])
    relabelled(normed, values.astype(jnp.bfloat16), place)


def middle_kernel(place, inputs, own, other, gain, middle, normed):
    values = inputs[...].astype(jnp.float32) + own[...] + other[...].astype(jnp.float32)
    middle[...] = values
    normed[...] = norm_rows(values, gain[...])[0].astype(jnp.bfloat16)


def middle_back_kernel(
    place, middle, cotangent, two, gain, middle_grad, branch, gain_grad
):
    two_grad = two[...]
    values = middle[...]
    _, factor = norm_rows(values, gain[...])
    add_gain(gain_grad, two_grad * values * factor)
    grads = cotangent[...].astype(jnp.float32) + norm_back(values, factor, gain[...], two_grad)
    middle_grad[...] = grads
    relabelled(branch, grads.astype(jnp.bfloat16), place)


def input_back_kernel(
    place, inputs, middle_grad, own, other, gain, input_grad, rounded, gain_grad
):
    one_grad = own[...] + other[...].astype(jnp.float32)
    values = inputs[...].astype(jnp.float32)
    _, factor = norm_rows(values, gain[...])
    add_gain(gain_grad, one_grad * values * factor)
    grads = middle_grad[...] + norm_back(values, factor, gain[...], one_grad)
    input_grad[...] = grads
    rounded[...] = grads.astype(jnp.bfloat16)


def output_kernel(place, middle, own, over_x, over_y, output):
    parts = [part[...].astype(jnp.float32) for part in (own, over_x, over_y)]
    output[...] = (middle[...] + parts[0] + parts[1] + parts[2]).astype(jnp.bfloat16)


def exchange(values, bit):
    return lax.ppermute(values, "dp", [(i, i ^ bit) for i in range(8)])


def swap_halves(values):
    pairs = []
    for i in range(8):
        for m in range(4):
            if (i & 1) != (m & 1):
                pairs.append((i * 4 + m, (i ^ 1) * 4 + (m ^ 1)))
    return lax.ppermute(values, ("dp", "mp"), pairs)


def after(values, earlier):
    return lax.optimization_barrier((values, earlier))[0]


def gather_near(block):
    return [exchange(block, 2), exchange(block, 4)]


def gather_far(near):
    half = near[0].shape[0] // 2
    return [exchange(near[0][:half], 4), exchange(near[1][half:], 2)]


def add_low(left, right):
    return (left.astype(jnp.float32) + right.astype(jnp.float32)).astype(jnp.bfloat16)


def pick(values, index, width, axis):
    return lax.dynamic_slice_in_dim(values, index * width, width, axis)


def in_order(own, other, core, axis=0):
    return jnp.where(
        core == 0,
        jnp.concatenate([own, other], axis),
        jnp.concatenate([other, own], axis),
    )


def total_plane(values):
    for bit in (1, 2, 4):
        values = values + exchange(values, bit)
    return values


def total_z(values):
    others = [lax.ppermute(values, "mp", [(i, i ^ bit) for i in range(4)]) for bit in (1, 2, 3)]
    return (values + others[0]) + (others[1] + others[2])


def fast(
    layer_input,
    out_grad,
    norm_attn,
    query_norm,
    key_norm,
    w_query,
    key_matrix,
    value_matrix,
    w_output,
    norm_mlp,
    w_gate,
    w_up,
    w_down,
):
    bf16, f32 = jnp.bfloat16, jnp.float32
    device = lax.axis_index("dp")
    core = device & 1
    place = jnp.reshape(device >> 1, (1,)).astype(jnp.int32)
    core_index = jnp.reshape(core, (1,)).astype(jnp.int32)
    crossing = core != (lax.axis_index("mp") & 1)
    planes = 4
    rows = layer_input.shape[0]
    width = layer_input.shape[1]
    units = w_gate.shape[1] // planes
    array = jax.ShapeDtypeStruct

    query_cols = w_query.shape[1] // 2
    key_cols = key_matrix.shape[1] // 2

    def heads_of(which):
        return jnp.concatenate(
            [
                pick(w_query, which, query_cols, 1),
                pick(key_matrix, which, key_cols, 1),
                pick(value_matrix, which, key_cols, 1),
            ],
            1,
        )

    qkv_pair = in_order(heads_of(core), exchange(heads_of(1 - core), 1), core)
    out_rows = w_output.shape[0] // 2
    out_pair = in_order(
        pick(w_output, core, out_rows, 0),
        exchange(pick(w_output, 1 - core, out_rows, 0), 1),
        core,
        1,
    )
    qkv_z = lax.all_gather(qkv_pair, "mp", axis=1, tiled=True)
    pieces = jnp.concatenate(
        [w.reshape(planes, units, w.shape[1]) for w in (w_gate.T, w_up.T, w_down)], 1
    )

    def piece_for(k):
        return pick(pieces, place[0] ^ k, 1, 0)[0]

    feed_own = jnp.concatenate(
        [piece_for(0)] + [exchange(piece_for(k), 2 * k) for k in (1, 2, 3)], 1
    )

    gate_up_own, down_part = feed_own[: 2 * units], feed_own[2 * units :]
    qkv_z = after(qkv_z, (gate_up_own, down_part))
    qkv_near = gather_near(qkv_z)
    moved = swap_halves(after(layer_input, qkv_z))
    moved_grad = swap_halves(after(out_grad, qkv_z))
    out_z = lax.all_gather(
        after(out_pair, (moved, moved_grad, qkv_near)), "mp", axis=0, tiled=True
    )

    inputs = jnp.where(crossing, moved, layer_input)
    cotangent = jnp.where(crossing, moved_grad, out_grad)

    gain_one, gain_two = norm_attn[None, :], norm_mlp[None, :]
    gain_query, gain_key = query_norm[None, :], key_norm[None, :]
    (normed,) = tile_call(
        first_norm_kernel,
        place,
        [(inputs, "rows"), (gain_one, 1)],
        [(array((rows, width), bf16), "rows")],
        4,
    )
    cosines, sines = wide_tables(2 * rows)
    qkv_chips = [
        qkv_z,
        *qkv_near,
        *gather_far(after(qkv_near, (normed, cosines, sines, cotangent))),
    ]
    out_near = gather_near(after(out_z, qkv_chips))
    gate_up_own, down_part = after((gate_up_own, down_part), (out_z, qkv_chips))
    gate_up_half = lax.all_gather(
        gate_up_own.reshape(2, units, width // 2), "mp", axis=1, tiled=True
    )
    down_half = lax.all_gather(down_part, "mp", axis=0, tiled=True)
    normed_other = after(exchange(normed, 1), out_z)
    proj, query_rot, key_rot, value_low, attended, log_total = attend(
        core_index,
        normed,
        normed_other,
        qkv_chips,
        cosines,
        sines,
        gain_query,
        gain_key,
        planes,
        query_cols,
    )
    out_near = after(out_near, attended)
    out_chips = [out_z, *out_near, *gather_far(out_near)]
    grads_near = gather_near(after(cotangent, qkv_chips))
    branch_own, branch_other = columns(place, attended, out_chips, False)
    middle, tokens = tile_call(
        middle_kernel,
        place,
        [(inputs, "rows"), (branch_own, "rows"), (after(exchange(branch_other, 1), grads_near), "rows"), (gain_two, 1)],
        [
            (array((rows, width), f32), "rows"),
            (array((rows, width), bf16), "rows"),
        ],
        14,
    )

    tokens_near = gather_near(tokens)
    gate_up_w = [gate_up_half, exchange(after(gate_up_half, tokens), 1)]
    all_tokens, all_grads, all_hidden, gate_slope, up_slope = gather_hidden(
        [tokens, *tokens_near], [cotangent, *grads_near], gate_up_w
    )
    down_half = after(down_half, all_hidden)
    down_w = [down_half, exchange(down_half, 1)]

    def over_z(grad):
        return lax.psum_scatter(grad, "mp", scatter_dimension=0, tiled=True)

    half = width // 2
    down_other = dot_first(all_hidden, all_grads[:, half:]).astype(bf16)
    all_gate, all_up, out_own, out_x, out_y, two_grad = feed_back(
        after(all_grads, down_other),
        [all_hidden, gate_slope, up_slope],
        gate_up_w,
        down_w,
    )
    gate_other = dot_first(all_gate, all_tokens[:, half:]).astype(bf16)

    def own_half(left, right, other):
        own = dot_first(left, right[:, :half])
        return (own + exchange(other, 1).astype(f32)).astype(bf16)

    down_local = own_half(after(all_hidden, two_grad), all_grads, down_other)
    down_sum = over_z(down_local)
    gate_local = own_half(all_gate, all_tokens, gate_other)
    gate_sum = over_z(gate_local)
    middle_grad, branch, gain_two_part = tile_call(
        middle_back_kernel,
        place,
        [(middle, "rows"), (cotangent, "rows"), (two_grad, "rows"), (gain_two, 1)],
        [
            (array((rows, width), f32), "rows"),
            (array((rows, width), bf16), "rows"),
            (array((8, width), f32), 8),
        ],
        18,
    )

    def unspread(own):
        cols = own.shape[1] // planes
        got = [own[:, :cols]] + [
            exchange(own[:, k * cols : (k + 1) * cols], 2 * k) for k in (1, 2, 3)
        ]
        return jnp.concatenate(got, 1), cols

    def chips_in_order(got, cols, rows):
        return jnp.concatenate([pick(got[rows], place[0] ^ k, cols, 1) for k in range(planes)], 0)

    down_got, cols = unspread(down_sum)
    down_own = chips_in_order(down_got, cols, slice(0, units)).astype(f32)

    branch_pair = after(exchange(branch, 1), (gate_local, down_local))
    out_local, up_local = outer(
        [(attended, 0), (attended, 1)],
        [(branch, 0), (branch_pair, 0)],
        False,
        4,
        product=(all_up, all_tokens),
    )
    up_sum = over_z(up_local)
    out_sum = over_z(out_local)
    branch_pair, out_x, out_y = after((branch_pair, out_x, out_y), out_local)
    out_parts = [out_own, exchange(out_x, 2), exchange(out_y, 4)]
    proj_grad, head_gains = attend_back(
        core_index,
        branch,
        branch_pair,
        out_chips,
        cosines,
        sines,
        gain_query,
        gain_key,
        (proj, query_rot, key_rot, value_low, log_total),
        planes,
        query_cols,
    )

    out_parts = after(out_parts, proj_grad)
    (layer_output,) = tile_call(
        output_kernel,
        place,
        [(middle, "rows")] + [(part, "rows") for part in out_parts],
        [(array((rows, width), bf16), "rows")],
        12,
    )
    proj_grad = after(proj_grad, (down_sum, gate_sum, out_local))
    qkv_local, one_own, one_other, output_moved = outer(
        [(normed, 0), (normed_other, 0)],
        [(proj_grad, 0), (proj_grad, 1)],
        True,
        3,
        qkv_chips,
        layer_output,
    )
    qkv_local = after(qkv_local, (up_sum, out_sum))
    qkv_sum = lax.psum_scatter(qkv_local, "mp", scatter_dimension=1, tiled=True)
    input_grad, rounded_grad, gain_one_part = tile_call(
        input_back_kernel,
        place,
        [
            (inputs, "rows"),
            (middle_grad, "rows"),
            (one_own, "rows"),
            (exchange(one_other, 1), "rows"),
            (gain_one, 1),
        ],
        [
            (array((rows, width), f32), "rows"),
            (array((rows, width), bf16), "rows"),
            (array((8, width), f32), 8),
        ],
        18,
    )
    gate_up_got, cols = unspread(
        after(jnp.concatenate([gate_sum, up_sum], 0), rounded_grad)
    )
    gate_own = chips_in_order(gate_up_got, cols, slice(0, units)).T.astype(f32)
    up_own = chips_in_order(gate_up_got, cols, slice(units, 2 * units)).T.astype(f32)
    gain_sums = total_plane(
        after(jnp.concatenate(
            [
                jnp.sum(gain_one_part, 0),
                jnp.sum(head_gains[:8], 0),
                jnp.sum(head_gains[8:], 0),
                jnp.sum(gain_two_part, 0),
            ]
        ), qkv_local)
    )
    grad_moved = swap_halves(rounded_grad)
    gain_sums = total_z(after(gain_sums, (gate_own, up_own, grad_moved)))
    pair_rows = qkv_sum.shape[0] // 2
    qkv_other = exchange(pick(qkv_sum, 1 - core, pair_rows, 0), 1)
    qkv_own = pick(qkv_sum, core, pair_rows, 0)

    def both(start, stop):
        return in_order(qkv_own[:, start:stop], qkv_other[:, start:stop], core, 1).astype(f32)

    pair_cols = out_sum.shape[1] // 2
    out_other = exchange(pick(out_sum, 1 - core, pair_cols, 1), 1)
    out_own = pick(out_sum, core, pair_cols, 1)
    return (
        output_moved,
        jnp.where(crossing, grad_moved.astype(f32), input_grad),
        gain_sums[:width],
        gain_sums[width : width + HEAD_SIZE],
        gain_sums[width + HEAD_SIZE : width + 2 * HEAD_SIZE],
        both(0, query_cols),
        both(query_cols, query_cols + key_cols),
        both(query_cols + key_cols, query_cols + 2 * key_cols),
        in_order(out_own, out_other, core, 0).astype(f32),
        gain_sums[width + 2 * HEAD_SIZE :],
        gate_own,
        up_own,
        down_own,
    )


def solution(mesh):
    in_specs = (
        P(("dp", "mp"), None),
        P(("dp", "mp"), None),
        P(),
        P(),
        P(),
        P("dp", "mp"),
        P("dp", "mp"),
        P("dp", "mp"),
        P("mp", "dp"),
        P(),
        P("dp", "mp"),
        P("dp", "mp"),
        P("mp", "dp"),
    )
    out_specs = (
        P(("dp", "mp"), None),
        P(("dp", "mp"), None),
        P(),
        P(),
        P(),
        P("dp", "mp"),
        P("dp", "mp"),
        P("dp", "mp"),
        P("mp", "dp"),
        P(),
        P("dp", "mp"),
        P("dp", "mp"),
        P("mp", "dp"),
    )
    whole_sequences = dict(mesh.shape) == {"dp": 8, "mp": 4}
    local = fast if whole_sequences else generic
    return jax.shard_map(local, mesh=mesh, in_specs=in_specs, out_specs=out_specs, check_vma=False)
```

```python
import functools

import jax
import jax.numpy as jnp
from jax import lax
from jax.experimental import pallas as pl
from jax.experimental.pallas import tpu as pltpu
from jax.sharding import PartitionSpec as P

HEAD_SIZE = 128
SEQUENCE_LENGTH = 1024


EPSILON = 1e-06
THETA = 1000000.0


def norm_rows(values, gain):
    factor = lax.rsqrt(jnp.mean(values * values, -1, keepdims=True) + EPSILON)
    return (values * factor * gain, factor)


def norm_back(values, factor, gain, upstream):
    scaled = upstream * gain
    inner = jnp.mean(scaled * values, -1, keepdims=True)
    return factor * scaled - values * (factor * factor * factor) * inner


def tables(length, width):
    half_width = width // 2
    frequencies = THETA ** (-(jnp.arange(half_width, dtype=jnp.float32) * 2.0 / width))
    angles = jnp.arange(length, dtype=jnp.float32)[:, None] * frequencies[None, :]
    return (jnp.cos(angles), jnp.sin(angles))


def rotate(values, cosine_table, sine_table):
    half_width = values.shape[-1] // 2
    first_half = values[..., :half_width]
    second_half = values[..., half_width:]
    cosine_part = cosine_table[:, None, :]
    sine_part = sine_table[:, None, :]
    return jnp.concatenate(
        [
            first_half * cosine_part - second_half * sine_part,
            second_half * cosine_part + first_half * sine_part,
        ],
        -1,
    )


def rotate_back(grads, cosine_table, sine_table):
    half_width = grads.shape[-1] // 2
    first_half = grads[..., :half_width]
    second_half = grads[..., half_width:]
    cosine_part = cosine_table[:, None, :]
    sine_part = sine_table[:, None, :]
    return jnp.concatenate(
        [
            first_half * cosine_part + second_half * sine_part,
            second_half * cosine_part - first_half * sine_part,
        ],
        -1,
    )


def matmul(left, right):
    return jnp.dot(left, right, preferred_element_type=jnp.float32)


def dot_last(left, right):
    return lax.dot_general(
        left, right, (((1,), (1,)), ((), ())), preferred_element_type=jnp.float32
    )


def dot_first(left, right):
    return lax.dot_general(
        left, right, (((0,), (0,)), ((), ())), preferred_element_type=jnp.float32
    )


def masked_scores(query_block, keys, start, block_rows, scale):
    raw = (
        jnp.einsum("qhgd,khd->hgqk", query_block, keys, preferred_element_type=jnp.float32) * scale
    )
    query_places = start + jnp.arange(block_rows)[:, None]
    key_places = jnp.arange(keys.shape[0])[None, :]
    return jnp.where(key_places <= query_places, raw, -jnp.inf)


def generic(
    layer_input,
    out_grad,
    norm_attn,
    query_norm,
    key_norm,
    w_query,
    key_matrix,
    value_matrix,
    w_output,
    norm_mlp,
    w_gate,
    w_up,
    w_down,
):
    inputs = layer_input.astype(jnp.float32)
    query_full, key_full, value_full, output_full = (
        lax.all_gather(w_query, "dp", axis=0, tiled=True),
        lax.all_gather(key_matrix, "dp", axis=0, tiled=True),
        lax.all_gather(value_matrix, "dp", axis=0, tiled=True),
        lax.all_gather(w_output, "dp", axis=1, tiled=True),
    )
    first_normed, factor_one = norm_rows(inputs, norm_attn)
    normed_all = lax.all_gather(first_normed.astype(jnp.bfloat16), "mp", axis=0, tiled=True)
    total_rows = normed_all.shape[0]
    sequence_batch = total_rows // SEQUENCE_LENGTH
    query_heads = query_full.shape[1] // HEAD_SIZE
    shared_heads = key_full.shape[1] // HEAD_SIZE
    heads_per_group = query_heads // shared_heads
    query_proj = matmul(normed_all, query_full).reshape(
        sequence_batch, SEQUENCE_LENGTH, query_heads, HEAD_SIZE
    )
    key_projected = matmul(normed_all, key_full).reshape(
        sequence_batch, SEQUENCE_LENGTH, shared_heads, HEAD_SIZE
    )
    value_low = (
        matmul(normed_all, value_full)
        .astype(jnp.bfloat16)
        .reshape(sequence_batch, SEQUENCE_LENGTH, shared_heads, HEAD_SIZE)
    )
    cosine_table, sine_table = tables(SEQUENCE_LENGTH, HEAD_SIZE)
    query_normed, query_factor = norm_rows(query_proj, query_norm)
    query_rotated = rotate(query_normed, cosine_table, sine_table).astype(jnp.bfloat16)
    query_rotated = query_rotated.reshape(
        sequence_batch, SEQUENCE_LENGTH, shared_heads, heads_per_group, HEAD_SIZE
    )
    key_normed, key_factor = norm_rows(key_projected, key_norm)
    key_rot = rotate(key_normed, cosine_table, sine_table).astype(jnp.bfloat16)
    block_rows = min(512, SEQUENCE_LENGTH)
    block_count = SEQUENCE_LENGTH // block_rows
    scale = HEAD_SIZE ** (-0.5)
    attended_pieces = []
    log_totals = []
    for seq_index in range(sequence_batch):
        for block_index in range(block_count):
            start = block_index * block_rows
            query_block = query_rotated[seq_index, start : start + block_rows]
            scores = masked_scores(query_block, key_rot[seq_index], start, block_rows, scale)
            largest = jnp.max(scores, -1, keepdims=True)
            expanded = jnp.exp(scores - largest)
            summed = jnp.sum(expanded, -1, keepdims=True)
            probs_low = (expanded / summed).astype(jnp.bfloat16)
            block_out = jnp.einsum(
                "hgqk,khd->qhgd",
                probs_low,
                value_low[seq_index],
                preferred_element_type=jnp.float32,
            )
            attended_pieces.append(block_out.reshape(block_rows, query_heads * HEAD_SIZE))
            log_totals.append(largest + jnp.log(summed))
    attended = jnp.concatenate(attended_pieces, 0).astype(jnp.bfloat16)
    attn_sum = lax.psum_scatter(
        matmul(attended, output_full), "mp", scatter_dimension=0, tiled=True
    )
    middle = inputs + attn_sum
    gate_full, up_full, down_full = (
        lax.all_gather(w_gate, "dp", axis=0, tiled=True),
        lax.all_gather(w_up, "dp", axis=0, tiled=True),
        lax.all_gather(w_down, "dp", axis=1, tiled=True),
    )
    normed_two, factor_two = norm_rows(middle, norm_mlp)
    normed_two_all = lax.all_gather(normed_two.astype(jnp.bfloat16), "mp", axis=0, tiled=True)
    gate_value = matmul(normed_two_all, gate_full)
    up_value = matmul(normed_two_all, up_full)
    hidden_low = (jax.nn.silu(gate_value) * up_value).astype(jnp.bfloat16)
    mlp_sum = lax.psum_scatter(
        matmul(hidden_low, down_full).astype(jnp.bfloat16), "mp", scatter_dimension=0, tiled=True
    ).astype(jnp.float32)
    layer_output = (middle + mlp_sum).astype(jnp.bfloat16)
    grad_rows = lax.all_gather(out_grad, "mp", axis=0, tiled=True)
    gate_back, up_back, down_back = (
        lax.all_gather(w_gate, "dp", axis=0, tiled=True),
        lax.all_gather(w_up, "dp", axis=0, tiled=True),
        lax.all_gather(w_down, "dp", axis=1, tiled=True),
    )
    hidden_grad = dot_last(grad_rows, down_back)
    down_grad = dot_first(hidden_low, grad_rows)
    sigmoid_gate = jax.nn.sigmoid(gate_value)
    gate_grad = (
        hidden_grad * up_value * sigmoid_gate * (1.0 + gate_value * (1.0 - sigmoid_gate))
    ).astype(jnp.bfloat16)
    up_grad = (hidden_grad * gate_value * sigmoid_gate).astype(jnp.bfloat16)
    gate_weight_grad = dot_first(normed_two_all, gate_grad)
    up_weight_grad = dot_first(normed_two_all, up_grad)
    two_grad = lax.psum_scatter(
        dot_last(gate_grad, gate_back) + dot_last(up_grad, up_back),
        "mp",
        scatter_dimension=0,
        tiled=True,
    )
    gain_two_grad = jnp.sum(two_grad * middle * factor_two, 0)
    middle_grad = out_grad.astype(jnp.float32) + norm_back(middle, factor_two, norm_mlp, two_grad)
    mlp_grads = (
        lax.psum_scatter(
            gate_weight_grad.astype(jnp.bfloat16), "dp", scatter_dimension=0, tiled=True
        ).astype(jnp.float32),
        lax.psum_scatter(
            up_weight_grad.astype(jnp.bfloat16), "dp", scatter_dimension=0, tiled=True
        ).astype(jnp.float32),
        lax.psum_scatter(
            down_grad.astype(jnp.bfloat16), "dp", scatter_dimension=1, tiled=True
        ).astype(jnp.float32),
    )
    branch_all = lax.all_gather(middle_grad.astype(jnp.bfloat16), "mp", axis=0, tiled=True)
    output_weight_grad = dot_first(attended, branch_all)
    attended_grad = dot_last(branch_all, output_full).astype(jnp.bfloat16)
    attended_grad = attended_grad.reshape(
        sequence_batch, SEQUENCE_LENGTH, shared_heads, heads_per_group, HEAD_SIZE
    )
    query_grad_seqs = []
    key_grad_seqs = []
    value_grad_seqs = []
    for seq_index in range(sequence_batch):
        key_running = jnp.zeros((SEQUENCE_LENGTH, shared_heads, HEAD_SIZE), jnp.float32)
        value_running = jnp.zeros((SEQUENCE_LENGTH, shared_heads, HEAD_SIZE), jnp.float32)
        query_blocks = []
        for block_index in range(block_count):
            start = block_index * block_rows
            query_block = query_rotated[seq_index, start : start + block_rows]
            scores = masked_scores(query_block, key_rot[seq_index], start, block_rows, scale)
            probs_full = jnp.exp(scores - log_totals[seq_index * block_count + block_index])
            probs_low = probs_full.astype(jnp.bfloat16)
            grad_block = attended_grad[seq_index, start : start + block_rows]
            prob_grad = jnp.einsum(
                "qhgd,khd->hgqk",
                grad_block,
                value_low[seq_index],
                preferred_element_type=jnp.float32,
            )
            row_inner = jnp.sum(probs_full * prob_grad, -1, keepdims=True)
            score_grad = (probs_full * (prob_grad - row_inner)).astype(jnp.bfloat16)
            query_blocks.append(
                jnp.einsum(
                    "hgqk,khd->qhgd",
                    score_grad,
                    key_rot[seq_index],
                    preferred_element_type=jnp.float32,
                )
                * scale
            )
            key_running = (
                key_running
                + jnp.einsum(
                    "hgqk,qhgd->khd", score_grad, query_block, preferred_element_type=jnp.float32
                )
                * scale
            )
            value_running = value_running + jnp.einsum(
                "hgqk,qhgd->khd", probs_low, grad_block, preferred_element_type=jnp.float32
            )
        query_grad_seqs.append(jnp.concatenate(query_blocks, 0))
        key_grad_seqs.append(key_running)
        value_grad_seqs.append(value_running)
    rot_query_grad = jnp.stack(query_grad_seqs, 0).reshape(
        sequence_batch, SEQUENCE_LENGTH, query_heads, HEAD_SIZE
    )
    rot_key_grad = jnp.stack(key_grad_seqs, 0)
    value_grad = (
        jnp.stack(value_grad_seqs, 0)
        .reshape(total_rows, shared_heads * HEAD_SIZE)
        .astype(jnp.bfloat16)
    )
    query_normed_grad = rotate_back(rot_query_grad, cosine_table, sine_table)
    query_gain_grad = jnp.sum(query_normed_grad * query_proj * query_factor, (0, 1, 2))
    query_grad = norm_back(query_proj, query_factor, query_norm, query_normed_grad)
    query_grad = query_grad.reshape(total_rows, query_heads * HEAD_SIZE).astype(jnp.bfloat16)
    key_normed_grad = rotate_back(rot_key_grad, cosine_table, sine_table)
    key_gain_grad = jnp.sum(key_normed_grad * key_projected * key_factor, (0, 1, 2))
    key_grad = norm_back(key_projected, key_factor, key_norm, key_normed_grad)
    key_grad = key_grad.reshape(total_rows, shared_heads * HEAD_SIZE).astype(jnp.bfloat16)
    query_weight_grad = dot_first(normed_all, query_grad)
    key_weight_grad = dot_first(normed_all, key_grad)
    value_weight_grad = dot_first(normed_all, value_grad)
    one_partial = (
        dot_last(query_grad, query_full)
        + dot_last(key_grad, key_full)
        + dot_last(value_grad, value_full)
    )
    one_grad = lax.psum_scatter(
        one_partial.astype(jnp.bfloat16), "mp", scatter_dimension=0, tiled=True
    ).astype(jnp.float32)
    gain_one_grad = jnp.sum(one_grad * inputs * factor_one, 0)
    input_grad = middle_grad + norm_back(inputs, factor_one, norm_attn, one_grad)
    attn_grads = (
        lax.psum_scatter(
            query_weight_grad.astype(jnp.bfloat16), "dp", scatter_dimension=0, tiled=True
        ).astype(jnp.float32),
        lax.psum_scatter(
            key_weight_grad.astype(jnp.bfloat16), "dp", scatter_dimension=0, tiled=True
        ).astype(jnp.float32),
        lax.psum_scatter(
            value_weight_grad.astype(jnp.bfloat16), "dp", scatter_dimension=0, tiled=True
        ).astype(jnp.float32),
        lax.psum_scatter(
            output_weight_grad.astype(jnp.bfloat16), "dp", scatter_dimension=1, tiled=True
        ).astype(jnp.float32),
    )
    gain_sums = lax.psum(
        (gain_one_grad, query_gain_grad, key_gain_grad, gain_two_grad), ("dp", "mp")
    )
    return (
        layer_output,
        input_grad,
        gain_sums[0],
        gain_sums[1],
        gain_sums[2],
        attn_grads[0],
        attn_grads[1],
        attn_grads[2],
        attn_grads[3],
        gain_sums[3],
        mlp_grads[0],
        mlp_grads[1],
        mlp_grads[2],
    )


ROW_BLOCK = 256


def wide_tables(length):
    cosine_table, sine_table = tables(length, HEAD_SIZE)
    return (
        jnp.concatenate([cosine_table, cosine_table], 1),
        jnp.concatenate([-sine_table, sine_table], 1),
    )


def turn(values, cosines, sines):
    return values * cosines + pltpu.roll(values, HEAD_SIZE // 2, 1) * sines


def turn_back(values, cosines, sines):
    return values * cosines - pltpu.roll(values, HEAD_SIZE // 2, 1) * sines


def causal(rows):
    query_places = lax.broadcasted_iota(jnp.int32, (rows, rows), 0)
    key_places = lax.broadcasted_iota(jnp.int32, (rows, rows), 1)
    return key_places <= query_places


def attend_kernel(
    core, own, other, w0, w1, w2, w3_low, w3_high, cosines, sines, query_gain, key_gain,
    proj, query_rot, key_rot, value, attended, log_total,
):
    half = own.shape[0]
    length = 2 * half
    scale = HEAD_SIZE ** (-0.5)
    query_cols = query_rot.shape[1]
    heads = query_cols // HEAD_SIZE
    for h in range(2):
        here = core[0] == h
        rows = slice(h * half, (h + 1) * half)
        block = None
        start = 0
        for weight in (w0, w1, w2, w3_low, w3_high):
            cols = slice(start, start + weight.shape[0])
            start = cols.stop
            tokens = jnp.where(here, own[:, cols], other[:, cols])
            term = matmul(tokens, weight[...])
            block = term if block is None else block + term
        proj[rows, :] = block
        cos_rows, sin_rows = cosines[rows, :], sines[rows, :]
        for head in range(heads):
            cols = slice(head * HEAD_SIZE, (head + 1) * HEAD_SIZE)
            normed, _ = norm_rows(block[:, cols], query_gain[...])
            query_rot[rows, cols] = turn(normed, cos_rows, sin_rows).astype(jnp.bfloat16)
        cols = slice(query_cols, query_cols + HEAD_SIZE)
        normed, _ = norm_rows(block[:, cols], key_gain[...])
        key_rot[rows, :] = turn(normed, cos_rows, sin_rows).astype(jnp.bfloat16)
        value[rows, :] = block[:, query_cols + HEAD_SIZE :].astype(jnp.bfloat16)
    allowed = causal(ROW_BLOCK)

    def place(start):
        return pl.ds(pl.multiple_of((start + core[0] * half) % length, ROW_BLOCK), ROW_BLOCK)

    lane = lax.broadcasted_iota(jnp.int32, (ROW_BLOCK, HEAD_SIZE), 1)
    for start in range(0, length, ROW_BLOCK):
        rows = slice(start, start + ROW_BLOCK)
        logs = jnp.zeros((ROW_BLOCK, HEAD_SIZE), jnp.float32)
        for head in range(heads):
            cols = slice(head * HEAD_SIZE, (head + 1) * HEAD_SIZE)
            query = query_rot[rows, cols]
            scores = [jnp.where(allowed, dot_last(query, key_rot[rows, :]) * scale, -jnp.inf)]
            if start:
                scores.append(dot_last(query, key_rot[:start, :]) * scale)
            largest = functools.reduce(
                jnp.maximum, [jnp.max(s, -1, keepdims=True) for s in scores]
            )
            expanded = [jnp.exp(s - largest) for s in scores]
            summed = sum(jnp.sum(e, -1, keepdims=True) for e in expanded)
            out = matmul(expanded[0].astype(jnp.bfloat16), value[rows, :])
            if start:
                out = out + matmul(expanded[1].astype(jnp.bfloat16), value[:start, :])
            attended[place(start), cols] = (out / summed).astype(jnp.bfloat16)
            logs = jnp.where(lane == head, largest + jnp.log(summed), logs)
        log_total[rows, :] = logs


def attend(core, own, other, weights, cosines, sines, query_gain, key_gain, planes, query_cols):
    half, width = own.shape
    length = 2 * half
    cols = weights[0].shape[1]
    group = cols // planes
    whole = lambda shape: pl.BlockSpec(shape, lambda g, core: (0, 0))
    column = lambda rows, width: pl.BlockSpec((rows, width), lambda g, core: (0, g))
    shape = jax.ShapeDtypeStruct
    return pl.pallas_call(
        attend_kernel,
        grid_spec=pltpu.PrefetchScalarGridSpec(
            num_scalar_prefetch=1,
            grid=(planes,),
            in_specs=[whole((half, width))] * 2
            + [column(weight.shape[0], group) for weight in weights]
            + [whole((length, HEAD_SIZE))] * 2
            + [whole((1, HEAD_SIZE))] * 2,
            out_specs=[
                column(length, group),
                column(length, query_cols),
                column(length, HEAD_SIZE),
                column(length, HEAD_SIZE),
                column(length, query_cols),
                column(length, HEAD_SIZE),
            ],
        ),
        out_shape=[
            shape((length, cols), jnp.float32),
            shape((length, planes * query_cols), jnp.bfloat16),
            shape((length, planes * HEAD_SIZE), jnp.bfloat16),
            shape((length, planes * HEAD_SIZE), jnp.bfloat16),
            shape((length, planes * query_cols), jnp.bfloat16),
            shape((length, planes * HEAD_SIZE), jnp.float32),
        ],
        compiler_params=pltpu.CompilerParams(vmem_limit_bytes=56 * 2**20),
        cost_estimate=pl.CostEstimate(flops=1, bytes_accessed=1, transcendentals=0),
    )(core, own, other, *weights, cosines, sines, query_gain, key_gain)


def attend_back_kernel(
    core, own, other, o0, o1, o2, o3_low, o3_high, cosines, sines, query_gain, key_gain,
    proj, query_rot, key_rot, value, log_total,
    proj_grad, gain_grads, grad, key_total, value_total,
):
    half = own.shape[0]
    length = 2 * half
    part = o0.shape[1]
    scale = HEAD_SIZE ** (-0.5)
    query_cols = query_rot.shape[1]
    heads = query_cols // HEAD_SIZE

    @pl.when(pl.program_id(0) == 0)
    def _():
        gain_grads[...] = jnp.zeros_like(gain_grads)

    low = pl.program_id(0) < pl.num_programs(0) // 2
    corner = jnp.where(low, o3_low[...], o3_high[...])
    for h in range(2):
        here = core[0] == h
        block = None
        for k, weight in enumerate((o0[...], o1[...], o2[...], corner)):
            cols = slice(k * part, (k + 1) * part)
            tokens = jnp.where(here, own[:, cols], other[:, cols])
            term = dot_last(tokens, weight)
            block = term if block is None else block + term
        grad[h * half : (h + 1) * half, :] = block.astype(jnp.bfloat16)
    key_total[...] = jnp.zeros_like(key_total)
    value_total[...] = jnp.zeros_like(value_total)
    allowed = causal(ROW_BLOCK)

    def fold(values):
        return jnp.sum(values.reshape(-1, 8, HEAD_SIZE), 0)

    def place(start):
        return pl.ds(pl.multiple_of((start + core[0] * half) % length, ROW_BLOCK), ROW_BLOCK)

    for start in range(0, length, ROW_BLOCK):
        rows = slice(start, start + ROW_BLOCK)
        for head in range(heads):
            cols = slice(head * HEAD_SIZE, (head + 1) * HEAD_SIZE)
            query = query_rot[rows, cols]
            upstream = grad[rows, cols]
            logs = log_total[rows, head : head + 1]
            spans = [rows] + ([slice(0, start)] if start else [])
            probs, prob_grads = [], []
            for n, span in enumerate(spans):
                raw = dot_last(query, key_rot[span, :]) * scale
                if n == 0:
                    raw = jnp.where(allowed, raw, -jnp.inf)
                probs.append(jnp.exp(raw - logs))
                prob_grads.append(dot_last(upstream, value[span, :]))
            inner = sum(jnp.sum(p * d, -1, keepdims=True) for p, d in zip(probs, prob_grads))
            query_back = None
            for span, p, d in zip(spans, probs, prob_grads):
                score_grad = (p * (d - inner)).astype(jnp.bfloat16)
                term = matmul(score_grad, key_rot[span, :])
                query_back = term if query_back is None else query_back + term
                key_total[span, :] += dot_first(score_grad, query)
                value_total[span, :] += dot_first(p.astype(jnp.bfloat16), upstream)
            normed_grad = turn_back(query_back * scale, cosines[rows, :], sines[rows, :])
            values = proj[rows, cols]
            _, factor = norm_rows(values, query_gain[...])
            gain_grads[:8, :] += fold(normed_grad * values * factor)
            back = norm_back(values, factor, query_gain[...], normed_grad)
            proj_grad[place(start), cols] = back.astype(jnp.bfloat16)
    for start in range(0, length, ROW_BLOCK):
        rows = slice(start, start + ROW_BLOCK)
        cols = slice(query_cols, query_cols + HEAD_SIZE)
        normed_grad = turn_back(key_total[rows, :] * scale, cosines[rows, :], sines[rows, :])
        values = proj[rows, cols]
        _, factor = norm_rows(values, key_gain[...])
        gain_grads[8:, :] += fold(normed_grad * values * factor)
        back = norm_back(values, factor, key_gain[...], normed_grad)
        proj_grad[place(start), cols] = back.astype(jnp.bfloat16)
        proj_grad[place(start), query_cols + HEAD_SIZE :] = value_total[rows, :].astype(
            jnp.bfloat16
        )


def attend_back(
    core, own, other, weights, cosines, sines, query_gain, key_gain, saved, planes, query_cols
):
    half, width = own.shape
    length = 2 * half
    part = weights[0].shape[1]
    proj, query_rot, key_rot, value, log_total = saved
    cols = proj.shape[1]
    group = cols // planes
    whole = lambda shape: pl.BlockSpec(shape, lambda g, core: (0, 0))
    column = lambda rows, width: pl.BlockSpec((rows, width), lambda g, core: (0, g))
    shape = jax.ShapeDtypeStruct
    return pl.pallas_call(
        attend_back_kernel,
        grid_spec=pltpu.PrefetchScalarGridSpec(
            num_scalar_prefetch=1,
            grid=(planes,),
            in_specs=[whole((half, width))] * 2
            + [pl.BlockSpec((query_cols, part), lambda g, core: (g, 0))] * 3
            + [
                pl.BlockSpec((query_cols, part), lambda g, core: (jnp.minimum(g, 1), 0)),
                pl.BlockSpec((query_cols, part), lambda g, core: (jnp.maximum(g - 2, 0), 0)),
            ]
            + [whole((length, HEAD_SIZE))] * 2
            + [whole((1, HEAD_SIZE))] * 2
            + [
                column(length, group),
                column(length, query_cols),
                column(length, HEAD_SIZE),
                column(length, HEAD_SIZE),
                column(length, HEAD_SIZE),
            ],
            out_specs=[column(length, group), whole((16, HEAD_SIZE))],
            scratch_shapes=[
                pltpu.VMEM((length, query_cols), jnp.bfloat16),
                pltpu.VMEM((length, HEAD_SIZE), jnp.float32),
                pltpu.VMEM((length, HEAD_SIZE), jnp.float32),
            ],
        ),
        out_shape=[
            shape((length, cols), jnp.bfloat16),
            shape((16, HEAD_SIZE), jnp.float32),
        ],
        compiler_params=pltpu.CompilerParams(vmem_limit_bytes=56 * 2**20),
        cost_estimate=pl.CostEstimate(flops=1, bytes_accessed=1, transcendentals=0),
    )(core, own, other, *weights, cosines, sines, query_gain, key_gain, *saved)


MESH = pl.DeviceIdType.MESH


def neighbours():
    me = lax.axis_index("dp")
    x, y = (me // 2) % 2, me // 4
    return me, me + 2 - 4 * x, me + 4 - 8 * y


def greet(others):
    barrier = pltpu.get_barrier_semaphore()
    for other in others:
        pl.semaphore_signal(barrier, inc=1, device_id={"dp": other}, device_id_type=MESH)
    pl.semaphore_wait(barrier, len(others))


def column_places(width):
    me = lax.axis_index("dp")
    core, x, y = me % 2, (me // 2) % 2, me // 4
    block = 256
    places = []
    for n in range(width // block):
        here = core if n < 4 else 1 - core
        far_x = 1 - x if n % 2 else x
        far_y = 1 - y if (n // 2) % 2 else y
        start = (4 * far_y + 2 * far_x + here) * block
        places.append(pl.ds(pl.multiple_of(start, block), block))
    return places


def split_columns(target, values):
    for n, cols in enumerate(column_places(values.shape[1])):
        target[:, n * 256 : (n + 1) * 256] = values[:, cols]


def merge_columns(target, sums):
    for n, cols in enumerate(column_places(sums.shape[1])):
        target[:, cols] = sums[:, n * 256 : (n + 1) * 256].astype(target.dtype)


def both_halves(left, own, other):
    half = own.shape[1]
    return dot_last(left[:, :half], own[...]) + dot_last(left[:, half:], other[...])


def hidden_kernel(
    x_tokens_out, y_tokens_out, x_grads_out, y_grads_out,
    own_tokens, x_tokens, y_tokens, own_grads, x_grads, y_grads,
    gate_own, gate_other, up_own, up_other,
    all_tokens, all_grads, hidden, gate_slope, up_slope,
    far_tokens, far_grads, send, receive,
):
    block, chunk = pl.program_id(0), pl.program_id(1)
    _, over_x, over_y = neighbours()
    half = far_tokens.shape[0] // 2
    low, high = pl.ds(0, half), pl.ds(half, half)
    copies = [
        pltpu.make_async_remote_copy(
            src_ref=source.at[rows],
            dst_ref=target.at[rows],
            send_sem=send.at[n],
            recv_sem=receive.at[n],
            device_id={"dp": other},
            device_id_type=MESH,
        )
        for n, (source, target, rows, other) in enumerate(
            (
                (x_tokens_out, far_tokens, low, over_y),
                (y_tokens_out, far_tokens, high, over_x),
                (x_grads_out, far_grads, low, over_y),
                (y_grads_out, far_grads, high, over_x),
            )
        )
    ]

    @pl.when((block == 0) & (chunk == 0))
    def _():
        greet((over_x, over_y))
        for transfer in copies:
            transfer.start()

    parts = ((own_tokens, own_grads), (x_tokens, x_grads), (y_tokens, y_grads), (far_tokens, far_grads))
    for n, (tokens, grads) in enumerate(parts):

        @pl.when((block == n) & (chunk == 0))
        def _():
            if n == 3:
                for transfer in copies:
                    transfer.wait_recv()
            split_columns(all_tokens, tokens)
            split_columns(all_grads, grads)

    values = all_tokens[...]
    gate = both_halves(values, gate_own, gate_other)
    up = both_halves(values, up_own, up_other)
    sigmoid_gate = 1.0 / (1.0 + jnp.exp(-gate))
    silu = gate * sigmoid_gate
    hidden[...] = (silu * up).astype(jnp.bfloat16)
    gate_slope[...] = (up * sigmoid_gate * (1.0 + gate * (1.0 - sigmoid_gate))).astype(
        jnp.bfloat16
    )
    up_slope[...] = silu.astype(jnp.bfloat16)

    @pl.when((block == 3) & (chunk == pl.num_programs(1) - 1))
    def _():
        for transfer in copies:
            transfer.wait_send()


def gather_hidden(tokens, grads, weights):
    rows, width = tokens[0].shape
    hidden_count, half = weights[0].shape
    chunk = 512
    spec = pl.BlockSpec
    shape = jax.ShapeDtypeStruct
    outside = spec(memory_space=pl.ANY)
    whole = spec((rows, width), lambda b, c: (0, 0), pipeline_mode=pl.Buffered(1))
    bf16 = jnp.bfloat16
    return pl.pallas_call(
        hidden_kernel,
        grid=(4, hidden_count // chunk),
        in_specs=[outside] * 4 + [whole] * 6
        + [spec((chunk, half), lambda b, c: (c, 0))] * 4,
        out_specs=[spec((rows, width), lambda b, c: (b, 0))] * 2
        + [spec((rows, chunk), lambda b, c: (b, c))] * 3,
        out_shape=[shape((4 * rows, width), bf16)] * 2 + [shape((4 * rows, hidden_count), bf16)] * 3,
        scratch_shapes=[pltpu.VMEM((rows, width), bf16)] * 2
        + [pltpu.SemaphoreType.DMA((4,)), pltpu.SemaphoreType.DMA((4,))],
        compiler_params=pltpu.CompilerParams(
            collective_id=1, has_side_effects=True, vmem_limit_bytes=60 * 2**20
        ),
        cost_estimate=pl.CostEstimate(flops=1, bytes_accessed=1, transcendentals=0),
    )(*tokens[1:], *grads[1:], *tokens, *grads, *weights)


def reduce_copies(corner, send_x, send_y, got_corner, got_x, got_y, send, receive):
    _, over_x, over_y = neighbours()
    half = corner.shape[0] // 2
    low, high = pl.ds(0, half), pl.ds(half, half)
    plan = [
        (corner.at[low], got_corner.at[low], over_y),
        (corner.at[high], got_corner.at[high], over_x),
        (send_y.at[low], got_y.at[low], over_y),
        (send_y.at[high], got_y.at[high], over_y),
        (send_x.at[high], got_x.at[high], over_x),
        (send_x.at[low], got_x.at[low], over_x),
    ]
    return [
        pltpu.make_async_remote_copy(
            src_ref=source,
            dst_ref=target,
            send_sem=send.at[n],
            recv_sem=receive.at[n],
            device_id={"dp": other},
            device_id_type=MESH,
        )
        for n, (source, target, other) in enumerate(plan)
    ]


def corner_copies(corner, got_corner, send, receive, first):
    _, over_x, over_y = neighbours()
    half = corner.shape[0] // 2
    return [
        pltpu.make_async_remote_copy(
            src_ref=corner.at[rows],
            dst_ref=got_corner.at[rows],
            send_sem=send.at[first + n],
            recv_sem=receive.at[first + n],
            device_id={"dp": other},
            device_id_type=MESH,
        )
        for n, (rows, other) in enumerate(
            ((pl.ds(0, half), over_y), (pl.ds(half, half), over_x))
        )
    ]


def add_into(target, rows, other):
    total_rows = target[rows, :].astype(jnp.float32) + other[rows, :].astype(jnp.float32)
    target[rows, :] = total_rows.astype(target.dtype)


def feed_back_kernel(
    grads, hidden, gate_slope, up_slope,
    gate_own, gate_other, up_own, up_other, down_own, down_other,
    gate_grad, up_grad, out_own, out_x, out_y, two_grad,
    out_sum, two_sum, out_corner, keep_x, keep_y, got_out, local, corner, send_x, send_y, got_corner, got_x, got_y, send, receive,
):
    turn_index, chunk = pl.program_id(0), pl.program_id(1)
    last = chunk == pl.num_programs(1) - 1
    rows = grads.shape[0]
    low, high = slice(0, rows // 2), slice(rows // 2, rows)
    copies = reduce_copies(corner, send_x, send_y, got_corner, got_x, got_y, send, receive)
    copies += corner_copies(out_corner, got_out, send, receive, len(copies))
    writes = [
        pltpu.make_async_copy(source, target, local.at[n])
        for n, (source, target) in enumerate(
            ((keep_y, out_y), (keep_x, out_x), (out_corner, out_own))
        )
    ]

    @pl.when((turn_index == 0) & (chunk == 0))
    def _():
        _, over_x, over_y = neighbours()
        greet((over_x, over_y))

    @pl.when(chunk == 0)
    def _():
        out_sum[...] = jnp.zeros_like(out_sum)
        two_sum[...] = jnp.zeros_like(two_sum)

    hidden_grad = both_halves(grads[...], down_own, down_other)
    gate_back = (hidden_grad * gate_slope[...].astype(jnp.float32)).astype(jnp.bfloat16)
    up_back = (hidden_grad * up_slope[...].astype(jnp.float32)).astype(jnp.bfloat16)
    gate_grad[...] = gate_back
    up_grad[...] = up_back
    active = hidden[...]
    half = down_own.shape[1]
    for n, (gate, up, down) in enumerate(
        ((gate_own, up_own, down_own), (gate_other, up_other, down_other))
    ):
        for part in range(0, half, 512):
            cols = slice(part, part + 512)
            place = slice(n * half + part, n * half + part + 512)
            out_sum[:, place] += matmul(active, down[:, cols])
            two_sum[:, place] += matmul(gate_back, gate[:, cols]) + matmul(up_back, up[:, cols])

    @pl.when(last & (turn_index == 0))
    def _():
        merge_columns(corner, two_sum)
        copies[0].start()
        copies[1].start()
        merge_columns(out_corner, out_sum)
        copies[6].start()
        copies[7].start()

    @pl.when(last & (turn_index == 1))
    def _():
        merge_columns(send_y, two_sum)
        copies[2].start()
        merge_columns(keep_y, out_sum)

    @pl.when((chunk == 0) & (turn_index == 2))
    def _():
        copies[1].wait_recv()
        add_into(send_y, high, got_corner)
        copies[3].start()

    @pl.when(last & (turn_index == 2))
    def _():
        merge_columns(send_x, two_sum)
        copies[4].start()
        copies[0].wait_recv()
        add_into(send_x, low, got_corner)
        copies[5].start()
        merge_columns(keep_x, out_sum)
        copies[7].wait_recv()
        add_into(keep_y, high, got_out)
        writes[0].start()

    @pl.when(last & (turn_index == 3))
    def _():
        copies[6].wait_recv()
        add_into(keep_x, low, got_out)
        writes[1].start()
        copies[6].wait_send()
        copies[7].wait_send()
        merge_columns(out_corner, out_sum)
        writes[2].start()
        merge_columns(two_grad, two_sum)
        copies[2].wait_recv()
        copies[3].wait_recv()
        two_grad[...] += got_y[...].astype(jnp.float32)
        copies[4].wait_recv()
        copies[5].wait_recv()
        two_grad[...] += got_x[...].astype(jnp.float32)
        for transfer in copies[:6]:
            transfer.wait_send()
        for write in writes:
            write.wait()


def feed_back(grads, saved, weights, down):
    rows, width = grads.shape[0] // 4, grads.shape[1]
    hidden_count, half = weights[0].shape
    chunk = 512
    spec = pl.BlockSpec
    shape = jax.ShapeDtypeStruct
    bf16, f32 = jnp.bfloat16, jnp.float32
    block = lambda q, c: (3 - q, 0)
    piece = lambda q, c: (3 - q, c)
    return pl.pallas_call(
        feed_back_kernel,
        grid=(4, hidden_count // chunk),
        in_specs=[spec((rows, width), block)]
        + [spec((rows, chunk), piece)] * 3
        + [spec((chunk, half), lambda q, c: (c, 0))] * 6,
        out_specs=[spec((rows, chunk), piece)] * 2
        + [spec(memory_space=pl.ANY)] * 3
        + [spec((rows, width), lambda q, c: (0, 0))],
        out_shape=[shape((4 * rows, hidden_count), bf16)] * 2
        + [shape((rows, width), bf16)] * 3
        + [shape((rows, width), f32)],
        scratch_shapes=[pltpu.VMEM((rows, width), f32)] * 2
        + [pltpu.VMEM((rows, width), bf16)] * 4
        + [pltpu.SemaphoreType.DMA((3,))]
        + [pltpu.VMEM((rows, width), bf16)] * 6
        + [pltpu.SemaphoreType.DMA((8,)), pltpu.SemaphoreType.DMA((8,))],
        compiler_params=pltpu.CompilerParams(
            collective_id=2, has_side_effects=True, vmem_limit_bytes=62 * 2**20
        ),
        cost_estimate=pl.CostEstimate(flops=1, bytes_accessed=1, transcendentals=0),
    )(grads, *saved, *weights, *down)


def is_crossing():
    return (lax.axis_index("dp") + lax.axis_index("mp")) % 2 == 1


def crossing_partner():
    me, z = lax.axis_index("dp"), lax.axis_index("mp")
    return {"dp": me + 1 - 2 * (me % 2), "mp": z + 1 - 2 * (z % 2)}


def crossing_copy(source, target, send, receive):
    return pltpu.make_async_remote_copy(
        src_ref=source,
        dst_ref=target,
        send_sem=send.at[0],
        recv_sem=receive.at[0],
        device_id=crossing_partner(),
        device_id_type=MESH,
    )


def core_copy(source, target, send, receive, n, chunk):
    me = lax.axis_index("dp")
    rows = pl.ds(n * chunk, chunk)
    return pltpu.make_async_remote_copy(
        src_ref=source.at[rows],
        dst_ref=target.at[rows],
        send_sem=send.at[n],
        recv_sem=receive.at[n],
        device_id={"dp": me + 1 - 2 * (me % 2)},
        device_id_type=MESH,
    )


def outer_kernel(extra, more, left_own, left_other, right_own, right_other, *refs):
    weights = refs[:extra]
    if extra:
        layer, total_out, *spread, layer_out = refs[extra : extra + 5]
        cross = crossing_copy(layer, layer_out, refs[-3], refs[-2])
        stay = pltpu.make_async_copy(layer, layer_out, refs[-1].at[0])
        crossing = is_crossing()
        refs = refs[:-3]
    elif more:
        product_left, product_right, total_out, product_out = refs[:4]
        product_own, product_send, product_got, product_sent, product_came = refs[-5:]
        refs = refs[:-5]
        chunk = product_left.shape[1]
        exchanges = [
            core_copy(product_send, product_got, product_sent, product_came, n, chunk)
            for n in range(more)
        ]
    else:
        total_out = refs[0]
    own, corner, send_x, send_y, got_corner, got_x, got_y, send, receive = refs[-9:]
    step = pl.program_id(0)
    half = own.shape[0] // 2
    low, high = slice(0, half), slice(half, 2 * half)
    copies = reduce_copies(corner, send_x, send_y, got_corner, got_x, got_y, send, receive)

    if not extra:

        @pl.when(step == 0)
        def _():
            me, over_x, over_y = neighbours()
            greet((over_x, over_y) + ((me + 1 - 2 * (me % 2),) if more else ()))

    else:

        @pl.when((step == 0) & crossing)
        def _():
            _, over_x, over_y = neighbours()
            partner = crossing_partner()
            barrier = pltpu.get_barrier_semaphore()
            for other in (over_x, over_y):
                pl.semaphore_signal(barrier, inc=1, device_id={"dp": other}, device_id_type=MESH)
            pl.semaphore_signal(barrier, inc=1, device_id=partner, device_id_type=MESH)
            pl.semaphore_wait(barrier, 3)
            cross.start()

        @pl.when((step == 0) & jnp.logical_not(crossing))
        def _():
            _, over_x, over_y = neighbours()
            greet((over_x, over_y))
            stay.start()

    @pl.when(step < 8)
    def _():
        result = dot_first(left_own[...], right_own[...]) + dot_first(
            left_other[...], right_other[...]
        )
        order = (corner, corner, send_y, send_y, send_x, send_x, own, own)
        starts = (0, 1, 2, None, None, 4, None, None)
        for n, (target, first) in enumerate(zip(order, starts)):

            @pl.when(step == n)
            def _():
                target[high if n % 2 else low, :] = result.astype(target.dtype)
                if first is not None:
                    copies[first].start()

    for n, weight in enumerate(weights):

        @pl.when(step == 8 + n)
        def _():
            me = lax.axis_index("dp")
            x, y = (me // 2) % 2, me // 4
            k = min(n, 3)
            far_x = 1 - x if k % 2 else x
            far_y = 1 - y if k // 2 else y
            part = 512
            start = (2 * far_y + far_x) * part + (part // 2 if n == 4 else 0)
            cols = pl.ds(pl.multiple_of(start, 256), weight.shape[0])
            spread[0][:, cols] = dot_last(right_own[...], weight[...])
            spread[1][:, cols] = dot_last(right_other[...], weight[...]).astype(jnp.bfloat16)

    if more:

        @pl.when(step >= 8)
        def _():
            product = dot_first(product_left[...], product_right[...])
            middle = product_own.shape[1]
            for n in range(more):

                @pl.when(step == 8 + n)
                def _():
                    rows = slice(n * chunk, (n + 1) * chunk)
                    product_own[rows, :] = product[:, :middle]
                    product_send[rows, :] = product[:, middle:].astype(jnp.bfloat16)
                    exchanges[n].start()

    last = pl.num_programs(0) - 1

    @pl.when(step == min(9, 7 + extra + more))
    def _():
        copies[1].wait_recv()
        add_into(send_y, high, got_corner)
        copies[3].start()
        copies[0].wait_recv()
        add_into(send_x, low, got_corner)
        copies[5].start()

    @pl.when(step == last)
    def _():
        for n in (2, 4, 3, 5):
            copies[n].wait_recv()
        total_out[...] = (
            own[...] + got_x[...].astype(jnp.float32) + got_y[...].astype(jnp.float32)
        ).astype(total_out.dtype)
        for transfer in copies:
            transfer.wait_send()

    if more:

        @pl.when(step == last)
        def _():
            for transfer in exchanges:
                transfer.wait()
            product_out[...] = (
                product_own[...] + product_got[...].astype(jnp.float32)
            ).astype(jnp.bfloat16)

    if extra:

        @pl.when((step == last) & crossing)
        def _():
            cross.wait()

        @pl.when((step == last) & jnp.logical_not(crossing))
        def _():
            stay.wait()


def outer(lefts, rights, by_left, collective_id, weights=(), layer=None, product=None):
    rows = 512
    wide = lefts[0][0].shape[1]
    right_wide = rights[0][0].shape[1]
    turn_of = lambda s: 6 - 2 * (jnp.minimum(s, 7) // 2) + jnp.minimum(s, 7) % 2
    if by_left:
        size = (wide // 8, right_wide)
        left_size = (rows, wide // 8)
        place_left = lambda row: lambda s: (row, turn_of(s))
        place_right = lambda row: lambda s: (row, 0)
    else:
        size = (wide // 2, right_wide // 4)
        left_size = (rows, wide // 2)
        place_left = lambda row: lambda s: (row, jnp.minimum(s, 7) % 2)
        place_right = lambda row: lambda s: (row, 3 - jnp.minimum(s, 7) // 2)
    both = (2 * size[0], size[1])
    spec, shape = pl.BlockSpec, jax.ShapeDtypeStruct
    out_specs = [spec(both, lambda s: (0, 0))]
    out_shape = [shape(both, jnp.bfloat16)]
    if weights:
        out_specs += [spec((rows, wide), lambda s: (0, 0))] * 2
        out_shape += [shape((rows, wide), jnp.float32), shape((rows, wide), jnp.bfloat16)]
        out_specs += [spec(memory_space=pl.ANY)]
        out_shape += [shape(layer.shape, layer.dtype)]
    more, product_specs = 0, []
    if product:
        chunk = 256
        tokens, hidden_count = product[0].shape
        more = hidden_count // chunk
        turn = lambda s: jnp.maximum(s - 8, 0)
        product_specs = [
            spec((tokens, chunk), lambda s: (0, turn(s))),
            spec(product[1].shape, lambda s: (0, 0), pipeline_mode=pl.Buffered(1)),
        ]
        half = product[1].shape[1] // 2
        out_specs += [spec((hidden_count, half), lambda s: (0, 0))]
        out_shape += [shape((hidden_count, half), jnp.bfloat16)]
    made = pl.pallas_call(
        functools.partial(outer_kernel, len(weights), more),
        grid=(8 + len(weights) + more,),
        in_specs=[spec(left_size, place_left(row)) for _, row in lefts]
        + [spec((rows, size[1]), place_right(row)) for _, row in rights]
        + [
            spec(weight.shape, lambda s: (0, 0), pipeline_mode=pl.Buffered(1))
            for weight in weights
        ]
        + ([spec(memory_space=pl.ANY)] if weights else [])
        + product_specs,
        out_specs=out_specs,
        out_shape=out_shape,
        scratch_shapes=[pltpu.VMEM(both, jnp.float32)]
        + [pltpu.VMEM(both, jnp.bfloat16)] * 6
        + [pltpu.SemaphoreType.DMA((6,)), pltpu.SemaphoreType.DMA((6,))]
        + ([pltpu.SemaphoreType.DMA((1,))] * 3 if weights else [])
        + (
            [
                pltpu.VMEM((hidden_count, half), jnp.float32),
                pltpu.VMEM((hidden_count, half), jnp.bfloat16),
                pltpu.VMEM((hidden_count, half), jnp.bfloat16),
                pltpu.SemaphoreType.DMA((more,)),
                pltpu.SemaphoreType.DMA((more,)),
            ]
            if product
            else []
        ),
        compiler_params=pltpu.CompilerParams(
            collective_id=collective_id, has_side_effects=True, vmem_limit_bytes=60 * 2**20
        ),
        cost_estimate=pl.CostEstimate(flops=1, bytes_accessed=1, transcendentals=0),
    )(*[array for array, _ in (*lefts, *rights)], *weights, *([layer] if weights else []), *(product or []))
    return made


def columns_kernel(transposed, place, left, w0, w1, w2, w3_low, w3_high, own, other):
    rows = own.shape[0]

    def write(lines, result):
        for ref, kind in ((own, jnp.float32), (other, jnp.bfloat16)):
            start = 0 if ref is own else rows
            ref[...] = result(lines[start : start + rows]).astype(kind)

    for k, weight in enumerate((w0, w1, w2)):

        @pl.when(pl.program_id(0) == k)
        def _():
            step = dot_last if transposed else matmul
            write(left, lambda lines: step(lines, weight[...]))

    @pl.when(pl.program_id(0) == 3)
    def _():
        if transposed:
            write(
                left,
                lambda lines: jnp.concatenate(
                    [dot_last(lines, w3_low[...]), dot_last(lines, w3_high[...])], 1
                ),
            )
        else:
            middle = w3_low.shape[0]
            write(
                left,
                lambda lines: matmul(lines[:, :middle], w3_low[...])
                + matmul(lines[:, middle:], w3_high[...]),
            )


def columns(place, left, weights, transposed):
    length, depth = left.shape
    rows = length // 2
    part = weights[0].shape[0 if transposed else 1]
    width = 4 * part
    whole = lambda array: pl.BlockSpec(array.shape, lambda k, place: (0, 0))
    block = pl.BlockSpec((rows, part), lambda k, place: (0, k ^ place[0]))
    shape = jax.ShapeDtypeStruct
    return pl.pallas_call(
        functools.partial(columns_kernel, transposed),
        grid_spec=pltpu.PrefetchScalarGridSpec(
            num_scalar_prefetch=1,
            grid=(4,),
            in_specs=[whole(array) for array in (left, *weights)],
            out_specs=[block, block],
        ),
        out_shape=[shape((rows, width), jnp.float32), shape((rows, width), jnp.bfloat16)],
        compiler_params=pltpu.CompilerParams(vmem_limit_bytes=56 * 2**20),
        cost_estimate=pl.CostEstimate(flops=1, bytes_accessed=1, transcendentals=0),
    )(place, left, *weights)


def tile_call(kernel, place, ins, outs, kept):
    width = 2048
    tile = 256

    def spec(cut, columns):
        if cut == "rows":
            return pl.BlockSpec((tile, columns), lambda t, place: (t, 0))
        if cut == "low" or cut == "high":
            return pl.BlockSpec((tile, columns), lambda t, place: (0, 0))
        return pl.BlockSpec((cut, columns), lambda t, place: (0, 0))

    return pl.pallas_call(
        kernel,
        grid_spec=pltpu.PrefetchScalarGridSpec(
            num_scalar_prefetch=1,
            grid=(2,),
            in_specs=[spec(cut, array.shape[1]) for array, cut in ins],
            out_specs=[spec(cut, shape.shape[1]) for shape, cut in outs],
        ),
        out_shape=[shape for shape, _ in outs],
        compiler_params=pltpu.CompilerParams(vmem_limit_bytes=56 * 2**20),
        cost_estimate=pl.CostEstimate(flops=1, bytes_accessed=1, transcendentals=0),
    )(place, *[array for array, _ in ins])


def choose(low_ref, high_ref):
    return jnp.where(pl.program_id(0) == 0, low_ref[...], high_ref[...]).astype(jnp.float32)


def add_gain(gain_ref, values):
    @pl.when(pl.program_id(0) == 0)
    def _():
        gain_ref[...] = jnp.zeros_like(gain_ref)

    gain_ref[...] += jnp.sum(values.reshape(-1, 8, values.shape[1]), 0)


def relabelled(ref, values, place):
    width = values.shape[1] // 4
    for k in range(4):
        start = pl.multiple_of((place[0] ^ k) * width, width)
        ref[:, pl.ds(start, width)] = values[:, k * width : (k + 1) * width]


def first_norm_kernel(place, inputs, gain, normed):
    values, _ = norm_rows(inputs[...].astype(jnp.float32), gain[...])
    relabelled(normed, values.astype(jnp.bfloat16), place)


def middle_kernel(place, inputs, own, other, gain, middle, normed):
    values = inputs[...].astype(jnp.float32) + own[...] + other[...].astype(jnp.float32)
    middle[...] = values
    normed[...] = norm_rows(values, gain[...])[0].astype(jnp.bfloat16)


def middle_back_kernel(
    place, middle, cotangent, two, gain, middle_grad, branch, gain_grad
):
    two_grad = two[...]
    values = middle[...]
    _, factor = norm_rows(values, gain[...])
    add_gain(gain_grad, two_grad * values * factor)
    grads = cotangent[...].astype(jnp.float32) + norm_back(values, factor, gain[...], two_grad)
    middle_grad[...] = grads
    relabelled(branch, grads.astype(jnp.bfloat16), place)


def input_back_kernel(
    place, inputs, middle_grad, own, other, gain, input_grad, rounded, gain_grad
):
    one_grad = own[...] + other[...].astype(jnp.float32)
    values = inputs[...].astype(jnp.float32)
    _, factor = norm_rows(values, gain[...])
    add_gain(gain_grad, one_grad * values * factor)
    grads = middle_grad[...] + norm_back(values, factor, gain[...], one_grad)
    input_grad[...] = grads
    rounded[...] = grads.astype(jnp.bfloat16)


def output_kernel(place, middle, own, over_x, over_y, output):
    parts = [part[...].astype(jnp.float32) for part in (own, over_x, over_y)]
    output[...] = (middle[...] + parts[0] + parts[1] + parts[2]).astype(jnp.bfloat16)


def exchange(values, bit):
    return lax.ppermute(values, "dp", [(i, i ^ bit) for i in range(8)])


def swap_halves(values):
    pairs = []
    for i in range(8):
        for m in range(4):
            if (i & 1) != (m & 1):
                pairs.append((i * 4 + m, (i ^ 1) * 4 + (m ^ 1)))
    return lax.ppermute(values, ("dp", "mp"), pairs)


def after(values, earlier):
    return lax.optimization_barrier((values, earlier))[0]


def gather_near(block):
    return [exchange(block, 2), exchange(block, 4)]


def gather_far(near):
    half = near[0].shape[0] // 2
    return [exchange(near[0][:half], 4), exchange(near[1][half:], 2)]


def add_low(left, right):
    return (left.astype(jnp.float32) + right.astype(jnp.float32)).astype(jnp.bfloat16)


def pick(values, index, width, axis):
    return lax.dynamic_slice_in_dim(values, index * width, width, axis)


def in_order(own, other, core, axis=0):
    return jnp.where(
        core == 0,
        jnp.concatenate([own, other], axis),
        jnp.concatenate([other, own], axis),
    )


def total_plane(values):
    for bit in (1, 2, 4):
        values = values + exchange(values, bit)
    return values


def total_z(values):
    others = [lax.ppermute(values, "mp", [(i, i ^ bit) for i in range(4)]) for bit in (1, 2, 3)]
    return (values + others[0]) + (others[1] + others[2])


def fast(
    layer_input,
    out_grad,
    norm_attn,
    query_norm,
    key_norm,
    w_query,
    key_matrix,
    value_matrix,
    w_output,
    norm_mlp,
    w_gate,
    w_up,
    w_down,
):
    bf16, f32 = jnp.bfloat16, jnp.float32
    device = lax.axis_index("dp")
    core = device & 1
    place = jnp.reshape(device >> 1, (1,)).astype(jnp.int32)
    core_index = jnp.reshape(core, (1,)).astype(jnp.int32)
    crossing = core != (lax.axis_index("mp") & 1)
    planes = 4
    rows = layer_input.shape[0]
    width = layer_input.shape[1]
    units = w_gate.shape[1] // planes
    array = jax.ShapeDtypeStruct

    query_cols = w_query.shape[1] // 2
    key_cols = key_matrix.shape[1] // 2

    def heads_of(which):
        return jnp.concatenate(
            [
                pick(w_query, which, query_cols, 1),
                pick(key_matrix, which, key_cols, 1),
                pick(value_matrix, which, key_cols, 1),
            ],
            1,
        )

    qkv_pair = in_order(heads_of(core), exchange(heads_of(1 - core), 1), core)
    out_rows = w_output.shape[0] // 2
    out_pair = in_order(
        pick(w_output, core, out_rows, 0),
        exchange(pick(w_output, 1 - core, out_rows, 0), 1),
        core,
        1,
    )
    qkv_z = lax.all_gather(qkv_pair, "mp", axis=1, tiled=True)
    pieces = jnp.concatenate(
        [w.reshape(planes, units, w.shape[1]) for w in (w_gate.T, w_up.T, w_down)], 1
    )

    def piece_for(k):
        return pick(pieces, place[0] ^ k, 1, 0)[0]

    feed_own = jnp.concatenate(
        [piece_for(0)] + [exchange(piece_for(k), 2 * k) for k in (1, 2, 3)], 1
    )

    feed_parts = [feed_own[n * units : (n + 1) * units] for n in range(3)]
    qkv_z = after(qkv_z, feed_parts)
    qkv_near = gather_near(qkv_z)
    moved = swap_halves(after(layer_input, qkv_z))
    moved_grad = swap_halves(after(out_grad, qkv_z))
    out_z = lax.all_gather(
        after(out_pair, (moved, moved_grad, qkv_near)), "mp", axis=0, tiled=True
    )

    inputs = jnp.where(crossing, moved, layer_input)
    cotangent = jnp.where(crossing, moved_grad, out_grad)

    gain_one, gain_two = norm_attn[None, :], norm_mlp[None, :]
    gain_query, gain_key = query_norm[None, :], key_norm[None, :]
    (normed,) = tile_call(
        first_norm_kernel,
        place,
        [(inputs, "rows"), (gain_one, 1)],
        [(array((rows, width), bf16), "rows")],
        4,
    )
    cosines, sines = wide_tables(2 * rows)
    qkv_chips = [
        qkv_z,
        *qkv_near,
        *gather_far(after(qkv_near, (normed, cosines, sines, cotangent))),
    ]
    out_near = gather_near(after(out_z, qkv_chips))
    feed_parts = after(feed_parts, (out_z, qkv_chips))
    gate_half, up_half = [
        lax.all_gather(part, "mp", axis=0, tiled=True) for part in feed_parts[:2]
    ]
    down_half = lax.all_gather(feed_parts[2], "mp", axis=0, tiled=True)
    normed_other = after(exchange(normed, 1), out_z)
    proj, query_rot, key_rot, value_low, attended, log_total = attend(
        core_index,
        normed,
        normed_other,
        qkv_chips,
        cosines,
        sines,
        gain_query,
        gain_key,
        planes,
        query_cols,
    )
    out_near = after(out_near, attended)
    out_chips = [out_z, *out_near, *gather_far(out_near)]
    grads_near = gather_near(after(cotangent, qkv_chips))
    branch_own, branch_other = columns(place, attended, out_chips, False)
    middle, tokens = tile_call(
        middle_kernel,
        place,
        [(inputs, "rows"), (branch_own, "rows"), (after(exchange(branch_other, 1), grads_near), "rows"), (gain_two, 1)],
        [
            (array((rows, width), f32), "rows"),
            (array((rows, width), bf16), "rows"),
        ],
        14,
    )

    tokens_near = gather_near(tokens)
    gate_up_w = [
        gate_half,
        exchange(after(gate_half, tokens), 1),
        up_half,
        exchange(after(up_half, tokens_near), 1),
    ]
    all_tokens, all_grads, all_hidden, gate_slope, up_slope = gather_hidden(
        [tokens, *tokens_near], [cotangent, *grads_near], gate_up_w
    )
    down_half = after(down_half, all_hidden)
    down_w = [down_half, exchange(down_half, 1)]

    def over_z(grad):
        return lax.psum_scatter(grad, "mp", scatter_dimension=0, tiled=True)

    half = width // 2
    down_other = dot_first(all_hidden, all_grads[:, half:]).astype(bf16)
    all_gate, all_up, out_own, out_x, out_y, two_grad = feed_back(
        after(all_grads, down_other),
        [all_hidden, gate_slope, up_slope],
        gate_up_w,
        down_w,
    )
    gate_other = dot_first(all_gate, all_tokens[:, half:]).astype(bf16)

    def own_half(left, right, other):
        own = dot_first(left, right[:, :half])
        return (own + exchange(other, 1).astype(f32)).astype(bf16)

    down_local = own_half(after(all_hidden, two_grad), all_grads, down_other)
    down_sum = over_z(down_local)
    gate_local = own_half(all_gate, all_tokens, gate_other)
    gate_sum = over_z(gate_local)
    middle_grad, branch, gain_two_part = tile_call(
        middle_back_kernel,
        place,
        [(middle, "rows"), (cotangent, "rows"), (two_grad, "rows"), (gain_two, 1)],
        [
            (array((rows, width), f32), "rows"),
            (array((rows, width), bf16), "rows"),
            (array((8, width), f32), 8),
        ],
        18,
    )

    def unspread(own):
        cols = own.shape[1] // planes
        got = [own[:, :cols]] + [
            exchange(own[:, k * cols : (k + 1) * cols], 2 * k) for k in (1, 2, 3)
        ]
        return jnp.concatenate(got, 1), cols

    def chips_in_order(got, cols, rows):
        return jnp.concatenate([pick(got[rows], place[0] ^ k, cols, 1) for k in range(planes)], 0)

    down_got, cols = unspread(down_sum)
    down_own = chips_in_order(down_got, cols, slice(0, units)).astype(f32)

    branch_pair = after(exchange(branch, 1), (gate_local, down_local))
    out_local, up_local = outer(
        [(attended, 0), (attended, 1)],
        [(branch, 0), (branch_pair, 0)],
        False,
        4,
        product=(all_up, all_tokens),
    )
    up_sum = over_z(up_local)
    out_sum = over_z(out_local)
    branch_pair, out_x, out_y = after((branch_pair, out_x, out_y), out_local)
    out_parts = [out_own, exchange(out_x, 2), exchange(out_y, 4)]
    proj_grad, head_gains = attend_back(
        core_index,
        branch,
        branch_pair,
        out_chips,
        cosines,
        sines,
        gain_query,
        gain_key,
        (proj, query_rot, key_rot, value_low, log_total),
        planes,
        query_cols,
    )

    out_parts = after(out_parts, proj_grad)
    (layer_output,) = tile_call(
        output_kernel,
        place,
        [(middle, "rows")] + [(part, "rows") for part in out_parts],
        [(array((rows, width), bf16), "rows")],
        12,
    )
    proj_grad = after(proj_grad, (down_sum, gate_sum, out_local))
    qkv_local, one_own, one_other, output_moved = outer(
        [(normed, 0), (normed_other, 0)],
        [(proj_grad, 0), (proj_grad, 1)],
        True,
        3,
        qkv_chips,
        layer_output,
    )
    qkv_local = after(qkv_local, (up_sum, out_sum))
    qkv_sum = lax.psum_scatter(qkv_local, "mp", scatter_dimension=1, tiled=True)
    input_grad, rounded_grad, gain_one_part = tile_call(
        input_back_kernel,
        place,
        [
            (inputs, "rows"),
            (middle_grad, "rows"),
            (one_own, "rows"),
            (exchange(one_other, 1), "rows"),
            (gain_one, 1),
        ],
        [
            (array((rows, width), f32), "rows"),
            (array((rows, width), bf16), "rows"),
            (array((8, width), f32), 8),
        ],
        18,
    )
    gate_up_got, cols = unspread(
        after(jnp.concatenate([gate_sum, up_sum], 0), rounded_grad)
    )
    gate_own = chips_in_order(gate_up_got, cols, slice(0, units)).T.astype(f32)
    up_own = chips_in_order(gate_up_got, cols, slice(units, 2 * units)).T.astype(f32)
    gain_sums = total_plane(
        after(jnp.concatenate(
            [
                jnp.sum(gain_one_part, 0),
                jnp.sum(head_gains[:8], 0),
                jnp.sum(head_gains[8:], 0),
                jnp.sum(gain_two_part, 0),
            ]
        ), (qkv_local, gate_own, up_own))
    )
    pair_rows = qkv_sum.shape[0] // 2
    qkv_other = exchange(pick(qkv_sum, 1 - core, pair_rows, 0), 1)
    qkv_own = pick(qkv_sum, core, pair_rows, 0)

    grad_moved = after(swap_halves(rounded_grad), qkv_other)
    gain_sums = total_z(after(gain_sums, grad_moved))

    def both(start, stop):
        return in_order(qkv_own[:, start:stop], qkv_other[:, start:stop], core, 1).astype(f32)

    pair_cols = out_sum.shape[1] // 2
    out_other = exchange(pick(out_sum, 1 - core, pair_cols, 1), 1)
    out_own = pick(out_sum, core, pair_cols, 1)
    return (
        output_moved,
        jnp.where(crossing, grad_moved.astype(f32), input_grad),
        gain_sums[:width],
        gain_sums[width : width + HEAD_SIZE],
        gain_sums[width + HEAD_SIZE : width + 2 * HEAD_SIZE],
        both(0, query_cols),
        both(query_cols, query_cols + key_cols),
        both(query_cols + key_cols, query_cols + 2 * key_cols),
        in_order(out_own, out_other, core, 0).astype(f32),
        gain_sums[width + 2 * HEAD_SIZE :],
        gate_own,
        up_own,
        down_own,
    )


def solution(mesh):
    in_specs = (
        P(("dp", "mp"), None),
        P(("dp", "mp"), None),
        P(),
        P(),
        P(),
        P("dp", "mp"),
        P("dp", "mp"),
        P("dp", "mp"),
        P("mp", "dp"),
        P(),
        P("dp", "mp"),
        P("dp", "mp"),
        P("mp", "dp"),
    )
    out_specs = (
        P(("dp", "mp"), None),
        P(("dp", "mp"), None),
        P(),
        P(),
        P(),
        P("dp", "mp"),
        P("dp", "mp"),
        P("dp", "mp"),
        P("mp", "dp"),
        P(),
        P("dp", "mp"),
        P("dp", "mp"),
        P("mp", "dp"),
    )
    whole_sequences = dict(mesh.shape) == {"dp": 8, "mp": 4}
    local = fast if whole_sequences else generic
    return jax.shard_map(local, mesh=mesh, in_specs=in_specs, out_specs=out_specs, check_vma=False)
```
